256 devices in a mesh: chan: 64 (over z, y, core), row: 4 (over x).
Axes of the slice: x: 4, y: 4, z: 8, core: 2. Of those that a mesh axis runs over, the one named last changes fastest.
Arguments:
- generator: float32 [64, 1280, 1280], P('chan', 'row'), as said below
- hamiltonian: float32 [64, 1280, 1280], P('chan', 'row'), as said below
- recoupling: float32 [64, 1280, 1280], P('chan')
- channel_size: int32 [64], P('chan'), may hold values from 128 to 1280, as said below
- hole_first: int32 [64, 1280], P('chan'), may hold values 0 or 1
- hole_second: int32 [64, 1280], P('chan'), may hold values 0 or 1
Outputs:
- derivative: float32 [64, 1280, 1280], P('chan', 'row')
The draws below stay inside these ranges and needn't reach their ends.
Inputs may be any that keep to these rules, and one draw needn't show every extreme that they name: generator is antisymmetric and hamiltonian symmetric in every channel block. hamiltonian is symmetric in every channel block. `channel_size`: some channel has exactly 1280 states.
All inputs are finite; a program needn't handle non-finite values. No bound on the sum of `hole_first` or of `hole_second` on one device may be relied on, other than what follows from the above.
Results may differ from the reference program's by a relative error of at most 0.000076.
Values sent between devices are 32-bit elements; how exact they have to be, the bound alone decides.
No kernel may reach another device: no remote copies, remote signals or barrier semaphores. Data moves between devices by JAX's collectives and lax.ppermute only.
A program may use at most 128 MiB of HBM per device.

```python
import jax
import jax.numpy as jnp
from jax import lax

MAXB = 1280
CH_DEV = 1
CHANNELS = 64
N_CHAN = 64


def noise_field(key):
    shape = (CH_DEV * N_CHAN, MAXB, MAXB)
    return jax.random.normal(key, shape, jnp.float32)


def draw_generator(key, part):
    key = jax.random.fold_in(key, 11)
    raw = noise_field(key)
    return (raw - jnp.swapaxes(raw, 1, 2)) * (0.70710678 * MAXB ** (-0.25))


def draw_hamiltonian(key, part):
    key = jax.random.fold_in(key, 23)
    raw = noise_field(key)
    return (raw + jnp.swapaxes(raw, 1, 2)) * (0.70710678 * MAXB ** (-0.25))


def draw_recoupling(key, part):
    key = jax.random.fold_in(key, 37)
    raw = noise_field(key)
    positions = jnp.arange(MAXB, dtype=jnp.int32)
    identity = (positions[:, None] == positions[None, :]).astype(jnp.float32)
    return identity[None, :, :] + raw * (0.6 * MAXB ** (-0.5))


def draw_channel_size(key, part):
    key = jax.random.fold_in(key, 41)
    sizes = jax.random.randint(key, (CH_DEV * N_CHAN,), MAXB // 10, MAXB + 1).astype(jnp.int32)
    return sizes.at[0].set(MAXB)


def touch_ends(values, own_key, least, high):
    longest = values.shape.index(max(values.shape))
    spots = []
    for shift in (0, 1):
        where = [jax.random.randint(jax.random.fold_in(own_key, axis), (), 0, length) for axis, length in enumerate(values.shape)]
        where[longest] = (where[longest] + shift) % values.shape[longest]
        spots.append(tuple(where))
    return values.at[spots[0]].set(least).at[spots[1]].set(high)


def setup_inputs(seed: int = 0) -> dict:
    keys = jax.random.split(jax.random.key(seed), 7)
    generator = draw_generator(jax.random.fold_in(keys[6], 71), 0)
    hamiltonian = draw_hamiltonian(jax.random.fold_in(keys[6], 71), 0)
    recoupling = draw_recoupling(jax.random.fold_in(keys[6], 71), 0)
    channel_size = draw_channel_size(jax.random.fold_in(keys[6], 71), 0)
    hole_first = touch_ends((jax.random.randint(keys[4], (CHANNELS, MAXB), 0, 3) < 1).astype(jnp.int32), jax.random.fold_in(keys[4], 1), 0, 1)
    hole_second = touch_ends((jax.random.randint(keys[5], (CHANNELS, MAXB), 0, 3) < 1).astype(jnp.int32), jax.random.fold_in(keys[5], 1), 0, 1)
    return dict(generator=generator, hamiltonian=hamiltonian, recoupling=recoupling, channel_size=channel_size, hole_first=hole_first, hole_second=hole_second)


def regroup(stack):
    piece = MAXB // N_CHAN
    shaped = stack.reshape(N_CHAN, CH_DEV, MAXB, N_CHAN, piece)
    return shaped.transpose(3, 1, 2, 0, 4).reshape(CH_DEV * N_CHAN, MAXB, MAXB)


def batched(left, right):
    return jnp.einsum("cij,cjk->cik", left, right, precision=lax.Precision.HIGHEST)


def reference(generator, hamiltonian, recoupling, channel_size, hole_first, hole_second):
    positions = jnp.arange(MAXB, dtype=jnp.int32)
    inside = (positions[None, :] < channel_size[:, None]).astype(jnp.float32)
    block_mask = inside[:, :, None] * inside[:, None, :]
    gen_live = generator * block_mask
    ham_live = hamiltonian * block_mask
    weight_pp = (1 - hole_first - hole_second).astype(jnp.float32)
    weight_ph = (hole_first - hole_second).astype(jnp.float32)
    ladder = batched(gen_live * weight_pp[:, None, :], ham_live) - batched(ham_live * weight_pp[:, None, :], gen_live)
    gen_bar = batched(regroup(gen_live), recoupling)
    ham_bar = batched(regroup(ham_live), recoupling)
    ph_term = batched(gen_bar * weight_ph[:, None, :], ham_bar) - batched(ham_bar * weight_ph[:, None, :], gen_bar)
    turned = jnp.einsum("cij,ckj->cik", ph_term, recoupling, precision=lax.Precision.HIGHEST)
    ph_back = regroup(turned)
    return (ladder + ph_back) * block_mask
```

```python
import functools

import jax
import jax.numpy as jnp
from jax import lax
from jax.experimental import pallas as pl
from jax.experimental.pallas import tpu as pltpu
from jax.sharding import PartitionSpec as P

F32 = jnp.float32
BF16 = jnp.bfloat16
VMEM_LIMIT = 56 * 1024 * 1024
NN = ((1,), (0,))
NT = ((1,), (1,))
TILE = 256
LANES = 128


def split(x):
    high = x.astype(BF16)
    return high, (x - high.astype(F32)).astype(BF16)


def dot3(a, b, dims):
    def one(left, right):
        return lax.dot_general(left, right, (dims, ((), ())), preferred_element_type=F32)

    return one(a[0], b[0]) + (one(a[0], b[1]) + one(a[1], b[0]))


def call(kernel, out_shape, flops, **kwargs):
    return pl.pallas_call(
        kernel,
        out_shape=out_shape,
        compiler_params=pltpu.CompilerParams(vmem_limit_bytes=VMEM_LIMIT),
        cost_estimate=pl.CostEstimate(flops=flops, bytes_accessed=8_000_000, transcendentals=0),
        **kwargs,
    )


def whole(shape):
    return pl.BlockSpec(shape, lambda *_: (0,) * len(shape))


SMEM = pl.BlockSpec(memory_space=pltpu.SMEM)


def pack(source, target, count, width):
    rows = source.shape[1]
    half = width // 2
    body = rows // LANES * LANES

    def pair(step, _):
        block = source[pl.ds(pl.multiple_of(step * 2 * width, 8), 2 * width), :]
        for odd in range(2):
            part = block[odd * width : (odd + 1) * width]
            at = 0
            for lane in range(0, body, LANES):
                target[2 * step + odd, at : at + width, :] = part[:, lane : lane + LANES]
                at += width
            target[2 * step + odd, at : at + half, :] = jnp.concatenate(
                [part[:half, body:], part[half:, body:]], axis=1
            )
        return 0

    lax.fori_loop(0, count // 2, pair, 0)


def unpack(source, target, count, width):
    rows = target.shape[1]
    half = width // 2
    body = rows // LANES * LANES
    rest = rows - body

    def pair(step, _):
        parts = []
        for odd in range(2):
            at = 0
            columns = []
            for lane in range(0, body, LANES):
                columns.append(source[2 * step + odd, at : at + width, :])
                at += width
            tail = source[2 * step + odd, at : at + half, :]
            columns.append(jnp.concatenate([tail[:, :rest], tail[:, rest:]], axis=0))
            parts.append(jnp.concatenate(columns, axis=1))
        target[pl.ds(pl.multiple_of(step * 2 * width, 8), 2 * width), :] = jnp.concatenate(parts, axis=0)
        return 0

    lax.fori_loop(0, count // 2, pair, 0)


def encode_kernel(count, width, where_ref, x_ref, out_ref, turned):
    rows, order = x_ref.shape
    size, row_index = where_ref[0], where_ref[1]
    for start in range(0, order, TILE):
        block = x_ref[:, start : start + TILE]
        row = lax.broadcasted_iota(jnp.int32, block.shape, 0) + row_index * rows
        column = lax.broadcasted_iota(jnp.int32, block.shape, 1) + start
        live = jnp.where((row < size) & (column < size), block, 0.0)
        turned[start : start + TILE, :] = live.T
    pack(turned, out_ref, count, width)


def encode(x, where, count):
    rows, order = x.shape
    width = order // count
    depth = -(-(rows * width // LANES) // 8) * 8
    return call(
        functools.partial(encode_kernel, count, width),
        jax.ShapeDtypeStruct((count, depth, LANES), F32),
        1000,
        in_specs=[SMEM, whole(x.shape)],
        out_specs=whole((count, depth, LANES)),
        scratch_shapes=[pltpu.VMEM((order, rows), F32)],
        grid=(1,),
    )(where, x)


def bar_kernel(count, width, message_ref, recouple_ref, out_ref, turned, high, low):
    order = recouple_ref.shape[0]

    @pl.when(pl.program_id(0) == 0)
    def _():
        unpack(message_ref, turned, count, width)
        for start in range(0, order, TILE):
            piece = split(turned[start : start + TILE, :].T)
            high[:, start : start + TILE] = piece[0]
            low[:, start : start + TILE] = piece[1]

    out_ref[...] = dot3((high[...], low[...]), split(recouple_ref[...]), NN)


def bar(message, recoupling, rows):
    order = recoupling.shape[0]
    count = message.shape[0]
    return call(
        functools.partial(bar_kernel, count, order // count),
        jax.ShapeDtypeStruct((rows, order), F32),
        6 * rows * order * order,
        in_specs=[whole(message.shape), pl.BlockSpec((order, TILE), lambda n: (0, n))],
        out_specs=pl.BlockSpec((rows, TILE), lambda n: (0, n)),
        scratch_shapes=[
            pltpu.VMEM((order, rows), F32),
            pltpu.VMEM((rows, order), BF16),
            pltpu.VMEM((rows, order), BF16),
        ],
        grid=(order // TILE,),
    )(message, recoupling)


def ladder_kernel(where_ref, gen_ref, ham_ref, first_ref, second_ref, out_ref, left_high, left_low, right_high, right_low):
    rows, order = gen_ref.shape
    size, row_index = where_ref[0], where_ref[1]

    @pl.when(pl.program_id(0) == 0)
    def _():
        position = lax.broadcasted_iota(jnp.int32, (1, order), 1)
        weight = jnp.where(position < size, (first_ref[...] + second_ref[...] - 1).astype(F32), 0.0)
        mine = weight[:, :rows]
        for other in range(1, order // rows):
            mine = jnp.where(row_index == other, weight[:, other * rows : (other + 1) * rows], mine)
        for place, (left, right) in enumerate(((gen_ref, ham_ref), (ham_ref, gen_ref))):
            span = slice(place * rows, (place + 1) * rows)
            for start in range(0, order, TILE):
                piece = split(left[:, start : start + TILE].T * mine)
                left_high[start : start + TILE, span] = piece[0]
                left_low[start : start + TILE, span] = piece[1]
            right_high[span, :], right_low[span, :] = split(right[...])

    columns = pl.ds(pl.multiple_of(pl.program_id(0) * TILE, TILE), TILE)
    out_ref[...] = dot3((left_high[...], left_low[...]), (right_high[:, columns], right_low[:, columns]), NN)


def ladder_part(gen, ham, first, second, where):
    rows, order = gen.shape
    return call(
        ladder_kernel,
        jax.ShapeDtypeStruct((order, order), F32),
        12 * rows * order * order,
        in_specs=[SMEM, whole(gen.shape), whole(gen.shape), whole((1, order)), whole((1, order))],
        out_specs=pl.BlockSpec((order, TILE), lambda n: (0, n)),
        scratch_shapes=[pltpu.VMEM((order, 2 * rows), BF16)] * 2 + [pltpu.VMEM((2 * rows, order), BF16)] * 2,
        grid=(order // TILE,),
    )(where, gen, ham, first, second)


def commutator_kernel(gen_ref, ham_ref, first_ref, second_ref, gen_all, ham_all, out_ref, gen_high, gen_low, ham_high, ham_low):
    @pl.when(pl.program_id(0) == 0)
    def _():
        weight = (first_ref[...] - second_ref[...]).astype(F32)
        gen_high[...], gen_low[...] = split(gen_ref[...] * weight)
        ham_high[...], ham_low[...] = split(ham_ref[...] * weight)

    out_ref[...] = dot3((gen_high[...], gen_low[...]), split(ham_all[...]), NN) - dot3(
        (ham_high[...], ham_low[...]), split(gen_all[...]), NN
    )


def commutator(gen, ham, first, second, gen_all, ham_all):
    rows, order = gen.shape
    tall = pl.BlockSpec((order, TILE), lambda n: (0, n))
    return call(
        commutator_kernel,
        jax.ShapeDtypeStruct((rows, order), F32),
        12 * rows * order * order,
        in_specs=[whole(gen.shape), whole(gen.shape), whole((1, order)), whole((1, order)), tall, tall],
        out_specs=pl.BlockSpec((rows, TILE), lambda n: (0, n)),
        scratch_shapes=[pltpu.VMEM((rows, order), BF16)] * 4,
        grid=(order // TILE,),
    )(gen, ham, first, second, gen_all, ham_all)


def turn_kernel(count, width, term_ref, recouple_ref, out_ref, high, low, turned):
    @pl.when(pl.program_id(0) == 0)
    def _():
        high[...], low[...] = split(term_ref[...])

    turned[...] = dot3(split(recouple_ref[...]), (high[...], low[...]), NT)
    pack(turned, out_ref, count, width)


def turn(term, recoupling, count):
    rows, order = term.shape
    width = order // count
    steps = 4
    depth = -(-(rows * width // LANES) // 8) * 8
    return call(
        functools.partial(turn_kernel, count // steps, width),
        jax.ShapeDtypeStruct((count, depth, LANES), F32),
        6 * rows * order * order,
        in_specs=[whole(term.shape), pl.BlockSpec((order // steps, order), lambda n: (n, 0))],
        out_specs=pl.BlockSpec((count // steps, depth, LANES), lambda n: (n, 0, 0)),
        scratch_shapes=[
            pltpu.VMEM((rows, order), BF16),
            pltpu.VMEM((rows, order), BF16),
            pltpu.VMEM((order // steps, rows), F32),
        ],
        grid=(steps,),
    )(term, recoupling)


def finish_kernel(count, width, where_ref, message_ref, ladder_ref, out_ref, turned):
    rows, order = out_ref.shape
    size, row_index = where_ref[0], where_ref[1]
    unpack(message_ref, turned, count, width)
    for start in range(0, order, TILE):
        span = slice(start, start + TILE)
        total = ladder_ref[:, span] + turned[span, :].T
        row = lax.broadcasted_iota(jnp.int32, total.shape, 0) + row_index * rows
        column = lax.broadcasted_iota(jnp.int32, total.shape, 1) + start
        out_ref[:, span] = jnp.where((row < size) & (column < size), total, 0.0)


def finish(message, ladder, where):
    rows, order = ladder.shape
    count = message.shape[0]
    return call(
        functools.partial(finish_kernel, count, order // count),
        jax.ShapeDtypeStruct((rows, order), F32),
        1000,
        in_specs=[SMEM, whole(message.shape), whole(ladder.shape)],
        out_specs=whole(ladder.shape),
        scratch_shapes=[pltpu.VMEM((order, rows), F32)],
        grid=(1,),
    )(where, message, ladder)


def exchange(message):
    return lax.all_to_all(message, "chan", 0, 0, tiled=True)


def gather(x):
    return lax.all_gather(x, "row", axis=0, tiled=True)


def shards(generator, hamiltonian, recoupling, channel_size, hole_first, hole_second):
    gen, ham, recouple = generator[0], hamiltonian[0], recoupling[0]
    rows = gen.shape[0]
    count = lax.axis_size("chan")
    where = jnp.stack([channel_size[0], lax.axis_index("row").astype(jnp.int32)])
    gen_moved = exchange(encode(gen, where, count))
    ham_moved = exchange(encode(ham, where, count))
    part = ladder_part(gen, ham, hole_first, hole_second, where)
    ladder = lax.psum_scatter(part, "row", scatter_dimension=0, tiled=True)
    gen_bar = bar(gen_moved, recouple, rows)
    gen_all = gather(gen_bar)
    ham_bar = bar(ham_moved, recouple, rows)
    ham_all = gather(ham_bar)
    term = commutator(gen_bar, ham_bar, hole_first, hole_second, gen_all, ham_all)
    back = exchange(turn(term, recouple, count))
    return finish(back, ladder, where)[None]


def solution(mesh):
    in_specs = (
        P("chan", "row", None),
        P("chan", "row", None),
        P("chan", None, None),
        P("chan"),
        P("chan", None),
        P("chan", None),
    )
    out_specs = P("chan", "row", None)
    return jax.shard_map(shards, mesh=mesh, in_specs=in_specs, out_specs=out_specs, check_vma=False)
```

```python
import functools

import jax
import jax.numpy as jnp
from jax import lax
from jax.experimental import pallas as pl
from jax.experimental.pallas import tpu as pltpu
from jax.sharding import PartitionSpec as P

F32 = jnp.float32
BF16 = jnp.bfloat16
VMEM_LIMIT = 56 * 1024 * 1024
NN = ((1,), (0,))
NT = ((1,), (1,))
TILE = 256
LANES = 128
FAST = 1000


def split(x):
    high = x.astype(BF16)
    return high, (x - high.astype(F32)).astype(BF16)


def dot3(a, b, dims):
    def one(left, right):
        return lax.dot_general(left, right, (dims, ((), ())), preferred_element_type=F32)

    return one(a[0], b[0]) + (one(a[0], b[1]) + one(a[1], b[0]))


def call(kernel, out_shape, flops, inputs, in_specs, after=(), **kwargs):
    first, last = len(inputs), len(inputs) + len(after)

    def body(*refs):
        kernel(*refs[:first], *refs[last:])

    return pl.pallas_call(
        body,
        out_shape=out_shape,
        in_specs=list(in_specs) + [pl.BlockSpec(memory_space=pl.ANY)] * len(after),
        compiler_params=pltpu.CompilerParams(vmem_limit_bytes=VMEM_LIMIT),
        cost_estimate=pl.CostEstimate(flops=flops, bytes_accessed=8_000_000, transcendentals=0),
        **kwargs,
    )(*inputs, *after)


def whole(shape):
    return pl.BlockSpec(shape, lambda *_: (0,) * len(shape))


SMEM = pl.BlockSpec(memory_space=pltpu.SMEM)


def pack(source, target, count, width):
    rows = source.shape[1]
    half = width // 2
    body = rows // LANES * LANES

    def pair(step, _):
        block = source[pl.ds(pl.multiple_of(step * 2 * width, 8), 2 * width), :]
        for odd in range(2):
            part = block[odd * width : (odd + 1) * width]
            at = 0
            for lane in range(0, body, LANES):
                target[2 * step + odd, at : at + width, :] = part[:, lane : lane + LANES]
                at += width
            target[2 * step + odd, at : at + half, :] = jnp.concatenate(
                [part[:half, body:], part[half:, body:]], axis=1
            )
        return 0

    lax.fori_loop(0, count // 2, pair, 0)


def unpack(source, target, count, width):
    rows = target.shape[1]
    half = width // 2
    body = rows // LANES * LANES
    rest = rows - body

    def pair(step, _):
        parts = []
        for odd in range(2):
            at = 0
            columns = []
            for lane in range(0, body, LANES):
                columns.append(source[2 * step + odd, at : at + width, :])
                at += width
            tail = source[2 * step + odd, at : at + half, :]
            columns.append(jnp.concatenate([tail[:, :rest], tail[:, rest:]], axis=0))
            parts.append(jnp.concatenate(columns, axis=1))
        target[pl.ds(pl.multiple_of(step * 2 * width, 8), 2 * width), :] = jnp.concatenate(parts, axis=0)
        return 0

    lax.fori_loop(0, count // 2, pair, 0)


def encode_kernel(count, width, where_ref, x_ref, out_ref, turned):
    rows, order = x_ref.shape
    size, row_index = where_ref[0], where_ref[1]
    for start in range(0, order, TILE):
        block = x_ref[:, start : start + TILE]
        row = lax.broadcasted_iota(jnp.int32, block.shape, 0) + row_index * rows
        column = lax.broadcasted_iota(jnp.int32, block.shape, 1) + start
        live = jnp.where((row < size) & (column < size), block, 0.0)
        turned[start : start + TILE, :] = live.T
    pack(turned, out_ref, count, width)


def encode(x, where, count, after=()):
    rows, order = x.shape
    width = order // count
    depth = -(-(rows * width // LANES) // 8) * 8
    return call(
        functools.partial(encode_kernel, count, width),
        jax.ShapeDtypeStruct((count, depth, LANES), F32),
        FAST,
        (where, x),
        [SMEM, whole(x.shape)],
        after,
        out_specs=whole((count, depth, LANES)),
        scratch_shapes=[pltpu.VMEM((order, rows), F32)],
        grid=(1,),
    )


def bar_kernel(count, width, message_ref, recouple_ref, *refs):
    outs, (turned, high, low) = refs[:-3], refs[-3:]
    order = recouple_ref.shape[0]

    @pl.when(pl.program_id(0) == 0)
    def _():
        unpack(message_ref, turned, count, width)
        for start in range(0, order, TILE):
            piece = split(turned[start : start + TILE, :].T)
            high[:, start : start + TILE] = piece[0]
            low[:, start : start + TILE] = piece[1]

    product = dot3((high[...], low[...]), split(recouple_ref[...]), NN)
    if len(outs) == 1:
        outs[0][...] = product
        return
    for step, out in enumerate(outs):

        @pl.when(pl.program_id(0) == step)
        def _():
            out[...] = product


def bar(message, recoupling, rows, halves, after=()):
    order = recoupling.shape[0]
    count = message.shape[0]
    tile = order // 2 if halves else TILE
    if halves:
        out_shape = [jax.ShapeDtypeStruct((rows, tile), F32)] * 2
        out_specs = [whole((rows, tile))] * 2
    else:
        out_shape = jax.ShapeDtypeStruct((rows, order), F32)
        out_specs = pl.BlockSpec((rows, TILE), lambda n: (0, n))
    return call(
        functools.partial(bar_kernel, count, order // count),
        out_shape,
        6 * rows * order * order,
        (message, recoupling),
        [whole(message.shape), pl.BlockSpec((order, tile), lambda n: (0, n))],
        after,
        out_specs=out_specs,
        scratch_shapes=[
            pltpu.VMEM((order, rows), F32),
            pltpu.VMEM((rows, order), BF16),
            pltpu.VMEM((rows, order), BF16),
        ],
        grid=(order // tile,),
    )


def ladder_kernel(cut, where_ref, gen_ref, ham_ref, first_ref, second_ref, early_ref, late_ref, left_high, left_low, right_high, right_low):
    rows, order = gen_ref.shape
    size, row_index = where_ref[0], where_ref[1]
    step = pl.program_id(0)

    @pl.when(step == 0)
    def _():
        position = lax.broadcasted_iota(jnp.int32, (1, order), 1)
        weight = jnp.where(position < size, (first_ref[...] + second_ref[...] - 1).astype(F32), 0.0)
        mine = weight[:, :rows]
        for other in range(1, order // rows):
            mine = jnp.where(row_index == other, weight[:, other * rows : (other + 1) * rows], mine)
        for place, (left, right) in enumerate(((gen_ref, ham_ref), (ham_ref, gen_ref))):
            span = slice(place * rows, (place + 1) * rows)
            for start in range(0, order, TILE):
                piece = split(left[:, start : start + TILE].T * mine)
                left_high[start : start + TILE, span] = piece[0]
                left_low[start : start + TILE, span] = piece[1]
            right_high[span, :], right_low[span, :] = split(right[...])

    columns = pl.ds(pl.multiple_of(step * TILE, TILE), TILE)
    product = dot3((left_high[...], left_low[...]), (right_high[:, columns], right_low[:, columns]), NN)

    @pl.when(step < cut)
    def _():
        early_ref[...] = product

    @pl.when(step >= cut)
    def _():
        late_ref[...] = product


def ladder_part(gen, ham, first, second, where, after=()):
    rows, order = gen.shape
    steps = order // TILE
    cut = steps // 2
    return call(
        functools.partial(ladder_kernel, cut),
        [
            jax.ShapeDtypeStruct((order, cut * TILE), F32),
            jax.ShapeDtypeStruct((order, (steps - cut) * TILE), F32),
        ],
        12 * rows * order * order,
        (where, gen, ham, first, second),
        [SMEM, whole(gen.shape), whole(gen.shape), whole((1, order)), whole((1, order))],
        after,
        out_specs=[
            pl.BlockSpec((order, TILE), lambda n: (0, jnp.minimum(n, cut - 1))),
            pl.BlockSpec((order, TILE), lambda n: (0, jnp.maximum(n - cut, 0))),
        ],
        scratch_shapes=[pltpu.VMEM((order, 2 * rows), BF16)] * 2 + [pltpu.VMEM((2 * rows, order), BF16)] * 2,
        grid=(steps,),
    )


def weighted(first_ref, second_ref):
    return (first_ref[...] - second_ref[...]).astype(F32)


def local_kernel(gen_all, low_ref, high_ref, first_ref, second_ref, out_ref, ham_high, ham_low):
    half = low_ref.shape[1]

    @pl.when(pl.program_id(0) == 0)
    def _():
        weight = weighted(first_ref, second_ref)
        for place, ref in enumerate((low_ref, high_ref)):
            span = slice(place * half, (place + 1) * half)
            ham_high[:, span], ham_low[:, span] = split(ref[...] * weight[:, span])

    out_ref[...] = dot3((ham_high[...], ham_low[...]), split(gen_all[...]), NN)


def local_term(gen_all, ham_halves, first, second, after=()):
    rows, half = ham_halves[0].shape
    order = 2 * half
    return call(
        local_kernel,
        jax.ShapeDtypeStruct((rows, order), F32),
        6 * rows * order * order,
        (gen_all, *ham_halves, first, second),
        [pl.BlockSpec((order, TILE), lambda n: (0, n))]
        + [whole((rows, half))] * 2
        + [whole((1, order))] * 2,
        after,
        out_specs=pl.BlockSpec((rows, TILE), lambda n: (0, n)),
        scratch_shapes=[pltpu.VMEM((rows, order), BF16)] * 2,
        grid=(order // TILE,),
    )


def pair_kernel(pick_ref, gen_ref, own_ref, got_ref, first_ref, second_ref, out_ref, right_high, right_low):
    rows, order = gen_ref.shape
    half = order // 2
    kind = pick_ref[2]
    scaled = gen_ref[...] * weighted(first_ref, second_ref)
    outer = jnp.concatenate([scaled[:, :rows], scaled[:, order - rows :]], axis=1)
    inner = scaled[:, rows : order - rows]
    ends = jnp.where(kind == 2, scaled[:, :half], scaled[:, half:])
    left = split(jnp.where(kind == 0, outer, jnp.where(kind == 1, inner, ends)))
    own_at = pl.multiple_of(pick_ref[1], 64)
    got_at = pl.multiple_of(rows - pick_ref[1], 64)
    for at, ref in ((own_at, own_ref), (got_at, got_ref)):
        right_high[pl.ds(at, rows), :], right_low[pl.ds(at, rows), :] = split(ref[...])
    out_ref[...] = dot3(left, (right_high[...], right_low[...]), NN)


def pair_product(pick, gen_all, own, got, first, second, after=()):
    rows, half = own.shape
    order = 2 * half
    inputs = (gen_all, own, got, first, second)
    count = 1 + len(inputs)

    def body(*refs):
        pair_kernel(*refs[:count], *refs[count + len(after) :])

    def fixed(shape):
        return pl.BlockSpec(shape, lambda n, pick: (0, 0))

    return pl.pallas_call(
        body,
        out_shape=jax.ShapeDtypeStruct((rows, half), F32),
        grid_spec=pltpu.PrefetchScalarGridSpec(
            num_scalar_prefetch=1,
            grid=(1,),
            in_specs=[
                pl.BlockSpec((rows, order), lambda n, pick: (pick[0], 0)),
                fixed((rows, half)),
                fixed((rows, half)),
                fixed((1, order)),
                fixed((1, order)),
            ]
            + [pl.BlockSpec(memory_space=pl.ANY)] * len(after),
            out_specs=fixed((rows, half)),
            scratch_shapes=[pltpu.VMEM((2 * rows, half), BF16)] * 2,
        ),
        compiler_params=pltpu.CompilerParams(vmem_limit_bytes=VMEM_LIMIT),
        cost_estimate=pl.CostEstimate(
            flops=6 * rows * half * half, bytes_accessed=6_000_000, transcendentals=0
        ),
    )(pick, *inputs, *after)


def turn_kernel(count, width, *refs):
    own, got, local_ref, recouple_ref, out_ref, high, low, turned = refs[:2], refs[2:4], *refs[4:]
    half = own[0].shape[1]

    @pl.when(pl.program_id(0) == 0)
    def _():
        for place in range(2):
            span = slice(place * half, (place + 1) * half)
            high[:, span], low[:, span] = split(own[place][...] + got[place][...] - local_ref[:, span])

    turned[...] = dot3(split(recouple_ref[...]), (high[...], low[...]), NT)
    pack(turned, out_ref, count, width)


def turn(own, got, local, recoupling, count, after=()):
    rows, order = local.shape
    width = order // count
    steps = 4
    depth = -(-(rows * width // LANES) // 8) * 8
    return call(
        functools.partial(turn_kernel, count // steps, width),
        jax.ShapeDtypeStruct((count, depth, LANES), F32),
        6 * rows * order * order,
        (*own, *got, local, recoupling),
        [whole(own[0].shape)] * 4
        + [whole(local.shape), pl.BlockSpec((order // steps, order), lambda n: (n, 0))],
        after,
        out_specs=pl.BlockSpec((count // steps, depth, LANES), lambda n: (n, 0, 0)),
        scratch_shapes=[
            pltpu.VMEM((rows, order), BF16),
            pltpu.VMEM((rows, order), BF16),
            pltpu.VMEM((order // steps, rows), F32),
        ],
        grid=(steps,),
    )


def finish_kernel(count, width, where_ref, message_ref, early_ref, late_ref, out_ref, turned):
    rows, order = out_ref.shape
    size, row_index = where_ref[0], where_ref[1]
    cut = early_ref.shape[1]
    unpack(message_ref, turned, count, width)
    for start in range(0, order, TILE):
        span = slice(start, start + TILE)
        ladder = early_ref[:, span] if start < cut else late_ref[:, start - cut : start - cut + TILE]
        total = ladder + turned[span, :].T
        row = lax.broadcasted_iota(jnp.int32, total.shape, 0) + row_index * rows
        column = lax.broadcasted_iota(jnp.int32, total.shape, 1) + start
        out_ref[:, span] = jnp.where((row < size) & (column < size), total, 0.0)


def finish(message, early, late, where):
    rows = early.shape[0]
    order = early.shape[1] + late.shape[1]
    count = message.shape[0]
    return call(
        functools.partial(finish_kernel, count, order // count),
        jax.ShapeDtypeStruct((rows, order), F32),
        FAST,
        (where, message, early, late),
        [SMEM, whole(message.shape), whole(early.shape), whole(late.shape)],
        out_specs=whole((rows, order)),
        scratch_shapes=[pltpu.VMEM((order, rows), F32)],
        grid=(1,),
    )


def hold_kernel(x_ref, out_ref):
    del x_ref, out_ref


def hold(x, *after):
    return call(
        hold_kernel,
        jax.ShapeDtypeStruct(x.shape, x.dtype),
        FAST,
        (x,),
        [pl.BlockSpec(memory_space=pl.ANY)],
        after,
        out_specs=pl.BlockSpec(memory_space=pl.ANY),
        input_output_aliases={0: 0},
    )


def exchange(message):
    return lax.all_to_all(message, "chan", 0, 0, tiled=True)


def reduced(part):
    return lax.psum_scatter(part, "row", scatter_dimension=0, tiled=True)


def shards(generator, hamiltonian, recoupling, channel_size, hole_first, hole_second):
    gen, ham, recouple = generator[0], hamiltonian[0], recoupling[0]
    rows = gen.shape[0]
    half = gen.shape[1] // 2
    count = lax.axis_size("chan")
    holes = (hole_first, hole_second)
    row = lax.axis_index("row").astype(jnp.int32)
    where = jnp.stack([channel_size[0], row])
    near, far = row ^ 1, 3 - row
    is_outer = (row == 0) | (row == 3)
    far_own = jnp.where(row < 2, 0, rows)
    near_own = jnp.where(row % 2 == 0, 0, rows)
    far_kind = jnp.where(is_outer, 0, 1)
    near_kind = jnp.where(row < 2, 2, 3)

    def pick(block, own, kind):
        return jnp.stack([block, own, kind]).astype(jnp.int32)

    def to_near(x):
        return lax.ppermute(x, "row", [(0, 1), (1, 0), (2, 3), (3, 2)])

    def to_far(x):
        return lax.ppermute(x, "row", [(0, 3), (3, 0), (1, 2), (2, 1)])

    gen_message = encode(gen, where, count)
    gen_moved = exchange(gen_message)
    early_part, late_part = ladder_part(gen, ham, *holes, where, after=(gen_message,))
    early = reduced(early_part)
    ham_message = encode(ham, where, count, after=(early_part,))
    gen_bar = bar(gen_moved, recouple, rows, False, after=(ham_message,))
    gen_all = lax.all_gather(hold(gen_bar, early), "row", axis=0, tiled=True)
    ham_moved = exchange(hold(ham_message, gen_bar))
    ham_bar = bar(ham_moved, recouple, rows, True)
    from_far = to_far(ham_bar[0])
    from_near = to_near(ham_bar[1])
    local = local_term(gen_all, ham_bar, *holes)
    send_near = pair_product(pick(near, far_own, far_kind), gen_all, ham_bar[0], from_far, *holes, after=(local,))
    got_near = to_near(send_near)
    send_far = pair_product(pick(far, near_own, near_kind), gen_all, ham_bar[1], from_near, *holes, after=(local,))
    got_far = to_far(send_far)
    own = (
        pair_product(pick(row, far_own, far_kind), gen_all, ham_bar[0], from_far, *holes, after=(send_near, send_far)),
        pair_product(pick(row, near_own, near_kind), gen_all, ham_bar[1], from_near, *holes, after=(send_near, send_far)),
    )
    message = turn(own, (got_near, got_far), local, recouple, count)
    back = exchange(message)
    late = reduced(hold(late_part, message))
    return finish(back, early, late, where)[None]


def solution(mesh):
    in_specs = (
        P("chan", "row", None),
        P("chan", "row", None),
        P("chan", None, None),
        P("chan"),
        P("chan", None),
        P("chan", None),
    )
    out_specs = P("chan", "row", None)
    return jax.shard_map(shards, mesh=mesh, in_specs=in_specs, out_specs=out_specs, check_vma=False)
```

```python
import functools

import jax
import jax.numpy as jnp
from jax import lax
from jax.experimental import pallas as pl
from jax.experimental.pallas import tpu as pltpu
from jax.sharding import PartitionSpec as P

F32 = jnp.float32
BF16 = jnp.bfloat16
MIB = 1024 * 1024
LARGE = 62
NN = ((1,), (0,))
NT = ((1,), (1,))
TILE = 256
LANES = 128
SUB = 8
FAST = 1000
SLOW = 10**12


def split(x):
    high = x.astype(BF16)
    return high, (x - high.astype(F32)).astype(BF16)


def dot3(a, b, dims):
    def one(left, right):
        return lax.dot_general(left, right, (dims, ((), ())), preferred_element_type=F32)

    return one(a[0], b[0]) + (one(a[0], b[1]) + one(a[1], b[0]))


VMEM = pl.BlockSpec(memory_space=pltpu.VMEM)
SMEM = pl.BlockSpec(memory_space=pltpu.SMEM)
ANY = pl.BlockSpec(memory_space=pl.ANY)


def call(kernel, out_shape, mib, inputs, after=(), flops=FAST, in_specs=None, out_specs=None, scratch_shapes=(), aliases=None):
    first, last = len(inputs), len(inputs) + len(after)

    def body(*refs):
        kernel(*refs[:first], *refs[last:])

    if in_specs is None:
        in_specs = [SMEM if x.ndim == 1 else VMEM for x in inputs]
    if out_specs is None:
        out_specs = [VMEM] * len(out_shape) if isinstance(out_shape, list) else VMEM
    return pl.pallas_call(
        body,
        out_shape=out_shape,
        in_specs=list(in_specs) + [ANY] * len(after),
        out_specs=out_specs,
        scratch_shapes=list(scratch_shapes),
        input_output_aliases=aliases or {},
        compiler_params=pltpu.CompilerParams(vmem_limit_bytes=mib * MIB),
        cost_estimate=pl.CostEstimate(flops=flops, bytes_accessed=4_000_000, transcendentals=0),
    )(*inputs, *after)


def message_shape(rows, order, count):
    return jax.ShapeDtypeStruct((count, 1, rows * order // count), F32)


def upper(shape):
    return lax.broadcasted_iota(jnp.int32, shape, 0) < shape[0] // 2


def swapped(x):
    middle = x.shape[0] // 2
    return jnp.concatenate([x[middle:], x[:middle]], axis=0)


def put(target, channel, at, tile):
    target[channel, :, at : at + tile.size] = tile.reshape(1, tile.size)
    return at + tile.size


def get(source, channel, at, rows):
    return source[channel, :, at : at + rows * LANES].reshape(rows, LANES)


def lane_parts(rows):
    return [(lane, min(LANES, rows - lane)) for lane in range(0, rows, LANES)]


def pack(source, target, count, width):
    parts = lane_parts(source.shape[1])

    def pair(step, _):
        base = pl.multiple_of(step * 2 * width, SUB)
        whole = ([], [])
        last = ([], [])
        for lane, size in parts:
            tile = [source[pl.ds(base + SUB * k, SUB), lane : lane + size] for k in range(5)]
            top = upper(tile[0].shape)
            turned = [swapped(tile[k]) for k in range(2, 5)]
            whole[0].append(tile[:2])
            last[0].append(tile[2])
            whole[1].append([jnp.where(top, turned[0], turned[1]), jnp.where(top, turned[1], turned[2])])
            last[1].append(turned[2])
        top = upper((SUB, LANES))
        for odd in range(2):
            channel = 2 * step + odd
            at = 0
            for tiles in whole[odd][:-1]:
                for tile in tiles:
                    at = put(target, channel, at, tile)
            at = put(target, channel, at, jnp.concatenate(whole[odd][-1], axis=1))
            first, second, tail = last[odd]
            at = put(target, channel, at, jnp.where(top, first, swapped(second)))
            put(target, channel, at, jnp.concatenate([tail[: SUB // 4], tail[SUB // 4 : SUB // 2]], axis=1))
        return 0

    lax.fori_loop(0, count // 2, pair, 0, unroll=4)


def unpack(source, target, count, width):
    parts = lane_parts(target.shape[1])
    rest = parts[-1][1]
    size = SUB * LANES

    def pair(step, _):
        base = pl.multiple_of(step * 2 * width, SUB)
        whole = ([], [])
        last = ([], [])
        for odd in range(2):
            channel = 2 * step + odd
            at = 0
            for _ in parts[:-1]:
                whole[odd].append([get(source, channel, at, SUB), get(source, channel, at + size, SUB)])
                at += 2 * size
            tail = get(source, channel, at, SUB)
            whole[odd].append([tail[:, :rest], tail[:, rest:]])
            at += size
            shared = get(source, channel, at, SUB)
            corner = get(source, channel, at + size, SUB // 4)
            corner = [corner[:, :rest], corner[:, rest:]]
            last[odd].extend([shared, swapped(shared), jnp.concatenate(corner + corner, axis=0)])
        for place, (lane, size_) in enumerate(parts):
            even, odd = whole[0][place], [swapped(tile) for tile in whole[1][place]]
            top = upper(even[0].shape)
            tiles = even + [
                jnp.where(top, last[0][place], odd[0]),
                jnp.where(top, odd[0], odd[1]),
                jnp.where(top, odd[1], swapped(last[1][place])),
            ]
            for k, tile in enumerate(tiles):
                target[pl.ds(base + SUB * k, SUB), lane : lane + size_] = tile
        return 0

    lax.fori_loop(0, count // 2, pair, 0, unroll=4)


def live(shape, where_ref, rows, start):
    row = lax.broadcasted_iota(jnp.int32, shape, 0) + where_ref[1] * rows
    column = lax.broadcasted_iota(jnp.int32, shape, 1) + start
    return (row < where_ref[0]) & (column < where_ref[0])


def encode_kernel(count, where_ref, x_ref, out_ref, turned):
    rows, order = x_ref.shape
    for start in range(0, order, TILE):
        block = x_ref[:, start : start + TILE]
        turned[start : start + TILE, :] = jnp.where(live(block.shape, where_ref, rows, start), block, 0.0).T
    pack(turned, out_ref, count, order // count)


def encode(x, where, count, after=()):
    rows, order = x.shape
    return call(
        functools.partial(encode_kernel, count),
        message_shape(rows, order, count),
        12,
        (where, x),
        after,
        scratch_shapes=[pltpu.VMEM((order, rows), F32)],
    )


def read_kernel(message_ref, high, low, turned):
    order = turned.shape[0]
    count = message_ref.shape[0]
    unpack(message_ref, turned, count, order // count)
    for start in range(0, order, TILE):
        span = slice(start, start + TILE)
        high[:, span], low[:, span] = split(turned[span, :].T)


def read(message, rows, after=(), flops=FAST):
    order = message.shape[0] * message.shape[2] // rows
    return call(
        read_kernel,
        [jax.ShapeDtypeStruct((rows, order), BF16)] * 2,
        12,
        (message,),
        after,
        flops,
        scratch_shapes=[pltpu.VMEM((order, rows), F32)],
    )


def bar_kernel(high, low, recouple_ref, *outs):
    order = recouple_ref.shape[0]
    width = order // len(outs)
    for start in range(0, order, TILE):
        product = dot3((high[...], low[...]), split(recouple_ref[:, start : start + TILE]), NN)
        for place, out in enumerate(outs):
            begin, end = max(start, place * width), min(start + TILE, (place + 1) * width)
            if begin < end:
                out[:, begin - place * width : end - place * width] = product[:, begin - start : end - start]


def bar(moved, recoupling, parts, flops=FAST):
    rows, order = moved[0].shape
    return call(
        bar_kernel,
        [jax.ShapeDtypeStruct((rows, order // parts), F32)] * parts,
        20,
        (*moved, recoupling),
        flops=flops,
    )


def ladder_kernel(where_ref, gen_ref, ham_ref, first_ref, second_ref, early_ref, late_ref, left_high, left_low, right_high, right_low):
    rows, order = gen_ref.shape
    cut = early_ref.shape[1]
    position = lax.broadcasted_iota(jnp.int32, (1, order), 1)
    weight = jnp.where(position < where_ref[0], (first_ref[...] + second_ref[...] - 1).astype(F32), 0.0)
    mine = weight[:, :rows]
    for other in range(1, order // rows):
        mine = jnp.where(where_ref[1] == other, weight[:, other * rows : (other + 1) * rows], mine)
    for place, (left, right) in enumerate(((gen_ref, ham_ref), (ham_ref, gen_ref))):
        span = slice(place * rows, (place + 1) * rows)
        for start in range(0, order, TILE):
            piece = split(left[:, start : start + TILE].T * mine)
            left_high[start : start + TILE, span] = piece[0]
            left_low[start : start + TILE, span] = piece[1]
        right_high[span, :], right_low[span, :] = split(right[...])
    for start in range(0, order, TILE):
        columns = slice(start, start + TILE)
        right = right_high[:, columns], right_low[:, columns]
        out, at = (early_ref, start) if start < cut else (late_ref, start - cut)
        out[:, at : at + TILE] = dot3((left_high[...], left_low[...]), right, NN)


def ladder_part(gen, ham, first, second, where, after=()):
    rows, order = gen.shape
    cut = order // TILE // 2 * TILE
    return call(
        ladder_kernel,
        [jax.ShapeDtypeStruct((order, cut), F32), jax.ShapeDtypeStruct((order, order - cut), F32)],
        28,
        (where, gen, ham, first, second),
        after,
        scratch_shapes=[pltpu.VMEM((order, 2 * rows), BF16)] * 2 + [pltpu.VMEM((2 * rows, order), BF16)] * 2,
    )


def weighted(first_ref, second_ref):
    return (first_ref[...] - second_ref[...]).astype(F32)


def local_kernel(gen_all, low_ref, high_ref, first_ref, second_ref, out_ref, ham_high, ham_low):
    half = low_ref.shape[1]
    weight = weighted(first_ref, second_ref)
    for place, ref in enumerate((low_ref, high_ref)):
        span = slice(place * half, (place + 1) * half)
        ham_high[:, span], ham_low[:, span] = split(ref[...] * weight[:, span])
    for start in range(0, 2 * half, TILE):
        span = slice(start, start + TILE)
        out_ref[:, span] = dot3((ham_high[...], ham_low[...]), split(gen_all[:, span]), NN)


def local_term(gen_all, ham_halves, first, second, after=()):
    rows, half = ham_halves[0].shape
    return call(
        local_kernel,
        jax.ShapeDtypeStruct((rows, 2 * half), F32),
        16,
        (gen_all, *ham_halves, first, second),
        after,
        scratch_shapes=[pltpu.VMEM((rows, 2 * half), BF16)] * 2,
    )


def pair_kernel(pick_ref, gen_all, own_ref, got_ref, first_ref, second_ref, out_ref, right_high, right_low):
    rows, half = own_ref.shape
    order = 2 * half
    kind = pick_ref[2]
    scaled = gen_all[pl.ds(pl.multiple_of(pick_ref[0] * rows, 64), rows), :] * weighted(first_ref, second_ref)
    outer = jnp.concatenate([scaled[:, :rows], scaled[:, order - rows :]], axis=1)
    inner = scaled[:, rows : order - rows]
    ends = jnp.where(kind == 2, scaled[:, :half], scaled[:, half:])
    left = split(jnp.where(kind == 0, outer, jnp.where(kind == 1, inner, ends)))
    own_at = pl.multiple_of(pick_ref[1], 64)
    got_at = pl.multiple_of(rows - pick_ref[1], 64)
    for at, ref in ((own_at, own_ref), (got_at, got_ref)):
        right_high[pl.ds(at, rows), :], right_low[pl.ds(at, rows), :] = split(ref[...])
    out_ref[...] = dot3(left, (right_high[...], right_low[...]), NN)


def pair_product(pick, gen_all, own, got, first, second, after=()):
    rows, half = own.shape
    return call(
        pair_kernel,
        jax.ShapeDtypeStruct((rows, half), F32),
        20,
        (pick, gen_all, own, got, first, second),
        after,
        scratch_shapes=[pltpu.VMEM((2 * rows, half), BF16)] * 2,
    )


def turn_kernel(count, *refs):
    own, got, local_ref, recouple_ref, out_ref, token_ref, high, low, turned = refs[:2], refs[2:4], *refs[4:]
    token_ref[...] = jnp.zeros_like(token_ref)
    half = own[0].shape[1]
    for place in range(2):
        span = slice(place * half, (place + 1) * half)
        high[:, span], low[:, span] = split(own[place][...] + got[place][...] - local_ref[:, span])
    order = recouple_ref.shape[0]
    for start in range(0, order, TILE):
        span = slice(start, start + TILE)
        turned[span, :] = dot3((high[...], low[...]), split(recouple_ref[span, :]), NT).T
    pack(turned, out_ref, count, order // count)


def turn(own, got, local, recoupling, count, after=()):
    rows, order = local.shape
    return call(
        functools.partial(turn_kernel, count),
        [message_shape(rows, order, count), jax.ShapeDtypeStruct((SUB, LANES), F32)],
        24,
        (*own, *got, local, recoupling),
        after,
        scratch_shapes=[
            pltpu.VMEM((rows, order), BF16),
            pltpu.VMEM((rows, order), BF16),
            pltpu.VMEM((order, rows), F32),
        ],
    )


def finish_kernel(where_ref, message_ref, early_hbm, late_hbm, out_ref, turned, ladder_ref, arrived):
    rows, order = out_ref.shape
    cut = early_hbm.shape[1]
    count = message_ref.shape[0]
    copies = [
        pltpu.make_async_copy(early_hbm, ladder_ref.at[:, pl.ds(0, cut)], arrived.at[0]),
        pltpu.make_async_copy(late_hbm, ladder_ref.at[:, pl.ds(cut, order - cut)], arrived.at[1]),
    ]
    for copy in copies:
        copy.start()
    unpack(message_ref, turned, count, order // count)
    for copy in copies:
        copy.wait()
    for start in range(0, order, TILE):
        span = slice(start, start + TILE)
        total = ladder_ref[:, span] + turned[span, :].T
        out_ref[:, span] = jnp.where(live(total.shape, where_ref, rows, start), total, 0.0)


def finish(message, early, late, where):
    rows = early.shape[0]
    order = early.shape[1] + late.shape[1]
    return call(
        finish_kernel,
        jax.ShapeDtypeStruct((rows, order), F32),
        LARGE,
        (where, message, early, late),
        in_specs=[SMEM, VMEM, ANY, ANY],
        scratch_shapes=[
            pltpu.VMEM((order, rows), F32),
            pltpu.VMEM((rows, order), F32),
            pltpu.SemaphoreType.DMA((2,)),
        ],
    )


def hold_kernel(x_ref, out_ref):
    del x_ref, out_ref


def hold(x, after, mib):
    return call(
        hold_kernel,
        jax.ShapeDtypeStruct(x.shape, x.dtype),
        mib,
        (x,),
        (after,),
        in_specs=[ANY],
        out_specs=ANY,
        aliases={0: 0},
    )


def exchange(message):
    return lax.all_to_all(message, "chan", 0, 0, tiled=True)


def reduced(part):
    return lax.psum_scatter(part, "row", scatter_dimension=0, tiled=True)


def shards(generator, hamiltonian, recoupling, channel_size, hole_first, hole_second):
    gen, ham, recouple = generator[0], hamiltonian[0], recoupling[0]
    rows = gen.shape[0]
    count = lax.axis_size("chan")
    holes = (hole_first, hole_second)
    row = lax.axis_index("row").astype(jnp.int32)
    where = jnp.stack([channel_size[0], row])
    far_own, far_kind = jnp.where(row < 2, 0, rows), jnp.where((row == 0) | (row == 3), 0, 1)
    near_own, near_kind = jnp.where(row % 2 == 0, 0, rows), jnp.where(row < 2, 2, 3)

    def far_pick(block):
        return jnp.stack([block, far_own, far_kind]).astype(jnp.int32)

    def near_pick(block):
        return jnp.stack([block, near_own, near_kind]).astype(jnp.int32)

    def to_near(x):
        return lax.ppermute(x, "row", [(0, 1), (1, 0), (2, 3), (3, 2)])

    def to_far(x):
        return lax.ppermute(x, "row", [(0, 3), (3, 0), (1, 2), (2, 1)])

    gen_message = encode(gen, where, count)
    gen_moved = exchange(gen_message)
    early_part, late_part = ladder_part(gen, ham, *holes, where, after=(gen_message,))
    early = reduced(early_part)
    ham_message = encode(ham, where, count, after=(early_part,))
    (gen_bar,) = bar(read(gen_moved, rows, after=(ham_message,), flops=SLOW), recouple, 1)
    gen_sent = hold(gen_bar, early, LARGE)
    gen_all = lax.all_gather(gen_sent, "row", axis=0, tiled=True)
    ham_moved = exchange(hold(ham_message, gen_sent, 2))
    ham_bar = bar(read(ham_moved, rows), recouple, 2)
    from_far = to_far(ham_bar[0])
    from_near = to_near(ham_bar[1])
    local = local_term(gen_all, ham_bar, *holes)
    send_near = pair_product(far_pick(row ^ 1), gen_all, ham_bar[0], from_far, *holes, after=(local,))
    got_near = to_near(send_near)
    send_far = pair_product(near_pick(3 - row), gen_all, ham_bar[1], from_near, *holes, after=(local,))
    got_far = to_far(send_far)
    sent = (send_near, send_far)
    own = (
        pair_product(far_pick(row), gen_all, ham_bar[0], from_far, *holes, after=sent),
        pair_product(near_pick(row), gen_all, ham_bar[1], from_near, *holes, after=sent),
    )
    message, token = turn(own, (got_near, got_far), local, recouple, count)
    back = exchange(message)
    late = reduced(hold(late_part, token, LARGE))
    return finish(back, early, late, where)[None]


def solution(mesh):
    in_specs = (
        P("chan", "row", None),
        P("chan", "row", None),
        P("chan", None, None),
        P("chan"),
        P("chan", None),
        P("chan", None),
    )
    out_specs = P("chan", "row", None)
    return jax.shard_map(shards, mesh=mesh, in_specs=in_specs, out_specs=out_specs, check_vma=False)
```

```python
import functools

import jax
import jax.numpy as jnp
from jax import lax
from jax.experimental import pallas as pl
from jax.experimental.pallas import tpu as pltpu
from jax.sharding import PartitionSpec as P

F32 = jnp.float32
BF16 = jnp.bfloat16
MIB = 1024 * 1024
NN = ((1,), (0,))
NT = ((1,), (1,))
TILE = 256
LANES = 128
SUB = 8
FAST = 1000
SLOW = 10**12


def split(x):
    high = x.astype(BF16)
    return high, (x - high.astype(F32)).astype(BF16)


def dot3(a, b, dims):
    def one(left, right):
        return lax.dot_general(left, right, (dims, ((), ())), preferred_element_type=F32)

    return one(a[0], b[0]) + (one(a[0], b[1]) + one(a[1], b[0]))


VMEM = pl.BlockSpec(memory_space=pltpu.VMEM)
SMEM = pl.BlockSpec(memory_space=pltpu.SMEM)
ANY = pl.BlockSpec(memory_space=pl.ANY)


def call(kernel, out_shape, mib, inputs, after=(), flops=FAST, in_specs=None, out_specs=None, scratch_shapes=(), aliases=None):
    first, last = len(inputs), len(inputs) + len(after)

    def body(*refs):
        kernel(*refs[:first], *refs[last:])

    if in_specs is None:
        in_specs = [SMEM if x.ndim == 1 else VMEM for x in inputs]
    if out_specs is None:
        out_specs = [VMEM] * len(out_shape) if isinstance(out_shape, list) else VMEM
    return pl.pallas_call(
        body,
        out_shape=out_shape,
        in_specs=list(in_specs) + [ANY] * len(after),
        out_specs=out_specs,
        scratch_shapes=list(scratch_shapes),
        input_output_aliases=aliases or {},
        compiler_params=pltpu.CompilerParams(vmem_limit_bytes=mib * MIB),
        cost_estimate=pl.CostEstimate(flops=flops, bytes_accessed=4_000_000, transcendentals=0),
    )(*inputs, *after)


def message_shape(rows, order, count):
    return jax.ShapeDtypeStruct((count, 1, rows * order // count), F32)


def upper(shape):
    return lax.broadcasted_iota(jnp.int32, shape, 0) < shape[0] // 2


def swapped(x):
    middle = x.shape[0] // 2
    return jnp.concatenate([x[middle:], x[:middle]], axis=0)


def put(target, channel, at, tile):
    target[channel, :, at : at + tile.size] = tile.reshape(1, tile.size)
    return at + tile.size


def get(source, channel, at, rows):
    return source[channel, :, at : at + rows * LANES].reshape(rows, LANES)


def lane_parts(rows):
    return [(lane, min(LANES, rows - lane)) for lane in range(0, rows, LANES)]


def pack(source, target, count, width):
    parts = lane_parts(source.shape[1])

    def pair(step, _):
        base = pl.multiple_of(step * 2 * width, SUB)
        whole = ([], [])
        last = ([], [])
        for lane, size in parts:
            tile = [source[pl.ds(base + SUB * k, SUB), lane : lane + size] for k in range(5)]
            top = upper(tile[0].shape)
            turned = [swapped(tile[k]) for k in range(2, 5)]
            whole[0].append(tile[:2])
            last[0].append(tile[2])
            whole[1].append([jnp.where(top, turned[0], turned[1]), jnp.where(top, turned[1], turned[2])])
            last[1].append(turned[2])
        top = upper((SUB, LANES))
        for odd in range(2):
            channel = 2 * step + odd
            at = 0
            for tiles in whole[odd][:-1]:
                for tile in tiles:
                    at = put(target, channel, at, tile)
            at = put(target, channel, at, jnp.concatenate(whole[odd][-1], axis=1))
            first, second, tail = last[odd]
            at = put(target, channel, at, jnp.where(top, first, swapped(second)))
            put(target, channel, at, jnp.concatenate([tail[: SUB // 4], tail[SUB // 4 : SUB // 2]], axis=1))
        return 0

    lax.fori_loop(0, count // 2, pair, 0, unroll=4)


def unpack(source, target, count, width):
    parts = lane_parts(target.shape[1])
    rest = parts[-1][1]
    size = SUB * LANES

    def pair(step, _):
        base = pl.multiple_of(step * 2 * width, SUB)
        whole = ([], [])
        last = ([], [])
        for odd in range(2):
            channel = 2 * step + odd
            at = 0
            for _ in parts[:-1]:
                whole[odd].append([get(source, channel, at, SUB), get(source, channel, at + size, SUB)])
                at += 2 * size
            tail = get(source, channel, at, SUB)
            whole[odd].append([tail[:, :rest], tail[:, rest:]])
            at += size
            shared = get(source, channel, at, SUB)
            corner = get(source, channel, at + size, SUB // 4)
            corner = [corner[:, :rest], corner[:, rest:]]
            last[odd].extend([shared, swapped(shared), jnp.concatenate(corner + corner, axis=0)])
        for place, (lane, size_) in enumerate(parts):
            even, odd = whole[0][place], [swapped(tile) for tile in whole[1][place]]
            top = upper(even[0].shape)
            tiles = even + [
                jnp.where(top, last[0][place], odd[0]),
                jnp.where(top, odd[0], odd[1]),
                jnp.where(top, odd[1], swapped(last[1][place])),
            ]
            for k, tile in enumerate(tiles):
                target[pl.ds(base + SUB * k, SUB), lane : lane + size_] = tile
        return 0

    lax.fori_loop(0, count // 2, pair, 0, unroll=4)


def live(shape, where_ref, rows, start):
    row = lax.broadcasted_iota(jnp.int32, shape, 0) + where_ref[1] * rows
    column = lax.broadcasted_iota(jnp.int32, shape, 1) + start
    return (row < where_ref[0]) & (column < where_ref[0])


def encode_kernel(count, where_ref, x_ref, out_ref, turned):
    rows, order = x_ref.shape
    for start in range(0, order, TILE):
        block = x_ref[:, start : start + TILE]
        turned[start : start + TILE, :] = jnp.where(live(block.shape, where_ref, rows, start), block, 0.0).T
    pack(turned, out_ref, count, order // count)


def encode(x, where, count, after=()):
    rows, order = x.shape
    return call(
        functools.partial(encode_kernel, count),
        message_shape(rows, order, count),
        12,
        (where, x),
        after,
        scratch_shapes=[pltpu.VMEM((order, rows), F32)],
    )


def read_kernel(message_ref, high, low, turned):
    order = turned.shape[0]
    count = message_ref.shape[0]
    unpack(message_ref, turned, count, order // count)
    for start in range(0, order, TILE):
        span = slice(start, start + TILE)
        high[:, span], low[:, span] = split(turned[span, :].T)


def read(message, rows, after=(), flops=FAST):
    order = message.shape[0] * message.shape[2] // rows
    return call(
        read_kernel,
        [jax.ShapeDtypeStruct((rows, order), BF16)] * 2,
        12,
        (message,),
        after,
        flops,
        scratch_shapes=[pltpu.VMEM((order, rows), F32)],
    )


def bar_product(high, low, recouple_ref, outs):
    order = recouple_ref.shape[0]
    width = order // 2
    for start in range(0, order, TILE):
        product = dot3((high[...], low[...]), split(recouple_ref[:, start : start + TILE]), NN)
        for place, out in enumerate(outs):
            begin, end = max(start, place * width), min(start + TILE, (place + 1) * width)
            if begin < end:
                out[:, begin - place * width : end - place * width] = product[:, begin - start : end - start]


def gen_bar_kernel(high, low, recouple_ref, out_ref):
    bar_product(high, low, recouple_ref, [out_ref.at[0], out_ref.at[1]])


def ham_bar_kernel(where_ref, high, low, recouple_ref, low_ref, high_ref, across_ref):
    bar_product(high, low, recouple_ref, [low_ref, high_ref])
    rows = low_ref.shape[0]
    across = where_ref[1] ^ 2
    left = jnp.where(across < 2, low_ref[:, :rows], high_ref[:, :rows])
    right = jnp.where(across < 2, low_ref[:, rows:], high_ref[:, rows:])
    block = jnp.where(across % 2 == 0, left, right)
    across_ref[...] = jnp.concatenate([block[: rows // 2], block[rows // 2 :]], axis=1)


def gen_bar_of(moved, recoupling, after=()):
    rows, order = moved[0].shape
    return call(
        gen_bar_kernel,
        jax.ShapeDtypeStruct((2, rows, order // 2), F32),
        20,
        (*moved, recoupling),
        after,
    )


def ham_bar_of(moved, recoupling, where, after=()):
    rows, order = moved[0].shape
    half = jax.ShapeDtypeStruct((rows, order // 2), F32)
    return call(
        ham_bar_kernel,
        [half, half, jax.ShapeDtypeStruct((rows // 2, 2 * rows), F32)],
        20,
        (where, *moved, recoupling),
        after,
    )


def partners(row):
    return row ^ 1, 3 - row, row ^ 2


def ladder_kernel(where_ref, gen_ref, ham_ref, first_ref, second_ref, *refs):
    outs, (left_high, left_low, right_high, right_low) = refs[:4], refs[4:]
    rows, order = gen_ref.shape
    half = order // 2
    row = where_ref[1]
    position = lax.broadcasted_iota(jnp.int32, (1, order), 1)
    weight = jnp.where(position < where_ref[0], (first_ref[...] + second_ref[...] - 1).astype(F32), 0.0)
    mine = block_of(weight, row, rows)
    for place, (left, right) in enumerate(((gen_ref, ham_ref), (ham_ref, gen_ref))):
        span = slice(place * rows, (place + 1) * rows)
        for start in range(0, order, TILE):
            piece = split(left[:, start : start + TILE].T * mine)
            left_high[start : start + TILE, span] = piece[0]
            left_low[start : start + TILE, span] = piece[1]
        right_high[span, :], right_low[span, :] = split(right[...])
    near, far, across = partners(row)
    blocks = ((row, far), (near, across)), ((row, near), (far, across))
    for place in range(2):
        columns = slice(place * half, (place + 1) * half)
        right = right_high[:, columns], right_low[:, columns]
        for kind in range(2):
            for which in range(2):
                at = pl.ds(pl.multiple_of(blocks[place][kind][which] * rows, 64), rows)
                outs[2 * place + kind][which] = dot3((left_high[at, :], left_low[at, :]), right, NN)


def ladder_part(gen, ham, first, second, where, after=()):
    rows, order = gen.shape
    return call(
        ladder_kernel,
        [jax.ShapeDtypeStruct((2, rows, order // 2), F32)] * 4,
        28,
        (where, gen, ham, first, second),
        after,
        scratch_shapes=[pltpu.VMEM((order, 2 * rows), BF16)] * 2 + [pltpu.VMEM((2 * rows, order), BF16)] * 2,
    )


def fold_kernel(keep_low, got_low, keep_high, got_high, own_ref, far_ref, near_ref):
    half = far_ref.shape[1]
    own_ref[:, :half] = keep_low[0] + got_low[0]
    own_ref[:, half:] = keep_high[0] + got_high[0]
    far_ref[...] = keep_low[1] + got_low[1]
    near_ref[...] = keep_high[1] + got_high[1]


def fold(keep_low, got_low, keep_high, got_high):
    _, rows, half = keep_low.shape
    return call(
        fold_kernel,
        [jax.ShapeDtypeStruct((rows, 2 * half), F32)] + [jax.ShapeDtypeStruct((rows, half), F32)] * 2,
        16,
        (keep_low, got_low, keep_high, got_high),
    )


def block_of(weight, index, rows):
    picked = weight[:, :rows]
    for other in range(1, weight.shape[1] // rows):
        picked = jnp.where(index == other, weight[:, other * rows : (other + 1) * rows], picked)
    return picked


def weighted(first_ref, second_ref):
    return (first_ref[...] - second_ref[...]).astype(F32)


def local_kernel(where_ref, mine_ref, near_ref, far_ref, low_ref, high_ref, first_ref, second_ref, out_ref, *scratch):
    ham_high, ham_low, gen_high, gen_low = scratch
    rows, half = low_ref.shape
    weight = weighted(first_ref, second_ref)
    row = where_ref[1]
    near, far, across = partners(row)
    for place, ham_ref in enumerate((low_ref, high_ref)):
        span = slice(place * half, (place + 1) * half)
        ham_high[:, span], ham_low[:, span] = split(ham_ref[...] * weight[:, span])
        for gen_ref, block in ((mine_ref, row), (near_ref, near), (far_ref, far)):
            at = pl.ds(pl.multiple_of(block * rows, 64), rows)
            gen_high[at, span], gen_low[at, span] = split(gen_ref[place])
        at = pl.ds(pl.multiple_of(across * rows, 64), rows)
        gen_high[at, span] = jnp.zeros((rows, half), BF16)
        gen_low[at, span] = jnp.zeros((rows, half), BF16)
    for start in range(0, 2 * half, TILE):
        span = slice(start, start + TILE)
        out_ref[:, span] = dot3((ham_high[...], ham_low[...]), (gen_high[:, span], gen_low[:, span]), NN)


def local_term(slabs, ham_halves, first, second, where, after=()):
    rows, half = ham_halves[0].shape
    return call(
        local_kernel,
        jax.ShapeDtypeStruct((rows, 2 * half), F32),
        26,
        (where, *slabs, *ham_halves, first, second),
        after,
        scratch_shapes=[pltpu.VMEM((rows, 2 * half), BF16)] * 2 + [pltpu.VMEM((2 * half, 2 * half), BF16)] * 2,
    )


def chosen(pick_ref, gen_ref, weight):
    rows, half = gen_ref.shape[1:]
    kind = pick_ref[1]
    low, high = gen_ref[0] * weight[:, :half], gen_ref[1] * weight[:, half:]
    outer = jnp.concatenate([low[:, :rows], high[:, half - rows :]], axis=1)
    inner = jnp.concatenate([low[:, rows:], high[:, : half - rows]], axis=1)
    return jnp.where(kind == 0, outer, jnp.where(kind == 1, inner, jnp.where(kind == 2, low, high)))


def place_pair(pick_ref, own_ref, got_ref, right_high, right_low):
    rows = own_ref.shape[0]
    own_at = pl.multiple_of(pick_ref[0], 64)
    got_at = pl.multiple_of(rows - pick_ref[0], 64)
    for at, ref in ((own_at, own_ref), (got_at, got_ref)):
        right_high[pl.ds(at, rows), :], right_low[pl.ds(at, rows), :] = split(ref[...])


def pair_kernel(pick_ref, gen_ref, own_ref, got_ref, first_ref, second_ref, out_ref, right_high, right_low):
    place_pair(pick_ref, own_ref, got_ref, right_high, right_low)
    left = split(chosen(pick_ref, gen_ref, weighted(first_ref, second_ref)))
    out_ref[...] = dot3(left, (right_high[...], right_low[...]), NN)


def pair_product(pick, slab, own, got, first, second, after=()):
    rows, half = own.shape
    return call(
        pair_kernel,
        jax.ShapeDtypeStruct((rows, half), F32),
        14,
        (pick, slab, own, got, first, second),
        after,
        scratch_shapes=[pltpu.VMEM((2 * rows, half), BF16)] * 2,
    )


def send_kernel(place, pick_ref, gen_ref, own_ref, got_ref, block_ref, other_ref, first_ref, second_ref, out_ref, *scratch):
    left_high, left_low, right_high, right_low = scratch
    rows, half = own_ref.shape
    weight = weighted(first_ref, second_ref)
    place_pair(pick_ref, own_ref, got_ref, right_high, right_low)
    left_high[:, :half], left_low[:, :half] = split(chosen(pick_ref, gen_ref, weight))
    block = jnp.concatenate([block_ref[:, :rows], block_ref[:, rows:]], axis=0)
    left_high[:, half:], left_low[:, half:] = split(-block * block_of(weight, pick_ref[2], rows))
    right_high[half:, :], right_low[half:, :] = split(other_ref[place])
    out_ref[...] = dot3((left_high[...], left_low[...]), (right_high[...], right_low[...]), NN)


def send_product(place, pick, slab, own, got, block, other, first, second, after=()):
    rows, half = own.shape
    depth = half + rows
    return call(
        functools.partial(send_kernel, place),
        jax.ShapeDtypeStruct((rows, half), F32),
        18,
        (pick, slab, own, got, block, other, first, second),
        after,
        scratch_shapes=[pltpu.VMEM((rows, depth), BF16)] * 2 + [pltpu.VMEM((depth, half), BF16)] * 2,
    )


def turn_kernel(count, *refs):
    own, got, local_ref, recouple_ref, out_ref, high, low, turned = refs[:2], refs[2:4], *refs[4:]
    half = own[0].shape[1]
    for place in range(2):
        span = slice(place * half, (place + 1) * half)
        high[:, span], low[:, span] = split(own[place][...] + got[place][...] - local_ref[:, span])
    order = recouple_ref.shape[0]
    for start in range(0, order, TILE):
        span = slice(start, start + TILE)
        turned[span, :] = dot3((high[...], low[...]), split(recouple_ref[span, :]), NT).T
    pack(turned, out_ref, count, order // count)


def turn(own, got, local, recoupling, count, after=()):
    rows, order = local.shape
    return call(
        functools.partial(turn_kernel, count),
        message_shape(rows, order, count),
        24,
        (*own, *got, local, recoupling),
        after,
        scratch_shapes=[
            pltpu.VMEM((rows, order), BF16),
            pltpu.VMEM((rows, order), BF16),
            pltpu.VMEM((order, rows), F32),
        ],
    )


def finish_kernel(where_ref, message_ref, own_ref, low_ref, high_ref, out_ref, turned):
    rows, order = out_ref.shape
    half = low_ref.shape[1]
    count = message_ref.shape[0]
    unpack(message_ref, turned, count, order // count)
    for place, ref in enumerate((low_ref, high_ref)):
        for start in range(0, half, LANES):
            at = place * half + start
            span = slice(at, at + LANES)
            total = own_ref[:, span] + ref[:, start : start + LANES] + turned[span, :].T
            out_ref[:, span] = jnp.where(live(total.shape, where_ref, rows, at), total, 0.0)


def finish(message, own, low, high, where):
    rows, order = own.shape
    return call(
        finish_kernel,
        jax.ShapeDtypeStruct((rows, order), F32),
        14,
        (where, message, own, low, high),
        scratch_shapes=[pltpu.VMEM((order, rows), F32)],
    )


def exchange(message):
    return lax.all_to_all(message, "chan", 0, 0, tiled=True)


def shards(generator, hamiltonian, recoupling, channel_size, hole_first, hole_second):
    gen, ham, recouple = generator[0], hamiltonian[0], recoupling[0]
    rows = gen.shape[0]
    count = lax.axis_size("chan")
    holes = (hole_first, hole_second)
    row = lax.axis_index("row").astype(jnp.int32)
    where = jnp.stack([channel_size[0], row])
    near, far, _ = partners(row)
    far_pick = jnp.stack([jnp.where(row < 2, 0, rows), jnp.where((row == 0) | (row == 3), 0, 1), far]).astype(jnp.int32)
    near_pick = jnp.stack([jnp.where(row % 2 == 0, 0, rows), jnp.where(row < 2, 2, 3), near]).astype(jnp.int32)

    def to_near(x):
        return lax.ppermute(x, "row", [(0, 1), (1, 0), (2, 3), (3, 2)])

    def to_far(x):
        return lax.ppermute(x, "row", [(0, 3), (3, 0), (1, 2), (2, 1)])

    gen_message = encode(gen, where, count)
    gen_moved = exchange(gen_message)
    keep_low, send_low, keep_high, send_high = ladder_part(gen, ham, *holes, where, after=(gen_message,))
    got_low, got_high = to_near(send_low), to_far(send_high)
    ham_message = encode(ham, where, count, after=(send_low,))
    ham_moved = exchange(ham_message)
    gen_bar = gen_bar_of(read(gen_moved, rows, after=(ham_message,), flops=SLOW), recouple, after=(got_low, got_high))
    gen_near, gen_far = to_near(gen_bar), to_far(gen_bar)
    *ham_bar, block = ham_bar_of(read(ham_moved, rows, flops=SLOW), recouple, where, after=(gen_near, gen_far))
    from_far, block_far = to_far(ham_bar[0]), to_far(block)
    from_near, block_near = to_near(ham_bar[1]), to_near(block)
    ladder_own, ladder_far, ladder_near = fold(keep_low, got_low, keep_high, got_high)
    local = local_term((gen_bar, gen_near, gen_far), ham_bar, *holes, where, after=(ladder_far,))
    send_near = send_product(0, far_pick, gen_near, ham_bar[0], from_far, block_near, gen_far, *holes, after=(local,))
    term_near = to_near(send_near)
    send_far = send_product(1, near_pick, gen_far, ham_bar[1], from_near, block_far, gen_near, *holes, after=(local,))
    term_far = to_far(send_far)
    sent = (send_near, send_far)
    own = (
        pair_product(far_pick, gen_bar, ham_bar[0], from_far, *holes, after=sent),
        pair_product(near_pick, gen_bar, ham_bar[1], from_near, *holes, after=sent),
    )
    message = turn(own, (term_near, term_far), local, recouple, count)
    back = exchange(message)
    return finish(back, ladder_own, to_far(ladder_far), to_near(ladder_near), where)[None]


def solution(mesh):
    in_specs = (
        P("chan", "row", None),
        P("chan", "row", None),
        P("chan", None, None),
        P("chan"),
        P("chan", None),
        P("chan", None),
    )
    out_specs = P("chan", "row", None)
    return jax.shard_map(shards, mesh=mesh, in_specs=in_specs, out_specs=out_specs, check_vma=False)
```

```python
import functools

import jax
import jax.numpy as jnp
from jax import lax
from jax.experimental import pallas as pl
from jax.experimental.pallas import tpu as pltpu
from jax.sharding import PartitionSpec as P

F32 = jnp.float32
BF16 = jnp.bfloat16
MIB = 1024 * 1024
LARGE = 60
NN = ((1,), (0,))
NT = ((1,), (1,))
TILE = 256
LANES = 128
SUB = 8
FAST = 1000
SLOW = 10**12


def split(x):
    high = x.astype(BF16)
    return high, (x - high.astype(F32)).astype(BF16)


def dot3(a, b, dims):
    def one(left, right):
        return lax.dot_general(left, right, (dims, ((), ())), preferred_element_type=F32)

    return one(a[0], b[0]) + (one(a[0], b[1]) + one(a[1], b[0]))


VMEM = pl.BlockSpec(memory_space=pltpu.VMEM)
SMEM = pl.BlockSpec(memory_space=pltpu.SMEM)
ANY = pl.BlockSpec(memory_space=pl.ANY)


def call(kernel, out_shape, mib, inputs, after=(), flops=FAST, in_specs=None, out_specs=None, scratch_shapes=(), aliases=None):
    first, last = len(inputs), len(inputs) + len(after)

    def body(*refs):
        kernel(*refs[:first], *refs[last:])

    if in_specs is None:
        in_specs = [SMEM if x.ndim == 1 else VMEM for x in inputs]
    if out_specs is None:
        out_specs = [VMEM] * len(out_shape) if isinstance(out_shape, list) else VMEM
    return pl.pallas_call(
        body,
        out_shape=out_shape,
        in_specs=list(in_specs) + [ANY] * len(after),
        out_specs=out_specs,
        scratch_shapes=list(scratch_shapes),
        input_output_aliases=aliases or {},
        compiler_params=pltpu.CompilerParams(vmem_limit_bytes=mib * MIB),
        cost_estimate=pl.CostEstimate(flops=flops, bytes_accessed=4_000_000, transcendentals=0),
    )(*inputs, *after)


def message_shape(rows, order, count):
    return jax.ShapeDtypeStruct((count, 1, rows * order // count), F32)


def upper(shape):
    return lax.broadcasted_iota(jnp.int32, shape, 0) < shape[0] // 2


def swapped(x):
    middle = x.shape[0] // 2
    return jnp.concatenate([x[middle:], x[:middle]], axis=0)


def put(target, channel, at, tile):
    target[channel, :, at : at + tile.size] = tile.reshape(1, tile.size)
    return at + tile.size


def get(source, channel, at, rows):
    return source[channel, :, at : at + rows * LANES].reshape(rows, LANES)


def lane_parts(rows):
    return [(lane, min(LANES, rows - lane)) for lane in range(0, rows, LANES)]


def pack(source, target, count, width):
    parts = lane_parts(source.shape[1])

    def pair(step, _):
        base = pl.multiple_of(step * 2 * width, SUB)
        whole = ([], [])
        last = ([], [])
        for lane, size in parts:
            tile = [source[pl.ds(base + SUB * k, SUB), lane : lane + size] for k in range(5)]
            top = upper(tile[0].shape)
            turned = [swapped(tile[k]) for k in range(2, 5)]
            whole[0].append(tile[:2])
            last[0].append(tile[2])
            whole[1].append([jnp.where(top, turned[0], turned[1]), jnp.where(top, turned[1], turned[2])])
            last[1].append(turned[2])
        top = upper((SUB, LANES))
        for odd in range(2):
            channel = 2 * step + odd
            at = 0
            for tiles in whole[odd][:-1]:
                for tile in tiles:
                    at = put(target, channel, at, tile)
            at = put(target, channel, at, jnp.concatenate(whole[odd][-1], axis=1))
            first, second, tail = last[odd]
            at = put(target, channel, at, jnp.where(top, first, swapped(second)))
            put(target, channel, at, jnp.concatenate([tail[: SUB // 4], tail[SUB // 4 : SUB // 2]], axis=1))
        return 0

    lax.fori_loop(0, count // 2, pair, 0, unroll=4)


def unpack(source, target, count, width):
    parts = lane_parts(target.shape[1])
    rest = parts[-1][1]
    size = SUB * LANES

    def pair(step, _):
        base = pl.multiple_of(step * 2 * width, SUB)
        whole = ([], [])
        last = ([], [])
        for odd in range(2):
            channel = 2 * step + odd
            at = 0
            for _ in parts[:-1]:
                whole[odd].append([get(source, channel, at, SUB), get(source, channel, at + size, SUB)])
                at += 2 * size
            tail = get(source, channel, at, SUB)
            whole[odd].append([tail[:, :rest], tail[:, rest:]])
            at += size
            shared = get(source, channel, at, SUB)
            corner = get(source, channel, at + size, SUB // 4)
            corner = [corner[:, :rest], corner[:, rest:]]
            last[odd].extend([shared, swapped(shared), jnp.concatenate(corner + corner, axis=0)])
        for place, (lane, size_) in enumerate(parts):
            even, odd = whole[0][place], [swapped(tile) for tile in whole[1][place]]
            top = upper(even[0].shape)
            tiles = even + [
                jnp.where(top, last[0][place], odd[0]),
                jnp.where(top, odd[0], odd[1]),
                jnp.where(top, odd[1], swapped(last[1][place])),
            ]
            for k, tile in enumerate(tiles):
                target[pl.ds(base + SUB * k, SUB), lane : lane + size_] = tile
        return 0

    lax.fori_loop(0, count // 2, pair, 0, unroll=4)


def live(shape, where_ref, rows, start):
    row = lax.broadcasted_iota(jnp.int32, shape, 0) + where_ref[1] * rows
    column = lax.broadcasted_iota(jnp.int32, shape, 1) + start
    return (row < where_ref[0]) & (column < where_ref[0])


def encode_kernel(count, where_ref, x_ref, out_ref, turned):
    rows, order = x_ref.shape
    for start in range(0, order, TILE):
        block = x_ref[:, start : start + TILE]
        turned[start : start + TILE, :] = jnp.where(live(block.shape, where_ref, rows, start), block, 0.0).T
    pack(turned, out_ref, count, order // count)


def encode(x, where, count, after=()):
    rows, order = x.shape
    return call(
        functools.partial(encode_kernel, count),
        message_shape(rows, order, count),
        12,
        (where, x),
        after,
        scratch_shapes=[pltpu.VMEM((order, rows), F32)],
    )


def read_kernel(message_ref, high, low, turned):
    order = turned.shape[0]
    count = message_ref.shape[0]
    unpack(message_ref, turned, count, order // count)
    for start in range(0, order, TILE):
        span = slice(start, start + TILE)
        high[:, span], low[:, span] = split(turned[span, :].T)


def read(message, rows, after=(), flops=FAST):
    order = message.shape[0] * message.shape[2] // rows
    return call(
        read_kernel,
        [jax.ShapeDtypeStruct((rows, order), BF16)] * 2,
        12,
        (message,),
        after,
        flops,
        scratch_shapes=[pltpu.VMEM((order, rows), F32)],
    )


def bar_product(high, low, recouple_ref, outs):
    order = recouple_ref.shape[0]
    width = order // 2
    for start in range(0, order, TILE):
        product = dot3((high[...], low[...]), split(recouple_ref[:, start : start + TILE]), NN)
        for place, out in enumerate(outs):
            begin, end = max(start, place * width), min(start + TILE, (place + 1) * width)
            if begin < end:
                out[:, begin - place * width : end - place * width] = product[:, begin - start : end - start]


def gen_bar_kernel(high, low, recouple_ref, out_ref):
    bar_product(high, low, recouple_ref, [out_ref.at[0], out_ref.at[1]])


def ham_bar_kernel(where_ref, message_ref, recouple_hbm, low_ref, high_ref, across_ref, turned, high, low, recouple_ref, arrived):
    rows, half = low_ref.shape
    order = 2 * half
    fetches = [
        pltpu.make_async_copy(
            recouple_hbm.at[:, pl.ds(start, TILE)], recouple_ref.at[:, pl.ds(start, TILE)], arrived.at[start // TILE]
        )
        for start in range(0, order, TILE)
    ]
    for fetch in fetches:
        fetch.start()
    read_kernel(message_ref, high, low, turned)
    for fetch in fetches:
        fetch.wait()
    bar_product(high, low, recouple_ref, [low_ref, high_ref])
    across = where_ref[1] ^ 2
    left = jnp.where(across < 2, low_ref[:, :rows], high_ref[:, :rows])
    right = jnp.where(across < 2, low_ref[:, rows:], high_ref[:, rows:])
    block = jnp.where(across % 2 == 0, left, right)
    across_ref[...] = jnp.concatenate([block[: rows // 2], block[rows // 2 :]], axis=1)


def gen_bar_of(moved, recoupling, after=()):
    rows, order = moved[0].shape
    return call(
        gen_bar_kernel,
        jax.ShapeDtypeStruct((2, rows, order // 2), F32),
        20,
        (*moved, recoupling),
        after,
    )


def ham_bar_of(message, recoupling, where, rows, after=(), flops=FAST):
    order = recoupling.shape[0]
    half = jax.ShapeDtypeStruct((rows, order // 2), F32)
    return call(
        ham_bar_kernel,
        [half, half, jax.ShapeDtypeStruct((rows // 2, 2 * rows), F32)],
        LARGE,
        (where, message, recoupling),
        after,
        flops,
        in_specs=[SMEM, VMEM, ANY],
        scratch_shapes=[
            pltpu.VMEM((order, rows), F32),
            pltpu.VMEM((rows, order), BF16),
            pltpu.VMEM((rows, order), BF16),
            pltpu.VMEM((order, order), F32),
            pltpu.SemaphoreType.DMA((order // TILE,)),
        ],
    )


def partners(row):
    return row ^ 1, 3 - row, row ^ 2


def ladder_kernel(where_ref, gen_ref, ham_ref, first_ref, second_ref, *refs):
    outs, (left_high, left_low, right_high, right_low) = refs[:4], refs[4:]
    rows, order = gen_ref.shape
    half = order // 2
    row = where_ref[1]
    position = lax.broadcasted_iota(jnp.int32, (1, order), 1)
    weight = jnp.where(position < where_ref[0], (first_ref[...] + second_ref[...] - 1).astype(F32), 0.0)
    mine = block_of(weight, row, rows)
    near, far, across = partners(row)
    for place, (left, right) in enumerate(((gen_ref, ham_ref), (ham_ref, gen_ref))):
        span = slice(place * rows, (place + 1) * rows)
        for block in range(order // rows):
            spot = jnp.where(block == near, 0, jnp.where(block == row, 1, jnp.where(block == far, 2, 3)))
            high, low = split(left[:, block * rows : (block + 1) * rows].T * mine)
            at = pl.ds(pl.multiple_of(spot * rows, 64), rows)
            left_high[at, span], left_low[at, span] = high, low

            @pl.when(block == near)
            def _():
                left_high[order:, span], left_low[order:, span] = high, low

        right_high[span, :], right_low[span, :] = split(right[...])
    for place, starts in enumerate(((1, 3), (0, 2))):
        columns = slice(place * half, (place + 1) * half)
        right = right_high[:, columns], right_low[:, columns]
        for kind, start in enumerate(starts):
            at = slice(start * rows, (start + 2) * rows)
            outs[2 * place + kind][...] = dot3((left_high[at, :], left_low[at, :]), right, NN).reshape(2, rows, half)


def ladder_part(gen, ham, first, second, where, after=()):
    rows, order = gen.shape
    return call(
        ladder_kernel,
        [jax.ShapeDtypeStruct((2, rows, order // 2), F32)] * 4,
        LARGE,
        (where, gen, ham, first, second),
        after,
        scratch_shapes=[pltpu.VMEM((order + rows, 2 * rows), BF16)] * 2
        + [pltpu.VMEM((2 * rows, order), BF16)] * 2,
    )


def fold_kernel(keep_low, got_low, keep_high, got_high, own_ref, far_ref, near_ref):
    half = far_ref.shape[1]
    own_ref[:, :half] = keep_low[0] + got_low[1]
    own_ref[:, half:] = keep_high[1] + got_high[0]
    far_ref[...] = keep_low[1] + got_low[0]
    near_ref[...] = keep_high[0] + got_high[1]


def fold(keep_low, got_low, keep_high, got_high):
    _, rows, half = keep_low.shape
    return call(
        fold_kernel,
        [jax.ShapeDtypeStruct((rows, 2 * half), F32)] + [jax.ShapeDtypeStruct((rows, half), F32)] * 2,
        16,
        (keep_low, got_low, keep_high, got_high),
    )


def block_of(weight, index, rows):
    picked = weight[:, :rows]
    for other in range(1, weight.shape[1] // rows):
        picked = jnp.where(index == other, weight[:, other * rows : (other + 1) * rows], picked)
    return picked


def weighted(first_ref, second_ref):
    return (first_ref[...] - second_ref[...]).astype(F32)


def local_kernel(where_ref, mine_ref, near_ref, far_ref, low_ref, high_ref, first_ref, second_ref, out_ref, *scratch):
    ham_high, ham_low, gen_high, gen_low = scratch
    rows, half = low_ref.shape
    weight = weighted(first_ref, second_ref)
    row = where_ref[1]
    near, far, across = partners(row)
    for place, ham_ref in enumerate((low_ref, high_ref)):
        span = slice(place * half, (place + 1) * half)
        ham_high[:, span], ham_low[:, span] = split(ham_ref[...] * weight[:, span])
        for gen_ref, block in ((mine_ref, row), (near_ref, near), (far_ref, far)):
            at = pl.ds(pl.multiple_of(block * rows, 64), rows)
            gen_high[at, span], gen_low[at, span] = split(gen_ref[place])
        at = pl.ds(pl.multiple_of(across * rows, 64), rows)
        gen_high[at, span] = jnp.zeros((rows, half), BF16)
        gen_low[at, span] = jnp.zeros((rows, half), BF16)
    for start in range(0, 2 * half, TILE):
        span = slice(start, start + TILE)
        out_ref[:, span] = dot3((ham_high[...], ham_low[...]), (gen_high[:, span], gen_low[:, span]), NN)


def local_term(slabs, ham_halves, first, second, where, after=()):
    rows, half = ham_halves[0].shape
    return call(
        local_kernel,
        jax.ShapeDtypeStruct((rows, 2 * half), F32),
        26,
        (where, *slabs, *ham_halves, first, second),
        after,
        scratch_shapes=[pltpu.VMEM((rows, 2 * half), BF16)] * 2 + [pltpu.VMEM((2 * half, 2 * half), BF16)] * 2,
    )


def chosen(pick_ref, gen_ref, weight):
    rows, half = gen_ref.shape[1:]
    kind = pick_ref[1]
    low, high = gen_ref[0] * weight[:, :half], gen_ref[1] * weight[:, half:]
    outer = jnp.concatenate([low[:, :rows], high[:, half - rows :]], axis=1)
    inner = jnp.concatenate([low[:, rows:], high[:, : half - rows]], axis=1)
    return jnp.where(kind == 0, outer, jnp.where(kind == 1, inner, jnp.where(kind == 2, low, high)))


def place_pair(pick_ref, own_ref, got_ref, right_high, right_low):
    rows = own_ref.shape[0]
    own_at = pl.multiple_of(pick_ref[0], 64)
    got_at = pl.multiple_of(rows - pick_ref[0], 64)
    for at, ref in ((own_at, own_ref), (got_at, got_ref)):
        right_high[pl.ds(at, rows), :], right_low[pl.ds(at, rows), :] = split(ref[...])


def pair_kernel(pick_ref, gen_ref, own_ref, got_ref, first_ref, second_ref, out_ref, right_high, right_low):
    place_pair(pick_ref, own_ref, got_ref, right_high, right_low)
    left = split(chosen(pick_ref, gen_ref, weighted(first_ref, second_ref)))
    for start in range(0, out_ref.shape[1], TILE):
        span = slice(start, min(start + TILE, out_ref.shape[1]))
        out_ref[:, span] = dot3(left, (right_high[:, span], right_low[:, span]), NN)


def pair_product(pick, slab, own, got, first, second, after=()):
    rows, half = own.shape
    return call(
        pair_kernel,
        jax.ShapeDtypeStruct((rows, half), F32),
        14,
        (pick, slab, own, got, first, second),
        after,
        scratch_shapes=[pltpu.VMEM((2 * rows, half), BF16)] * 2,
    )


def send_kernel(place, pick_ref, gen_ref, own_ref, got_ref, block_ref, other_ref, first_ref, second_ref, out_ref, *scratch):
    left_high, left_low, right_high, right_low = scratch
    rows, half = own_ref.shape
    weight = weighted(first_ref, second_ref)
    place_pair(pick_ref, own_ref, got_ref, right_high, right_low)
    left_high[:, :half], left_low[:, :half] = split(chosen(pick_ref, gen_ref, weight))
    block = jnp.concatenate([block_ref[:, :rows], block_ref[:, rows:]], axis=0)
    left_high[:, half:], left_low[:, half:] = split(-block * block_of(weight, pick_ref[2], rows))
    right_high[half:, :], right_low[half:, :] = split(other_ref[place])
    for start in range(0, half, TILE):
        span = slice(start, min(start + TILE, half))
        out_ref[:, span] = dot3((left_high[...], left_low[...]), (right_high[:, span], right_low[:, span]), NN)


def send_product(place, pick, slab, own, got, block, other, first, second, after=()):
    rows, half = own.shape
    depth = half + rows
    return call(
        functools.partial(send_kernel, place),
        jax.ShapeDtypeStruct((rows, half), F32),
        18,
        (pick, slab, own, got, block, other, first, second),
        after,
        scratch_shapes=[pltpu.VMEM((rows, depth), BF16)] * 2 + [pltpu.VMEM((depth, half), BF16)] * 2,
    )


def turn_kernel(count, *refs):
    own, got, local_ref, recouple_ref, out_ref, high, low, turned = refs[:2], refs[2:4], *refs[4:]
    half = own[0].shape[1]
    for place in range(2):
        span = slice(place * half, (place + 1) * half)
        high[:, span], low[:, span] = split(own[place][...] + got[place][...] - local_ref[:, span])
    order = recouple_ref.shape[0]
    for start in range(0, order, TILE):
        span = slice(start, start + TILE)
        turned[span, :] = dot3((high[...], low[...]), split(recouple_ref[span, :]), NT).T
    pack(turned, out_ref, count, order // count)


def turn(own, got, local, recoupling, count, after=()):
    rows, order = local.shape
    return call(
        functools.partial(turn_kernel, count),
        message_shape(rows, order, count),
        24,
        (*own, *got, local, recoupling),
        after,
        scratch_shapes=[
            pltpu.VMEM((rows, order), BF16),
            pltpu.VMEM((rows, order), BF16),
            pltpu.VMEM((order, rows), F32),
        ],
    )


def finish_kernel(where_ref, message_ref, own_hbm, low_hbm, high_hbm, out_ref, turned, own_ref, part_ref, arrived):
    rows, order = out_ref.shape
    half = low_hbm.shape[1]
    count = message_ref.shape[0]
    copies = [
        pltpu.make_async_copy(own_hbm, own_ref, arrived.at[0]),
        pltpu.make_async_copy(low_hbm, part_ref.at[0], arrived.at[1]),
        pltpu.make_async_copy(high_hbm, part_ref.at[1], arrived.at[2]),
    ]
    for copy in copies:
        copy.start()
    unpack(message_ref, turned, count, order // count)
    for copy in copies:
        copy.wait()
    for place in range(2):
        for start in range(0, half, LANES):
            at = place * half + start
            span = slice(at, at + LANES)
            total = own_ref[:, span] + part_ref[place, :, start : start + LANES] + turned[span, :].T
            out_ref[:, span] = jnp.where(live(total.shape, where_ref, rows, at), total, 0.0)


def finish(message, own, low, high, where):
    rows, order = own.shape
    return call(
        finish_kernel,
        jax.ShapeDtypeStruct((rows, order), F32),
        LARGE,
        (where, message, own, low, high),
        in_specs=[SMEM, VMEM, ANY, ANY, ANY],
        scratch_shapes=[
            pltpu.VMEM((order, rows), F32),
            pltpu.VMEM((rows, order), F32),
            pltpu.VMEM((2, rows, order // 2), F32),
            pltpu.SemaphoreType.DMA((3,)),
        ],
    )


def hold_kernel(*refs):
    del refs


def hold(arrays, after):
    count = len(arrays)
    return call(
        hold_kernel,
        [jax.ShapeDtypeStruct(x.shape, x.dtype) for x in arrays],
        2,
        arrays,
        after,
        in_specs=[ANY] * count,
        out_specs=[ANY] * count,
        aliases={k: k for k in range(count)},
    )


def exchange(message):
    return lax.all_to_all(message, "chan", 0, 0, tiled=True)


def shards(generator, hamiltonian, recoupling, channel_size, hole_first, hole_second):
    gen, ham, recouple = generator[0], hamiltonian[0], recoupling[0]
    rows = gen.shape[0]
    count = lax.axis_size("chan")
    holes = (hole_first, hole_second)
    row = lax.axis_index("row").astype(jnp.int32)
    where = jnp.stack([channel_size[0], row])
    near, far, _ = partners(row)
    far_pick = jnp.stack([jnp.where(row < 2, 0, rows), jnp.where((row == 0) | (row == 3), 0, 1), far]).astype(jnp.int32)
    near_pick = jnp.stack([jnp.where(row % 2 == 0, 0, rows), jnp.where(row < 2, 2, 3), near]).astype(jnp.int32)

    def to_near(x):
        return lax.ppermute(x, "row", [(0, 1), (1, 0), (2, 3), (3, 2)])

    def to_far(x):
        return lax.ppermute(x, "row", [(0, 3), (3, 0), (1, 2), (2, 1)])

    gen_message = encode(gen, where, count)
    gen_moved = exchange(gen_message)
    keep_low, send_low, keep_high, send_high = ladder_part(gen, ham, *holes, where, after=(gen_message,))
    got_low, got_high = to_near(send_low), to_far(send_high)
    ham_message = encode(ham, where, count, after=(send_low,))
    ham_moved = exchange(ham_message)
    gen_bar = gen_bar_of(read(gen_moved, rows, after=(ham_message,), flops=SLOW), recouple)
    (gen_bar,) = hold((gen_bar,), (got_low, got_high))
    gen_near, gen_far = to_near(gen_bar), to_far(gen_bar)
    *ham_bar, block = ham_bar_of(ham_moved, recouple, where, rows, flops=SLOW)
    *ham_bar, block = hold((*ham_bar, block), (gen_near, gen_far))
    from_far, block_far = to_far(ham_bar[0]), to_far(block)
    from_near, block_near = to_near(ham_bar[1]), to_near(block)
    ladder_own, ladder_far, ladder_near = fold(keep_low, got_low, keep_high, got_high)
    local = local_term((gen_bar, gen_near, gen_far), ham_bar, *holes, where, after=(ladder_far,))
    send_near = send_product(0, far_pick, gen_near, ham_bar[0], from_far, block_near, gen_far, *holes, after=(local,))
    term_near = to_near(send_near)
    send_far = send_product(1, near_pick, gen_far, ham_bar[1], from_near, block_far, gen_near, *holes, after=(local,))
    term_far = to_far(send_far)
    sent = (send_near, send_far)
    own = (
        pair_product(far_pick, gen_bar, ham_bar[0], from_far, *holes, after=sent),
        pair_product(near_pick, gen_bar, ham_bar[1], from_near, *holes, after=sent),
    )
    message = turn(own, (term_near, term_far), local, recouple, count)
    back = exchange(message)
    return finish(back, ladder_own, to_far(ladder_far), to_near(ladder_near), where)[None]


def solution(mesh):
    in_specs = (
        P("chan", "row", None),
        P("chan", "row", None),
        P("chan", None, None),
        P("chan"),
        P("chan", None),
        P("chan", None),
    )
    out_specs = P("chan", "row", None)
    return jax.shard_map(shards, mesh=mesh, in_specs=in_specs, out_specs=out_specs, check_vma=False)
```

```python
import functools

import jax
import jax.numpy as jnp
from jax import lax
from jax.experimental import pallas as pl
from jax.experimental.pallas import tpu as pltpu
from jax.sharding import PartitionSpec as P

F32 = jnp.float32
BF16 = jnp.bfloat16
MIB = 1024 * 1024
LARGE = 60
LARGEST = 62
NN = ((1,), (0,))
NT = ((1,), (1,))
TILE = 256
LANES = 128
SUB = 8
FAST = 1000
SLOW = 10**12


def split(x):
    high = x.astype(BF16)
    return high, (x - high.astype(F32)).astype(BF16)


def dot3(a, b, dims):
    def one(left, right):
        return lax.dot_general(left, right, (dims, ((), ())), preferred_element_type=F32)

    return one(a[0], b[0]) + (one(a[0], b[1]) + one(a[1], b[0]))


VMEM = pl.BlockSpec(memory_space=pltpu.VMEM)
SMEM = pl.BlockSpec(memory_space=pltpu.SMEM)
ANY = pl.BlockSpec(memory_space=pl.ANY)


def call(kernel, out_shape, mib, inputs, after=(), flops=FAST, in_specs=None, out_specs=None, scratch_shapes=(), aliases=None):
    first, last = len(inputs), len(inputs) + len(after)

    def body(*refs):
        kernel(*refs[:first], *refs[last:])

    if in_specs is None:
        in_specs = [SMEM if x.ndim == 1 else VMEM for x in inputs]
    if out_specs is None:
        out_specs = [VMEM] * len(out_shape) if isinstance(out_shape, list) else VMEM
    return pl.pallas_call(
        body,
        out_shape=out_shape,
        in_specs=list(in_specs) + [ANY] * len(after),
        out_specs=out_specs,
        scratch_shapes=list(scratch_shapes),
        input_output_aliases=aliases or {},
        compiler_params=pltpu.CompilerParams(vmem_limit_bytes=mib * MIB),
        cost_estimate=pl.CostEstimate(flops=flops, bytes_accessed=4_000_000, transcendentals=0),
    )(*inputs, *after)


def message_shape(rows, order, count):
    return jax.ShapeDtypeStruct((count, 1, rows * order // count), F32)


def upper(shape):
    return lax.broadcasted_iota(jnp.int32, shape, 0) < shape[0] // 2


def swapped(x):
    middle = x.shape[0] // 2
    return jnp.concatenate([x[middle:], x[:middle]], axis=0)


def put(target, channel, at, tile):
    target[channel, :, at : at + tile.size] = tile.reshape(1, tile.size)
    return at + tile.size


def get(source, channel, at, rows):
    return source[channel, :, at : at + rows * LANES].reshape(rows, LANES)


def lane_parts(rows):
    return [(lane, min(LANES, rows - lane)) for lane in range(0, rows, LANES)]


def pack(source, target, count, width):
    parts = lane_parts(source.shape[1])

    def pair(step, _):
        base = pl.multiple_of(step * 2 * width, SUB)
        whole = ([], [])
        last = ([], [])
        for lane, size in parts:
            tile = [source[pl.ds(base + SUB * k, SUB), lane : lane + size] for k in range(5)]
            top = upper(tile[0].shape)
            turned = [swapped(tile[k]) for k in range(2, 5)]
            whole[0].append(tile[:2])
            last[0].append(tile[2])
            whole[1].append([jnp.where(top, turned[0], turned[1]), jnp.where(top, turned[1], turned[2])])
            last[1].append(turned[2])
        top = upper((SUB, LANES))
        for odd in range(2):
            channel = 2 * step + odd
            at = 0
            for tiles in whole[odd][:-1]:
                for tile in tiles:
                    at = put(target, channel, at, tile)
            at = put(target, channel, at, jnp.concatenate(whole[odd][-1], axis=1))
            first, second, tail = last[odd]
            at = put(target, channel, at, jnp.where(top, first, swapped(second)))
            put(target, channel, at, jnp.concatenate([tail[: SUB // 4], tail[SUB // 4 : SUB // 2]], axis=1))
        return 0

    lax.fori_loop(0, count // 2, pair, 0, unroll=4)


def unpack(source, target, count, width):
    parts = lane_parts(target.shape[1])
    rest = parts[-1][1]
    size = SUB * LANES

    def pair(step, _):
        base = pl.multiple_of(step * 2 * width, SUB)
        whole = ([], [])
        last = ([], [])
        for odd in range(2):
            channel = 2 * step + odd
            at = 0
            for _ in parts[:-1]:
                whole[odd].append([get(source, channel, at, SUB), get(source, channel, at + size, SUB)])
                at += 2 * size
            tail = get(source, channel, at, SUB)
            whole[odd].append([tail[:, :rest], tail[:, rest:]])
            at += size
            shared = get(source, channel, at, SUB)
            corner = get(source, channel, at + size, SUB // 4)
            corner = [corner[:, :rest], corner[:, rest:]]
            last[odd].extend([shared, swapped(shared), jnp.concatenate(corner + corner, axis=0)])
        for place, (lane, size_) in enumerate(parts):
            even, odd = whole[0][place], [swapped(tile) for tile in whole[1][place]]
            top = upper(even[0].shape)
            tiles = even + [
                jnp.where(top, last[0][place], odd[0]),
                jnp.where(top, odd[0], odd[1]),
                jnp.where(top, odd[1], swapped(last[1][place])),
            ]
            for k, tile in enumerate(tiles):
                target[pl.ds(base + SUB * k, SUB), lane : lane + size_] = tile
        return 0

    lax.fori_loop(0, count // 2, pair, 0, unroll=4)


def live(shape, where_ref, rows, start):
    row = lax.broadcasted_iota(jnp.int32, shape, 0) + where_ref[1] * rows
    column = lax.broadcasted_iota(jnp.int32, shape, 1) + start
    return (row < where_ref[0]) & (column < where_ref[0])


def encode_kernel(count, where_ref, x_hbm, out_ref, x_ref, turned, arrived):
    rows, order = x_ref.shape
    fetches = [
        pltpu.make_async_copy(x_hbm.at[:, pl.ds(start, TILE)], x_ref.at[:, pl.ds(start, TILE)], arrived.at[start // TILE])
        for start in range(0, order, TILE)
    ]
    for fetch in fetches:
        fetch.start()
    for start, fetch in zip(range(0, order, TILE), fetches):
        fetch.wait()
        block = x_ref[:, start : start + TILE]
        turned[start : start + TILE, :] = jnp.where(live(block.shape, where_ref, rows, start), block, 0.0).T
    pack(turned, out_ref, count, order // count)


def encode(x, where, count, after=()):
    rows, order = x.shape
    return call(
        functools.partial(encode_kernel, count),
        message_shape(rows, order, count),
        LARGEST,
        (where, x),
        after,
        in_specs=[SMEM, ANY],
        scratch_shapes=[
            pltpu.VMEM((rows, order), F32),
            pltpu.VMEM((order, rows), F32),
            pltpu.SemaphoreType.DMA((order // TILE,)),
        ],
    )


def read_kernel(message_ref, high, low, turned):
    order = turned.shape[0]
    count = message_ref.shape[0]
    unpack(message_ref, turned, count, order // count)
    for start in range(0, order, TILE):
        span = slice(start, start + TILE)
        high[:, span], low[:, span] = split(turned[span, :].T)


def read(message, rows, after=(), flops=FAST):
    order = message.shape[0] * message.shape[2] // rows
    return call(
        read_kernel,
        [jax.ShapeDtypeStruct((rows, order), BF16)] * 2,
        12,
        (message,),
        after,
        flops,
        scratch_shapes=[pltpu.VMEM((order, rows), F32)],
    )


def bar_product(high, low, recouple_ref, outs):
    order = recouple_ref.shape[0]
    width = order // 2
    for start in range(0, order, TILE):
        product = dot3((high[...], low[...]), split(recouple_ref[:, start : start + TILE]), NN)
        for place, out in enumerate(outs):
            begin, end = max(start, place * width), min(start + TILE, (place + 1) * width)
            if begin < end:
                out[:, begin - place * width : end - place * width] = product[:, begin - start : end - start]


def gen_bar_kernel(high, low, recouple_ref, out_ref):
    bar_product(high, low, recouple_ref, [out_ref.at[0], out_ref.at[1]])


def ham_bar_kernel(where_ref, message_ref, recouple_hbm, low_ref, high_ref, across_ref, turned, high, low, recouple_ref, arrived):
    rows, half = low_ref.shape
    order = 2 * half
    fetches = [
        pltpu.make_async_copy(
            recouple_hbm.at[:, pl.ds(start, TILE)], recouple_ref.at[:, pl.ds(start, TILE)], arrived.at[start // TILE]
        )
        for start in range(0, order, TILE)
    ]
    for fetch in fetches:
        fetch.start()
    read_kernel(message_ref, high, low, turned)
    for fetch in fetches:
        fetch.wait()
    bar_product(high, low, recouple_ref, [low_ref, high_ref])
    across = where_ref[1] ^ 2
    left = jnp.where(across < 2, low_ref[:, :rows], high_ref[:, :rows])
    right = jnp.where(across < 2, low_ref[:, rows:], high_ref[:, rows:])
    block = jnp.where(across % 2 == 0, left, right)
    across_ref[...] = jnp.concatenate([block[: rows // 2], block[rows // 2 :]], axis=1)


def gen_bar_of(moved, recoupling, after=()):
    rows, order = moved[0].shape
    return call(
        gen_bar_kernel,
        jax.ShapeDtypeStruct((2, rows, order // 2), F32),
        20,
        (*moved, recoupling),
        after,
    )


def ham_bar_of(message, recoupling, where, rows, after=(), flops=FAST):
    order = recoupling.shape[0]
    half = jax.ShapeDtypeStruct((rows, order // 2), F32)
    return call(
        ham_bar_kernel,
        [half, half, jax.ShapeDtypeStruct((rows // 2, 2 * rows), F32)],
        LARGE,
        (where, message, recoupling),
        after,
        flops,
        in_specs=[SMEM, VMEM, ANY],
        scratch_shapes=[
            pltpu.VMEM((order, rows), F32),
            pltpu.VMEM((rows, order), BF16),
            pltpu.VMEM((rows, order), BF16),
            pltpu.VMEM((order, order), F32),
            pltpu.SemaphoreType.DMA((order // TILE,)),
        ],
    )


def partners(row):
    return row ^ 1, 3 - row, row ^ 2


def ladder_kernel(where_ref, gen_ref, ham_ref, first_ref, second_ref, *refs):
    outs, (left_high, left_low, right_high, right_low) = refs[:4], refs[4:]
    rows, order = gen_ref.shape
    half = order // 2
    row = where_ref[1]
    position = lax.broadcasted_iota(jnp.int32, (1, order), 1)
    weight = jnp.where(position < where_ref[0], (first_ref[...] + second_ref[...] - 1).astype(F32), 0.0)
    mine = block_of(weight, row, rows)
    near, far, across = partners(row)
    for place, (left, right) in enumerate(((gen_ref, ham_ref), (ham_ref, gen_ref))):
        span = slice(place * rows, (place + 1) * rows)
        for block in range(order // rows):
            spot = jnp.where(block == near, 0, jnp.where(block == row, 1, jnp.where(block == far, 2, 3)))
            high, low = split(left[:, block * rows : (block + 1) * rows].T * mine)
            at = pl.ds(pl.multiple_of(spot * rows, 64), rows)
            left_high[at, span], left_low[at, span] = high, low

            @pl.when(block == near)
            def _():
                left_high[order:, span], left_low[order:, span] = high, low

        right_high[span, :], right_low[span, :] = split(right[...])
    for place, starts in enumerate(((1, 3), (0, 2))):
        columns = slice(place * half, (place + 1) * half)
        right = right_high[:, columns], right_low[:, columns]
        for kind, start in enumerate(starts):
            at = slice(start * rows, (start + 2) * rows)
            outs[2 * place + kind][...] = dot3((left_high[at, :], left_low[at, :]), right, NN).reshape(2, rows, half)


def ladder_part(gen, ham, first, second, where, after=()):
    rows, order = gen.shape
    return call(
        ladder_kernel,
        [jax.ShapeDtypeStruct((2, rows, order // 2), F32)] * 4,
        LARGE,
        (where, gen, ham, first, second),
        after,
        scratch_shapes=[pltpu.VMEM((order + rows, 2 * rows), BF16)] * 2
        + [pltpu.VMEM((2 * rows, order), BF16)] * 2,
    )


def fold_kernel(keep_low, got_low, keep_high, got_high, own_ref, far_ref, near_ref):
    half = far_ref.shape[1]
    own_ref[:, :half] = keep_low[0] + got_low[1]
    own_ref[:, half:] = keep_high[1] + got_high[0]
    far_ref[...] = keep_low[1] + got_low[0]
    near_ref[...] = keep_high[0] + got_high[1]


def fold(keep_low, got_low, keep_high, got_high):
    _, rows, half = keep_low.shape
    return call(
        fold_kernel,
        [jax.ShapeDtypeStruct((rows, 2 * half), F32)] + [jax.ShapeDtypeStruct((rows, half), F32)] * 2,
        16,
        (keep_low, got_low, keep_high, got_high),
    )


def block_of(weight, index, rows):
    picked = weight[:, :rows]
    for other in range(1, weight.shape[1] // rows):
        picked = jnp.where(index == other, weight[:, other * rows : (other + 1) * rows], picked)
    return picked


def weighted(first_ref, second_ref):
    return (first_ref[...] - second_ref[...]).astype(F32)


def local_kernel(where_ref, mine_ref, near_ref, far_ref, low_ref, high_ref, first_ref, second_ref, out_ref, *scratch):
    ham_high, ham_low, gen_high, gen_low = scratch
    rows, half = low_ref.shape
    weight = weighted(first_ref, second_ref)
    row = where_ref[1]
    near, far, across = partners(row)
    for place, ham_ref in enumerate((low_ref, high_ref)):
        span = slice(place * half, (place + 1) * half)
        ham_high[:, span], ham_low[:, span] = split(ham_ref[...] * weight[:, span])
        for gen_ref, block in ((mine_ref, row), (near_ref, near), (far_ref, far)):
            at = pl.ds(pl.multiple_of(block * rows, 64), rows)
            gen_high[at, span], gen_low[at, span] = split(gen_ref[place])
        at = pl.ds(pl.multiple_of(across * rows, 64), rows)
        gen_high[at, span] = jnp.zeros((rows, half), BF16)
        gen_low[at, span] = jnp.zeros((rows, half), BF16)
    for start in range(0, 2 * half, TILE):
        span = slice(start, start + TILE)
        out_ref[:, span] = dot3((ham_high[...], ham_low[...]), (gen_high[:, span], gen_low[:, span]), NN)


def local_term(slabs, ham_halves, first, second, where, after=()):
    rows, half = ham_halves[0].shape
    return call(
        local_kernel,
        jax.ShapeDtypeStruct((rows, 2 * half), F32),
        26,
        (where, *slabs, *ham_halves, first, second),
        after,
        scratch_shapes=[pltpu.VMEM((rows, 2 * half), BF16)] * 2 + [pltpu.VMEM((2 * half, 2 * half), BF16)] * 2,
    )


def chosen(pick_ref, gen_ref, weight):
    rows, half = gen_ref.shape[1:]
    kind = pick_ref[1]
    low, high = gen_ref[0] * weight[:, :half], gen_ref[1] * weight[:, half:]
    outer = jnp.concatenate([low[:, :rows], high[:, half - rows :]], axis=1)
    inner = jnp.concatenate([low[:, rows:], high[:, : half - rows]], axis=1)
    return jnp.where(kind == 0, outer, jnp.where(kind == 1, inner, jnp.where(kind == 2, low, high)))


def place_pair(pick_ref, own_ref, got_ref, right_high, right_low):
    rows = own_ref.shape[0]
    own_at = pl.multiple_of(pick_ref[0], 64)
    got_at = pl.multiple_of(rows - pick_ref[0], 64)
    for at, ref in ((own_at, own_ref), (got_at, got_ref)):
        right_high[pl.ds(at, rows), :], right_low[pl.ds(at, rows), :] = split(ref[...])


def pair_kernel(place, pick_ref, gen_ref, own_ref, got_ref, local_ref, first_ref, second_ref, out_ref, right_high, right_low):
    half = own_ref.shape[1]
    place_pair(pick_ref, own_ref, got_ref, right_high, right_low)
    left = split(chosen(pick_ref, gen_ref, weighted(first_ref, second_ref)))
    for start in range(0, half, TILE):
        end = min(start + TILE, half)
        local = local_ref[:, place * half + start : place * half + end]
        out_ref[:, start:end] = dot3(left, (right_high[:, start:end], right_low[:, start:end]), NN) - local


def pair_product(place, pick, slab, own, got, local, first, second, after=()):
    rows, half = own.shape
    return call(
        functools.partial(pair_kernel, place),
        jax.ShapeDtypeStruct((rows, half), F32),
        16,
        (pick, slab, own, got, local, first, second),
        after,
        scratch_shapes=[pltpu.VMEM((2 * rows, half), BF16)] * 2,
    )


def columns_of(gen_ref, index, weight):
    rows = gen_ref.shape[1]
    left = jnp.where(index < 2, gen_ref[0, :, :rows], gen_ref[1, :, :rows])
    right = jnp.where(index < 2, gen_ref[0, :, rows:], gen_ref[1, :, rows:])
    return jnp.where(index % 2 == 0, left, right) * block_of(weight, index, rows)


def ready_kernel(where_ref, near_ref, far_ref, low_ref, high_ref, first_ref, second_ref, *outs):
    rows, half = low_ref.shape
    weight = weighted(first_ref, second_ref)
    row = where_ref[1]
    near, far, _ = partners(row)
    sides = ((near_ref, far_ref, low_ref, far), (far_ref, near_ref, high_ref, near))
    for place, (gen_ref, other_ref, ham_ref, index) in enumerate(sides):
        part, left_high, left_low, right_high, right_low = outs[5 * place : 5 * place + 5]
        left = split(columns_of(gen_ref, row, weight))
        for start in range(0, half, TILE):
            span = slice(start, min(start + TILE, half))
            part[:, span] = dot3(left, split(ham_ref[:, span]), NN)
        left_high[...], left_low[...] = split(columns_of(gen_ref, index, weight))
        right_high[...], right_low[...] = split(other_ref[place])


def ready(where, gen_near, gen_far, ham_halves, first, second):
    rows, half = ham_halves[0].shape
    side = (
        [jax.ShapeDtypeStruct((rows, half), F32)]
        + [jax.ShapeDtypeStruct((rows, rows), BF16)] * 2
        + [jax.ShapeDtypeStruct((rows, half), BF16)] * 2
    )
    outs = call(
        ready_kernel,
        side * 2,
        24,
        (where, gen_near, gen_far, *ham_halves, first, second),
    )
    return outs[:5], outs[5:]


def send_kernel(pick_ref, part_ref, first_high, first_low, other_high, other_low, got_ref, block_ref, first_ref, second_ref, out_ref, *scratch):
    left_high, left_low, right_high, right_low = scratch
    rows, half = got_ref.shape
    weight = block_of(weighted(first_ref, second_ref), pick_ref[2], rows)
    block = jnp.concatenate([block_ref[:, :rows], block_ref[:, rows:]], axis=0)
    left_high[:, :rows], left_low[:, :rows] = first_high[...], first_low[...]
    left_high[:, rows:], left_low[:, rows:] = split(-block * weight)
    right_high[:rows, :], right_low[:rows, :] = split(got_ref[...])
    right_high[rows:, :], right_low[rows:, :] = other_high[...], other_low[...]
    for start in range(0, half, TILE):
        span = slice(start, min(start + TILE, half))
        product = dot3((left_high[...], left_low[...]), (right_high[:, span], right_low[:, span]), NN)
        out_ref[:, span] = part_ref[:, span] + product


def send_product(pick, prepared, got, block, first, second, after=()):
    rows, half = got.shape
    return call(
        send_kernel,
        jax.ShapeDtypeStruct((rows, half), F32),
        18,
        (pick, *prepared, got, block, first, second),
        after,
        scratch_shapes=[pltpu.VMEM((rows, 2 * rows), BF16)] * 2 + [pltpu.VMEM((2 * rows, half), BF16)] * 2,
    )


def halves_kernel(x_ref, high, low):
    for start in range(0, x_ref.shape[0], TILE):
        span = slice(start, start + TILE)
        high[span, :], low[span, :] = split(x_ref[span, :])


def halves(x, after=()):
    return call(halves_kernel, [jax.ShapeDtypeStruct(x.shape, BF16)] * 2, 16, (x,), after)


def turn_kernel(count, *refs):
    own, got, (high_ref, low_ref, out_ref, high, low, turned) = refs[:2], refs[2:4], refs[4:]
    half = own[0].shape[1]
    for place in range(2):
        span = slice(place * half, (place + 1) * half)
        high[:, span], low[:, span] = split(own[place][...] + got[place][...])
    order = high_ref.shape[0]
    for start in range(0, order, TILE):
        span = slice(start, start + TILE)
        turned[span, :] = dot3((high[...], low[...]), (high_ref[span, :], low_ref[span, :]), NT).T
    pack(turned, out_ref, count, order // count)


def turn(own, got, recouple_parts, count, after=()):
    rows, half = own[0].shape
    order = 2 * half
    return call(
        functools.partial(turn_kernel, count),
        message_shape(rows, order, count),
        24,
        (*own, *got, *recouple_parts),
        after,
        scratch_shapes=[
            pltpu.VMEM((rows, order), BF16),
            pltpu.VMEM((rows, order), BF16),
            pltpu.VMEM((order, rows), F32),
        ],
    )


def finish_kernel(where_ref, message_ref, own_hbm, low_hbm, high_hbm, out_ref, turned, own_ref, part_ref, arrived):
    rows, order = out_ref.shape
    half = low_hbm.shape[1]
    count = message_ref.shape[0]
    copies = [
        pltpu.make_async_copy(own_hbm, own_ref, arrived.at[0]),
        pltpu.make_async_copy(low_hbm, part_ref.at[0], arrived.at[1]),
        pltpu.make_async_copy(high_hbm, part_ref.at[1], arrived.at[2]),
    ]
    for copy in copies:
        copy.start()
    unpack(message_ref, turned, count, order // count)
    for copy in copies:
        copy.wait()
    for place in range(2):
        for start in range(0, half, LANES):
            at = place * half + start
            span = slice(at, at + LANES)
            total = own_ref[:, span] + part_ref[place, :, start : start + LANES] + turned[span, :].T
            out_ref[:, span] = jnp.where(live(total.shape, where_ref, rows, at), total, 0.0)


def finish(message, own, low, high, where):
    rows, order = own.shape
    return call(
        finish_kernel,
        jax.ShapeDtypeStruct((rows, order), F32),
        LARGEST,
        (where, message, own, low, high),
        in_specs=[SMEM, VMEM, ANY, ANY, ANY],
        scratch_shapes=[
            pltpu.VMEM((order, rows), F32),
            pltpu.VMEM((rows, order), F32),
            pltpu.VMEM((2, rows, order // 2), F32),
            pltpu.SemaphoreType.DMA((3,)),
        ],
    )


def hold_kernel(*refs):
    del refs


def hold(arrays, after):
    count = len(arrays)
    return call(
        hold_kernel,
        [jax.ShapeDtypeStruct(x.shape, x.dtype) for x in arrays],
        2,
        arrays,
        after,
        in_specs=[ANY] * count,
        out_specs=[ANY] * count,
        aliases={k: k for k in range(count)},
    )


def exchange(message):
    return lax.all_to_all(message, "chan", 0, 0, tiled=True)


def shards(generator, hamiltonian, recoupling, channel_size, hole_first, hole_second):
    gen, ham, recouple = generator[0], hamiltonian[0], recoupling[0]
    rows = gen.shape[0]
    count = lax.axis_size("chan")
    holes = (hole_first, hole_second)
    row = lax.axis_index("row").astype(jnp.int32)
    where = jnp.stack([channel_size[0], row])
    near, far, _ = partners(row)
    far_pick = jnp.stack([jnp.where(row < 2, 0, rows), jnp.where((row == 0) | (row == 3), 0, 1), far]).astype(jnp.int32)
    near_pick = jnp.stack([jnp.where(row % 2 == 0, 0, rows), jnp.where(row < 2, 2, 3), near]).astype(jnp.int32)

    def to_near(x):
        return lax.ppermute(x, "row", [(0, 1), (1, 0), (2, 3), (3, 2)])

    def to_far(x):
        return lax.ppermute(x, "row", [(0, 3), (3, 0), (1, 2), (2, 1)])

    gen_message = encode(gen, where, count)
    gen_moved = exchange(gen_message)
    keep_low, send_low, keep_high, send_high = ladder_part(gen, ham, *holes, where, after=(gen_message,))
    got_low, got_high = to_near(send_low), to_far(send_high)
    ham_message = encode(ham, where, count, after=(send_low,))
    ham_moved = exchange(ham_message)
    gen_bar = gen_bar_of(read(gen_moved, rows, after=(ham_message,), flops=SLOW), recouple)
    (gen_bar,) = hold((gen_bar,), (got_low, got_high))
    gen_near, gen_far = to_near(gen_bar), to_far(gen_bar)
    *ham_bar, block = ham_bar_of(ham_moved, recouple, where, rows, flops=SLOW)
    *ham_bar, block = hold((*ham_bar, block), (gen_near, gen_far))
    from_far, block_far = to_far(ham_bar[0]), to_far(block)
    from_near, block_near = to_near(ham_bar[1]), to_near(block)
    ladder_own, ladder_far, ladder_near = fold(keep_low, got_low, keep_high, got_high)
    local = local_term((gen_bar, gen_near, gen_far), ham_bar, *holes, where, after=(ladder_far,))
    for_near, for_far = ready(where, gen_near, gen_far, ham_bar, *holes)
    send_near = send_product(far_pick, for_near, from_far, block_near, *holes, after=(local,))
    term_near = to_near(send_near)
    send_far = send_product(near_pick, for_far, from_near, block_far, *holes, after=(local,))
    term_far = to_far(send_far)
    sent = (send_near, send_far)
    own = (
        pair_product(0, far_pick, gen_bar, ham_bar[0], from_far, local, *holes, after=sent),
        pair_product(1, near_pick, gen_bar, ham_bar[1], from_near, local, *holes, after=sent),
    )
    message = turn(own, (term_near, term_far), halves(recouple, after=sent), count)
    back = exchange(message)
    return finish(back, ladder_own, to_far(ladder_far), to_near(ladder_near), where)[None]


def solution(mesh):
    in_specs = (
        P("chan", "row", None),
        P("chan", "row", None),
        P("chan", None, None),
        P("chan"),
        P("chan", None),
        P("chan", None),
    )
    out_specs = P("chan", "row", None)
    return jax.shard_map(shards, mesh=mesh, in_specs=in_specs, out_specs=out_specs, check_vma=False)
```

```python
import functools

import jax
import jax.numpy as jnp
from jax import lax
from jax.experimental import pallas as pl
from jax.experimental.pallas import tpu as pltpu
from jax.sharding import PartitionSpec as P

F32 = jnp.float32
BF16 = jnp.bfloat16
MIB = 1024 * 1024
LARGE = 60
LARGEST = 62
NN = ((1,), (0,))
NT = ((1,), (1,))
TILE = 256
LANES = 128
SUB = 8
FAST = 1000
SLOW = 10**12


def split(x):
    high = x.astype(BF16)
    return high, (x - high.astype(F32)).astype(BF16)


def dot3(a, b, dims):
    def one(left, right):
        return lax.dot_general(left, right, (dims, ((), ())), preferred_element_type=F32)

    return one(a[0], b[0]) + (one(a[0], b[1]) + one(a[1], b[0]))


VMEM = pl.BlockSpec(memory_space=pltpu.VMEM)
SMEM = pl.BlockSpec(memory_space=pltpu.SMEM)
ANY = pl.BlockSpec(memory_space=pl.ANY)


def call(kernel, out_shape, mib, inputs, after=(), flops=FAST, in_specs=None, out_specs=None, scratch_shapes=(), aliases=None):
    first, last = len(inputs), len(inputs) + len(after)

    def body(*refs):
        kernel(*refs[:first], *refs[last:])

    if in_specs is None:
        in_specs = [SMEM if x.ndim == 1 else VMEM for x in inputs]
    if out_specs is None:
        out_specs = [VMEM] * len(out_shape) if isinstance(out_shape, list) else VMEM
    return pl.pallas_call(
        body,
        out_shape=out_shape,
        in_specs=list(in_specs) + [ANY] * len(after),
        out_specs=out_specs,
        scratch_shapes=list(scratch_shapes),
        input_output_aliases=aliases or {},
        compiler_params=pltpu.CompilerParams(vmem_limit_bytes=mib * MIB),
        cost_estimate=pl.CostEstimate(flops=flops, bytes_accessed=4_000_000, transcendentals=0),
    )(*inputs, *after)


def message_shape(rows, order, count):
    return jax.ShapeDtypeStruct((count, 1, rows * order // count), F32)


def upper(shape):
    return lax.broadcasted_iota(jnp.int32, shape, 0) < shape[0] // 2


def swapped(x):
    middle = x.shape[0] // 2
    return jnp.concatenate([x[middle:], x[:middle]], axis=0)


def put(target, channel, at, tile):
    target[channel, :, at : at + tile.size] = tile.reshape(1, tile.size)
    return at + tile.size


def get(source, channel, at, rows):
    return source[channel, :, at : at + rows * LANES].reshape(rows, LANES)


def lane_parts(rows):
    return [(lane, min(LANES, rows - lane)) for lane in range(0, rows, LANES)]


def pack(source, target, count, width):
    parts = lane_parts(source.shape[1])

    def pair(step, _):
        base = pl.multiple_of(step * 2 * width, SUB)
        whole = ([], [])
        last = ([], [])
        for lane, size in parts:
            tile = [source[pl.ds(base + SUB * k, SUB), lane : lane + size] for k in range(5)]
            top = upper(tile[0].shape)
            turned = [swapped(tile[k]) for k in range(2, 5)]
            whole[0].append(tile[:2])
            last[0].append(tile[2])
            whole[1].append([jnp.where(top, turned[0], turned[1]), jnp.where(top, turned[1], turned[2])])
            last[1].append(turned[2])
        top = upper((SUB, LANES))
        for odd in range(2):
            channel = 2 * step + odd
            at = 0
            for tiles in whole[odd][:-1]:
                for tile in tiles:
                    at = put(target, channel, at, tile)
            at = put(target, channel, at, jnp.concatenate(whole[odd][-1], axis=1))
            first, second, tail = last[odd]
            at = put(target, channel, at, jnp.where(top, first, swapped(second)))
            put(target, channel, at, jnp.concatenate([tail[: SUB // 4], tail[SUB // 4 : SUB // 2]], axis=1))
        return 0

    lax.fori_loop(0, count // 2, pair, 0, unroll=4)


def unpack(source, target, count, width):
    parts = lane_parts(target.shape[1])
    rest = parts[-1][1]
    size = SUB * LANES

    def pair(step, _):
        base = pl.multiple_of(step * 2 * width, SUB)
        whole = ([], [])
        last = ([], [])
        for odd in range(2):
            channel = 2 * step + odd
            at = 0
            for _ in parts[:-1]:
                whole[odd].append([get(source, channel, at, SUB), get(source, channel, at + size, SUB)])
                at += 2 * size
            tail = get(source, channel, at, SUB)
            whole[odd].append([tail[:, :rest], tail[:, rest:]])
            at += size
            shared = get(source, channel, at, SUB)
            corner = get(source, channel, at + size, SUB // 4)
            corner = [corner[:, :rest], corner[:, rest:]]
            last[odd].extend([shared, swapped(shared), jnp.concatenate(corner + corner, axis=0)])
        for place, (lane, size_) in enumerate(parts):
            even, odd = whole[0][place], [swapped(tile) for tile in whole[1][place]]
            top = upper(even[0].shape)
            tiles = even + [
                jnp.where(top, last[0][place], odd[0]),
                jnp.where(top, odd[0], odd[1]),
                jnp.where(top, odd[1], swapped(last[1][place])),
            ]
            for k, tile in enumerate(tiles):
                target[pl.ds(base + SUB * k, SUB), lane : lane + size_] = tile
        return 0

    lax.fori_loop(0, count // 2, pair, 0, unroll=4)


def live(shape, where_ref, rows, start):
    row = lax.broadcasted_iota(jnp.int32, shape, 0) + where_ref[1] * rows
    column = lax.broadcasted_iota(jnp.int32, shape, 1) + start
    return (row < where_ref[0]) & (column < where_ref[0])


def encode_kernel(count, where_ref, x_hbm, out_ref, x_ref, turned, arrived):
    rows, order = x_ref.shape
    fetches = [
        pltpu.make_async_copy(x_hbm.at[:, pl.ds(start, TILE)], x_ref.at[:, pl.ds(start, TILE)], arrived.at[start // TILE])
        for start in range(0, order, TILE)
    ]
    for fetch in fetches:
        fetch.start()
    for start, fetch in zip(range(0, order, TILE), fetches):
        fetch.wait()
        block = x_ref[:, start : start + TILE]
        turned[start : start + TILE, :] = jnp.where(live(block.shape, where_ref, rows, start), block, 0.0).T
    pack(turned, out_ref, count, order // count)


def encode(x, where, count, after=()):
    rows, order = x.shape
    return call(
        functools.partial(encode_kernel, count),
        message_shape(rows, order, count),
        LARGEST,
        (where, x),
        after,
        in_specs=[SMEM, ANY],
        scratch_shapes=[
            pltpu.VMEM((rows, order), F32),
            pltpu.VMEM((order, rows), F32),
            pltpu.SemaphoreType.DMA((order // TILE,)),
        ],
    )


def read_kernel(message_ref, high, low, turned):
    order = turned.shape[0]
    count = message_ref.shape[0]
    unpack(message_ref, turned, count, order // count)
    for start in range(0, order, TILE):
        span = slice(start, start + TILE)
        high[:, span], low[:, span] = split(turned[span, :].T)


def read(message, rows, after=(), flops=FAST):
    order = message.shape[0] * message.shape[2] // rows
    return call(
        read_kernel,
        [jax.ShapeDtypeStruct((rows, order), BF16)] * 2,
        12,
        (message,),
        after,
        flops,
        scratch_shapes=[pltpu.VMEM((order, rows), F32)],
    )


def bar_product(high, low, recouple_ref, outs):
    order = recouple_ref.shape[0]
    width = order // 2
    for start in range(0, order, TILE):
        product = dot3((high[...], low[...]), split(recouple_ref[:, start : start + TILE]), NN)
        for place, out in enumerate(outs):
            begin, end = max(start, place * width), min(start + TILE, (place + 1) * width)
            if begin < end:
                out[:, begin - place * width : end - place * width] = product[:, begin - start : end - start]


def gen_bar_kernel(high, low, recouple_ref, out_ref):
    bar_product(high, low, recouple_ref, [out_ref.at[0], out_ref.at[1]])


def ham_bar_kernel(where_ref, message_ref, recouple_hbm, low_ref, high_ref, across_ref, turned, high, low, recouple_ref, arrived):
    rows, half = low_ref.shape
    order = 2 * half
    fetches = [
        pltpu.make_async_copy(
            recouple_hbm.at[:, pl.ds(start, TILE)], recouple_ref.at[:, pl.ds(start, TILE)], arrived.at[start // TILE]
        )
        for start in range(0, order, TILE)
    ]
    for fetch in fetches:
        fetch.start()
    read_kernel(message_ref, high, low, turned)
    for fetch in fetches:
        fetch.wait()
    bar_product(high, low, recouple_ref, [low_ref, high_ref])
    across = where_ref[1] ^ 2
    left = jnp.where(across < 2, low_ref[:, :rows], high_ref[:, :rows])
    right = jnp.where(across < 2, low_ref[:, rows:], high_ref[:, rows:])
    block = jnp.where(across % 2 == 0, left, right)
    across_ref[...] = jnp.concatenate([block[: rows // 2], block[rows // 2 :]], axis=1)


def gen_bar_of(moved, recoupling, after=()):
    rows, order = moved[0].shape
    return call(
        gen_bar_kernel,
        jax.ShapeDtypeStruct((2, rows, order // 2), F32),
        20,
        (*moved, recoupling),
        after,
    )


def ham_bar_of(message, recoupling, where, rows, after=(), flops=FAST):
    order = recoupling.shape[0]
    half = jax.ShapeDtypeStruct((rows, order // 2), F32)
    return call(
        ham_bar_kernel,
        [half, half, jax.ShapeDtypeStruct((rows // 2, 2 * rows), F32)],
        LARGE,
        (where, message, recoupling),
        after,
        flops,
        in_specs=[SMEM, VMEM, ANY],
        scratch_shapes=[
            pltpu.VMEM((order, rows), F32),
            pltpu.VMEM((rows, order), BF16),
            pltpu.VMEM((rows, order), BF16),
            pltpu.VMEM((order, order), F32),
            pltpu.SemaphoreType.DMA((order // TILE,)),
        ],
    )


def partners(row):
    return row ^ 1, 3 - row, row ^ 2


def ladder_kernel(where_ref, gen_ref, ham_ref, first_ref, second_ref, *refs):
    outs, (left_high, left_low, right_high, right_low) = refs[:4], refs[4:]
    rows, order = gen_ref.shape
    half = order // 2
    row = where_ref[1]
    position = lax.broadcasted_iota(jnp.int32, (1, order), 1)
    weight = jnp.where(position < where_ref[0], (first_ref[...] + second_ref[...] - 1).astype(F32), 0.0)
    mine = block_of(weight, row, rows)
    near, far, across = partners(row)
    for place, (left, right) in enumerate(((gen_ref, ham_ref), (ham_ref, gen_ref))):
        span = slice(place * rows, (place + 1) * rows)
        for block in range(order // rows):
            spot = jnp.where(block == near, 0, jnp.where(block == row, 1, jnp.where(block == far, 2, 3)))
            high, low = split(left[:, block * rows : (block + 1) * rows].T * mine)
            at = pl.ds(pl.multiple_of(spot * rows, 64), rows)
            left_high[at, span], left_low[at, span] = high, low

            @pl.when(block == near)
            def _():
                left_high[order:, span], left_low[order:, span] = high, low

        right_high[span, :], right_low[span, :] = split(right[...])
    for place, starts in enumerate(((1, 3), (0, 2))):
        columns = slice(place * half, (place + 1) * half)
        right = right_high[:, columns], right_low[:, columns]
        for kind, start in enumerate(starts):
            at = slice(start * rows, (start + 2) * rows)
            outs[2 * place + kind][...] = dot3((left_high[at, :], left_low[at, :]), right, NN).reshape(2, rows, half)


def ladder_part(gen, ham, first, second, where, after=()):
    rows, order = gen.shape
    return call(
        ladder_kernel,
        [jax.ShapeDtypeStruct((2, rows, order // 2), F32)] * 4,
        LARGE,
        (where, gen, ham, first, second),
        after,
        scratch_shapes=[pltpu.VMEM((order + rows, 2 * rows), BF16)] * 2
        + [pltpu.VMEM((2 * rows, order), BF16)] * 2,
    )


def fold_kernel(keep_low, got_low, keep_high, got_high, own_ref, far_ref, near_ref):
    half = far_ref.shape[1]
    own_ref[:, :half] = keep_low[0] + got_low[1]
    own_ref[:, half:] = keep_high[1] + got_high[0]
    far_ref[...] = keep_low[1] + got_low[0]
    near_ref[...] = keep_high[0] + got_high[1]


def fold(keep_low, got_low, keep_high, got_high):
    _, rows, half = keep_low.shape
    return call(
        fold_kernel,
        [jax.ShapeDtypeStruct((rows, 2 * half), F32)] + [jax.ShapeDtypeStruct((rows, half), F32)] * 2,
        16,
        (keep_low, got_low, keep_high, got_high),
    )


def block_of(weight, index, rows):
    picked = weight[:, :rows]
    for other in range(1, weight.shape[1] // rows):
        picked = jnp.where(index == other, weight[:, other * rows : (other + 1) * rows], picked)
    return picked


def weighted(first_ref, second_ref):
    return (first_ref[...] - second_ref[...]).astype(F32)


def local_kernel(where_ref, mine_ref, near_ref, far_ref, low_ref, high_ref, first_ref, second_ref, out_ref, *scratch):
    ham_high, ham_low, gen_high, gen_low = scratch
    rows, half = low_ref.shape
    weight = weighted(first_ref, second_ref)
    row = where_ref[1]
    near, far, across = partners(row)
    for place, ham_ref in enumerate((low_ref, high_ref)):
        span = slice(place * half, (place + 1) * half)
        ham_high[:, span], ham_low[:, span] = split(ham_ref[...] * weight[:, span])
        for gen_ref, block in ((mine_ref, row), (near_ref, near), (far_ref, far)):
            at = pl.ds(pl.multiple_of(block * rows, 64), rows)
            gen_high[at, span], gen_low[at, span] = split(gen_ref[place])
        at = pl.ds(pl.multiple_of(across * rows, 64), rows)
        gen_high[at, span] = jnp.zeros((rows, half), BF16)
        gen_low[at, span] = jnp.zeros((rows, half), BF16)
    for start in range(0, 2 * half, TILE):
        span = slice(start, start + TILE)
        out_ref[:, span] = dot3((ham_high[...], ham_low[...]), (gen_high[:, span], gen_low[:, span]), NN)


def local_term(slabs, ham_halves, first, second, where, after=()):
    rows, half = ham_halves[0].shape
    return call(
        local_kernel,
        jax.ShapeDtypeStruct((rows, 2 * half), F32),
        26,
        (where, *slabs, *ham_halves, first, second),
        after,
        scratch_shapes=[pltpu.VMEM((rows, 2 * half), BF16)] * 2 + [pltpu.VMEM((2 * half, 2 * half), BF16)] * 2,
    )


def chosen(pick_ref, gen_ref, weight):
    rows, half = gen_ref.shape[1:]
    kind = pick_ref[1]
    low, high = gen_ref[0] * weight[:, :half], gen_ref[1] * weight[:, half:]
    outer = jnp.concatenate([low[:, :rows], high[:, half - rows :]], axis=1)
    inner = jnp.concatenate([low[:, rows:], high[:, : half - rows]], axis=1)
    return jnp.where(kind == 0, outer, jnp.where(kind == 1, inner, jnp.where(kind == 2, low, high)))


def place_pair(pick_ref, own_ref, got_ref, right_high, right_low):
    rows = own_ref.shape[0]
    own_at = pl.multiple_of(pick_ref[0], 64)
    got_at = pl.multiple_of(rows - pick_ref[0], 64)
    for at, ref in ((own_at, own_ref), (got_at, got_ref)):
        right_high[pl.ds(at, rows), :], right_low[pl.ds(at, rows), :] = split(ref[...])


def pair_kernel(place, pick_ref, gen_ref, own_ref, got_ref, local_ref, first_ref, second_ref, out_ref, right_high, right_low):
    half = own_ref.shape[1]
    place_pair(pick_ref, own_ref, got_ref, right_high, right_low)
    left = split(chosen(pick_ref, gen_ref, weighted(first_ref, second_ref)))
    for start in range(0, half, TILE):
        end = min(start + TILE, half)
        local = local_ref[:, place * half + start : place * half + end]
        out_ref[:, start:end] = dot3(left, (right_high[:, start:end], right_low[:, start:end]), NN) - local


def pair_product(place, pick, slab, own, got, local, first, second, after=()):
    rows, half = own.shape
    return call(
        functools.partial(pair_kernel, place),
        jax.ShapeDtypeStruct((rows, half), F32),
        16,
        (pick, slab, own, got, local, first, second),
        after,
        scratch_shapes=[pltpu.VMEM((2 * rows, half), BF16)] * 2,
    )


def columns_of(gen_ref, index, weight):
    rows = gen_ref.shape[1]
    left = jnp.where(index < 2, gen_ref[0, :, :rows], gen_ref[1, :, :rows])
    right = jnp.where(index < 2, gen_ref[0, :, rows:], gen_ref[1, :, rows:])
    return jnp.where(index % 2 == 0, left, right) * block_of(weight, index, rows)


def ready_kernel(where_ref, near_ref, far_ref, low_ref, high_ref, first_ref, second_ref, *outs):
    rows, half = low_ref.shape
    weight = weighted(first_ref, second_ref)
    row = where_ref[1]
    near, far, _ = partners(row)
    sides = ((near_ref, far_ref, low_ref, far), (far_ref, near_ref, high_ref, near))
    for place, (gen_ref, other_ref, ham_ref, index) in enumerate(sides):
        part, left_high, left_low, right_high, right_low = outs[5 * place : 5 * place + 5]
        left = split(columns_of(gen_ref, row, weight))
        for start in range(0, half, TILE):
            span = slice(start, min(start + TILE, half))
            part[:, span] = dot3(left, split(ham_ref[:, span]), NN)
        left_high[...], left_low[...] = split(columns_of(gen_ref, index, weight))
        right_high[...], right_low[...] = split(other_ref[place])


def ready(where, gen_near, gen_far, ham_halves, first, second):
    rows, half = ham_halves[0].shape
    side = (
        [jax.ShapeDtypeStruct((rows, half), F32)]
        + [jax.ShapeDtypeStruct((rows, rows), BF16)] * 2
        + [jax.ShapeDtypeStruct((rows, half), BF16)] * 2
    )
    outs = call(
        ready_kernel,
        side * 2,
        24,
        (where, gen_near, gen_far, *ham_halves, first, second),
    )
    return outs[:5], outs[5:]


def send_kernel(pick_ref, part_ref, first_high, first_low, other_high, other_low, got_ref, block_ref, first_ref, second_ref, out_ref, *scratch):
    left_high, left_low, right_high, right_low = scratch
    rows, half = got_ref.shape
    weight = block_of(weighted(first_ref, second_ref), pick_ref[2], rows)
    block = jnp.concatenate([block_ref[:, :rows], block_ref[:, rows:]], axis=0)
    left_high[:, :rows], left_low[:, :rows] = first_high[...], first_low[...]
    left_high[:, rows:], left_low[:, rows:] = split(-block * weight)
    right_high[:rows, :], right_low[:rows, :] = split(got_ref[...])
    right_high[rows:, :], right_low[rows:, :] = other_high[...], other_low[...]
    for start in range(0, half, TILE):
        span = slice(start, min(start + TILE, half))
        product = dot3((left_high[...], left_low[...]), (right_high[:, span], right_low[:, span]), NN)
        out_ref[:, span] = part_ref[:, span] + product


def send_product(pick, prepared, got, block, first, second, after=()):
    rows, half = got.shape
    return call(
        send_kernel,
        jax.ShapeDtypeStruct((rows, half), F32),
        18,
        (pick, *prepared, got, block, first, second),
        after,
        scratch_shapes=[pltpu.VMEM((rows, 2 * rows), BF16)] * 2 + [pltpu.VMEM((2 * rows, half), BF16)] * 2,
    )


def halves_kernel(x_ref, high, low):
    for start in range(0, x_ref.shape[0], TILE):
        span = slice(start, start + TILE)
        high[span, :], low[span, :] = split(x_ref[span, :])


def halves(x, after=()):
    return call(halves_kernel, [jax.ShapeDtypeStruct(x.shape, BF16)] * 2, 16, (x,), after)


def turn_first_kernel(own_ref, got_ref, high_ref, low_ref, out_ref):
    half = own_ref.shape[1]
    left = split(own_ref[...] + got_ref[...])
    for start in range(0, high_ref.shape[0], TILE):
        span = slice(start, start + TILE)
        out_ref[:, span] = dot3(left, (high_ref[span, :half], low_ref[span, :half]), NT)


def turn_first(own, got, recouple_parts):
    rows, half = own.shape
    return call(
        turn_first_kernel,
        jax.ShapeDtypeStruct((rows, 2 * half), F32),
        20,
        (own, got, *recouple_parts),
    )


def turn_kernel(count, first_ref, own_ref, got_ref, high_ref, low_ref, out_ref, turned):
    half = own_ref.shape[1]
    left = split(own_ref[...] + got_ref[...])
    order = 2 * half
    for start in range(0, order, TILE):
        span = slice(start, start + TILE)
        product = dot3(left, (high_ref[span, half:], low_ref[span, half:]), NT)
        turned[span, :] = (first_ref[:, span] + product).T
    pack(turned, out_ref, count, order // count)


def turn(first, own, got, recouple_parts, count):
    rows, order = first.shape
    return call(
        functools.partial(turn_kernel, count),
        message_shape(rows, order, count),
        24,
        (first, own, got, *recouple_parts),
        scratch_shapes=[pltpu.VMEM((order, rows), F32)],
    )


def finish_kernel(where_ref, message_ref, own_hbm, low_hbm, high_hbm, out_ref, turned, own_ref, part_ref, arrived):
    rows, order = out_ref.shape
    half = low_hbm.shape[1]
    count = message_ref.shape[0]
    copies = [
        pltpu.make_async_copy(own_hbm, own_ref, arrived.at[0]),
        pltpu.make_async_copy(low_hbm, part_ref.at[0], arrived.at[1]),
        pltpu.make_async_copy(high_hbm, part_ref.at[1], arrived.at[2]),
    ]
    for copy in copies:
        copy.start()
    unpack(message_ref, turned, count, order // count)
    for copy in copies:
        copy.wait()
    for place in range(2):
        for start in range(0, half, LANES):
            at = place * half + start
            span = slice(at, at + LANES)
            total = own_ref[:, span] + part_ref[place, :, start : start + LANES] + turned[span, :].T
            out_ref[:, span] = jnp.where(live(total.shape, where_ref, rows, at), total, 0.0)


def finish(message, own, low, high, where):
    rows, order = own.shape
    return call(
        finish_kernel,
        jax.ShapeDtypeStruct((rows, order), F32),
        52,
        (where, message, own, low, high),
        in_specs=[SMEM, VMEM, ANY, ANY, ANY],
        scratch_shapes=[
            pltpu.VMEM((order, rows), F32),
            pltpu.VMEM((rows, order), F32),
            pltpu.VMEM((2, rows, order // 2), F32),
            pltpu.SemaphoreType.DMA((3,)),
        ],
    )


def hold_kernel(*refs):
    del refs


def hold(arrays, after):
    count = len(arrays)
    return call(
        hold_kernel,
        [jax.ShapeDtypeStruct(x.shape, x.dtype) for x in arrays],
        2,
        arrays,
        after,
        in_specs=[ANY] * count,
        out_specs=[ANY] * count,
        aliases={k: k for k in range(count)},
    )


def exchange(message):
    return lax.all_to_all(message, "chan", 0, 0, tiled=True)


def shards(generator, hamiltonian, recoupling, channel_size, hole_first, hole_second):
    gen, ham, recouple = generator[0], hamiltonian[0], recoupling[0]
    rows = gen.shape[0]
    count = lax.axis_size("chan")
    holes = (hole_first, hole_second)
    row = lax.axis_index("row").astype(jnp.int32)
    where = jnp.stack([channel_size[0], row])
    near, far, _ = partners(row)
    far_pick = jnp.stack([jnp.where(row < 2, 0, rows), jnp.where((row == 0) | (row == 3), 0, 1), far]).astype(jnp.int32)
    near_pick = jnp.stack([jnp.where(row % 2 == 0, 0, rows), jnp.where(row < 2, 2, 3), near]).astype(jnp.int32)

    def to_near(x):
        return lax.ppermute(x, "row", [(0, 1), (1, 0), (2, 3), (3, 2)])

    def to_far(x):
        return lax.ppermute(x, "row", [(0, 3), (3, 0), (1, 2), (2, 1)])

    gen_message = encode(gen, where, count)
    gen_moved = exchange(gen_message)
    keep_low, send_low, keep_high, send_high = ladder_part(gen, ham, *holes, where, after=(gen_message,))
    got_low, got_high = to_near(send_low), to_far(send_high)
    ham_message = encode(ham, where, count, after=(send_low,))
    ham_moved = exchange(ham_message)
    gen_bar = gen_bar_of(read(gen_moved, rows, after=(ham_message,), flops=SLOW), recouple)
    (gen_bar,) = hold((gen_bar,), (got_low, got_high))
    gen_near, gen_far = to_near(gen_bar), to_far(gen_bar)
    *ham_bar, block = ham_bar_of(ham_moved, recouple, where, rows, flops=SLOW)
    *ham_bar, block = hold((*ham_bar, block), (gen_near, gen_far))
    from_far, block_far = to_far(ham_bar[0]), to_far(block)
    from_near, block_near = to_near(ham_bar[1]), to_near(block)
    ladder_own, ladder_far, ladder_near = fold(keep_low, got_low, keep_high, got_high)
    local = local_term((gen_bar, gen_near, gen_far), ham_bar, *holes, where, after=(ladder_far,))
    for_near, for_far = ready(where, gen_near, gen_far, ham_bar, *holes)
    send_near = send_product(far_pick, for_near, from_far, block_near, *holes, after=(local,))
    term_near = to_near(send_near)
    send_far = send_product(near_pick, for_far, from_near, block_far, *holes, after=(local,))
    term_far = to_far(send_far)
    sent = (send_near, send_far)
    own = (
        pair_product(0, far_pick, gen_bar, ham_bar[0], from_far, local, *holes, after=sent),
        pair_product(1, near_pick, gen_bar, ham_bar[1], from_near, local, *holes, after=sent),
    )
    recouple_parts = halves(recouple, after=sent)
    first_half = turn_first(own[0], term_near, recouple_parts)
    message = turn(first_half, own[1], term_far, recouple_parts, count)
    back = exchange(message)
    return finish(back, ladder_own, to_far(ladder_far), to_near(ladder_near), where)[None]


def solution(mesh):
    in_specs = (
        P("chan", "row", None),
        P("chan", "row", None),
        P("chan", None, None),
        P("chan"),
        P("chan", None),
        P("chan", None),
    )
    out_specs = P("chan", "row", None)
    return jax.shard_map(shards, mesh=mesh, in_specs=in_specs, out_specs=out_specs, check_vma=False)
```

```python
import functools

import jax
import jax.numpy as jnp
from jax import lax
from jax.experimental import pallas as pl
from jax.experimental.pallas import tpu as pltpu
from jax.sharding import PartitionSpec as P

F32 = jnp.float32
BF16 = jnp.bfloat16
MIB = 1024 * 1024
LARGE = 60
LARGEST = 62
NN = ((1,), (0,))
NT = ((1,), (1,))
TILE = 256
LANES = 128
SUB = 8
FAST = 1000
SLOW = 10**12


def split(x):
    high = x.astype(BF16)
    return high, (x - high.astype(F32)).astype(BF16)


def dot3(a, b, dims):
    def one(left, right):
        return lax.dot_general(left, right, (dims, ((), ())), preferred_element_type=F32)

    return one(a[0], b[0]) + (one(a[0], b[1]) + one(a[1], b[0]))


VMEM = pl.BlockSpec(memory_space=pltpu.VMEM)
SMEM = pl.BlockSpec(memory_space=pltpu.SMEM)
ANY = pl.BlockSpec(memory_space=pl.ANY)


def call(kernel, out_shape, mib, inputs, after=(), flops=FAST, in_specs=None, out_specs=None, scratch_shapes=(), aliases=None):
    first, last = len(inputs), len(inputs) + len(after)

    def body(*refs):
        kernel(*refs[:first], *refs[last:])

    if in_specs is None:
        in_specs = [SMEM if x.ndim == 1 else VMEM for x in inputs]
    if out_specs is None:
        out_specs = [VMEM] * len(out_shape) if isinstance(out_shape, list) else VMEM
    return pl.pallas_call(
        body,
        out_shape=out_shape,
        in_specs=list(in_specs) + [ANY] * len(after),
        out_specs=out_specs,
        scratch_shapes=list(scratch_shapes),
        input_output_aliases=aliases or {},
        compiler_params=pltpu.CompilerParams(vmem_limit_bytes=mib * MIB),
        cost_estimate=pl.CostEstimate(flops=flops, bytes_accessed=4_000_000, transcendentals=0),
    )(*inputs, *after)


def message_shape(rows, order, count):
    return jax.ShapeDtypeStruct((count, 1, rows * order // count), F32)


def upper(shape):
    return lax.broadcasted_iota(jnp.int32, shape, 0) < shape[0] // 2


def swapped(x):
    middle = x.shape[0] // 2
    return jnp.concatenate([x[middle:], x[:middle]], axis=0)


def put(target, channel, at, tile):
    target[channel, :, at : at + tile.size] = tile.reshape(1, tile.size)
    return at + tile.size


def get(source, channel, at, rows):
    return source[channel, :, at : at + rows * LANES].reshape(rows, LANES)


def lane_parts(rows):
    return [(lane, min(LANES, rows - lane)) for lane in range(0, rows, LANES)]


def pack(source, target, count, width):
    parts = lane_parts(source.shape[1])

    def pair(step, _):
        base = pl.multiple_of(step * 2 * width, SUB)
        whole = ([], [])
        last = ([], [])
        for lane, size in parts:
            tile = [source[pl.ds(base + SUB * k, SUB), lane : lane + size] for k in range(5)]
            top = upper(tile[0].shape)
            turned = [swapped(tile[k]) for k in range(2, 5)]
            whole[0].append(tile[:2])
            last[0].append(tile[2])
            whole[1].append([jnp.where(top, turned[0], turned[1]), jnp.where(top, turned[1], turned[2])])
            last[1].append(turned[2])
        top = upper((SUB, LANES))
        for odd in range(2):
            channel = 2 * step + odd
            at = 0
            for tiles in whole[odd][:-1]:
                for tile in tiles:
                    at = put(target, channel, at, tile)
            at = put(target, channel, at, jnp.concatenate(whole[odd][-1], axis=1))
            first, second, tail = last[odd]
            at = put(target, channel, at, jnp.where(top, first, swapped(second)))
            put(target, channel, at, jnp.concatenate([tail[: SUB // 4], tail[SUB // 4 : SUB // 2]], axis=1))
        return 0

    lax.fori_loop(0, count // 2, pair, 0, unroll=4)


def unpack(source, target, count, width):
    parts = lane_parts(target.shape[1])
    rest = parts[-1][1]
    size = SUB * LANES

    def pair(step, _):
        base = pl.multiple_of(step * 2 * width, SUB)
        whole = ([], [])
        last = ([], [])
        for odd in range(2):
            channel = 2 * step + odd
            at = 0
            for _ in parts[:-1]:
                whole[odd].append([get(source, channel, at, SUB), get(source, channel, at + size, SUB)])
                at += 2 * size
            tail = get(source, channel, at, SUB)
            whole[odd].append([tail[:, :rest], tail[:, rest:]])
            at += size
            shared = get(source, channel, at, SUB)
            corner = get(source, channel, at + size, SUB // 4)
            corner = [corner[:, :rest], corner[:, rest:]]
            last[odd].extend([shared, swapped(shared), jnp.concatenate(corner + corner, axis=0)])
        for place, (lane, size_) in enumerate(parts):
            even, odd = whole[0][place], [swapped(tile) for tile in whole[1][place]]
            top = upper(even[0].shape)
            tiles = even + [
                jnp.where(top, last[0][place], odd[0]),
                jnp.where(top, odd[0], odd[1]),
                jnp.where(top, odd[1], swapped(last[1][place])),
            ]
            for k, tile in enumerate(tiles):
                target[pl.ds(base + SUB * k, SUB), lane : lane + size_] = tile
        return 0

    lax.fori_loop(0, count // 2, pair, 0, unroll=4)


def live(shape, where_ref, rows, start):
    row = lax.broadcasted_iota(jnp.int32, shape, 0) + where_ref[1] * rows
    column = lax.broadcasted_iota(jnp.int32, shape, 1) + start
    return (row < where_ref[0]) & (column < where_ref[0])


def encode_kernel(count, where_ref, x_hbm, out_ref, x_ref, turned, arrived):
    rows, order = x_ref.shape
    fetches = [
        pltpu.make_async_copy(x_hbm.at[:, pl.ds(start, TILE)], x_ref.at[:, pl.ds(start, TILE)], arrived.at[start // TILE])
        for start in range(0, order, TILE)
    ]
    for fetch in fetches:
        fetch.start()
    for start, fetch in zip(range(0, order, TILE), fetches):
        fetch.wait()
        block = x_ref[:, start : start + TILE]
        turned[start : start + TILE, :] = jnp.where(live(block.shape, where_ref, rows, start), block, 0.0).T
    pack(turned, out_ref, count, order // count)


def encode(x, where, count, after=()):
    rows, order = x.shape
    return call(
        functools.partial(encode_kernel, count),
        message_shape(rows, order, count),
        LARGEST,
        (where, x),
        after,
        in_specs=[SMEM, ANY],
        scratch_shapes=[
            pltpu.VMEM((rows, order), F32),
            pltpu.VMEM((order, rows), F32),
            pltpu.SemaphoreType.DMA((order // TILE,)),
        ],
    )


def read_kernel(message_ref, high, low, turned):
    order = turned.shape[0]
    count = message_ref.shape[0]
    unpack(message_ref, turned, count, order // count)
    for start in range(0, order, TILE):
        span = slice(start, start + TILE)
        high[:, span], low[:, span] = split(turned[span, :].T)


def read(message, rows, after=(), flops=FAST):
    order = message.shape[0] * message.shape[2] // rows
    return call(
        read_kernel,
        [jax.ShapeDtypeStruct((rows, order), BF16)] * 2,
        12,
        (message,),
        after,
        flops,
        scratch_shapes=[pltpu.VMEM((order, rows), F32)],
    )


def bar_product(high, low, recouple_ref, outs):
    order = recouple_ref.shape[0]
    width = order // 2
    for start in range(0, order, TILE):
        product = dot3((high[...], low[...]), split(recouple_ref[:, start : start + TILE]), NN)
        for place, out in enumerate(outs):
            begin, end = max(start, place * width), min(start + TILE, (place + 1) * width)
            if begin < end:
                out[:, begin - place * width : end - place * width] = product[:, begin - start : end - start]


def gen_bar_kernel(high, low, recouple_ref, out_ref):
    bar_product(high, low, recouple_ref, [out_ref.at[0], out_ref.at[1]])


def ham_bar_kernel(where_ref, message_ref, recouple_hbm, low_ref, high_ref, turned, high, low, recouple_ref, arrived):
    order, rows = turned.shape
    fetches = [
        pltpu.make_async_copy(
            recouple_hbm.at[:, pl.ds(start, TILE)], recouple_ref.at[:, pl.ds(start, TILE)], arrived.at[start // TILE]
        )
        for start in range(0, order, TILE)
    ]
    for fetch in fetches:
        fetch.start()
    read_kernel(message_ref, high, low, turned)
    for fetch in fetches:
        fetch.wait()
    bar_product(high, low, recouple_ref, [low_ref.at[pl.ds(0, rows)], high_ref.at[pl.ds(0, rows)]])
    across = where_ref[1] ^ 2
    left = jnp.where(across < 2, low_ref[:rows, :rows], high_ref[:rows, :rows])
    right = jnp.where(across < 2, low_ref[:rows, rows:], high_ref[:rows, rows:])
    block = jnp.where(across % 2 == 0, left, right)
    beside = jnp.concatenate([block[: rows // 2], block[rows // 2 :]], axis=1)
    low_ref[rows:, :] = beside
    high_ref[rows:, :] = beside


def gen_bar_of(moved, recoupling, after=()):
    rows, order = moved[0].shape
    return call(
        gen_bar_kernel,
        jax.ShapeDtypeStruct((2, rows, order // 2), F32),
        20,
        (*moved, recoupling),
        after,
    )


def ham_bar_of(message, recoupling, where, rows, after=(), flops=FAST):
    order = recoupling.shape[0]
    half = jax.ShapeDtypeStruct((rows + rows // 2, order // 2), F32)
    return call(
        ham_bar_kernel,
        [half, half],
        LARGE,
        (where, message, recoupling),
        after,
        flops,
        in_specs=[SMEM, VMEM, ANY],
        scratch_shapes=[
            pltpu.VMEM((order, rows), F32),
            pltpu.VMEM((rows, order), BF16),
            pltpu.VMEM((rows, order), BF16),
            pltpu.VMEM((order, order), F32),
            pltpu.SemaphoreType.DMA((order // TILE,)),
        ],
    )


def partners(row):
    return row ^ 1, 3 - row, row ^ 2


def ladder_kernel(where_ref, gen_ref, ham_ref, first_ref, second_ref, *refs):
    outs, (left_high, left_low, right_high, right_low) = refs[:4], refs[4:]
    rows, order = gen_ref.shape
    half = order // 2
    row = where_ref[1]
    position = lax.broadcasted_iota(jnp.int32, (1, order), 1)
    weight = jnp.where(position < where_ref[0], (first_ref[...] + second_ref[...] - 1).astype(F32), 0.0)
    mine = block_of(weight, row, rows)
    near, far, across = partners(row)
    for place, (left, right) in enumerate(((gen_ref, ham_ref), (ham_ref, gen_ref))):
        span = slice(place * rows, (place + 1) * rows)
        for block in range(order // rows):
            spot = jnp.where(block == near, 0, jnp.where(block == row, 1, jnp.where(block == far, 2, 3)))
            high, low = split(left[:, block * rows : (block + 1) * rows].T * mine)
            at = pl.ds(pl.multiple_of(spot * rows, 64), rows)
            left_high[at, span], left_low[at, span] = high, low

            @pl.when(block == near)
            def _():
                left_high[order:, span], left_low[order:, span] = high, low

        right_high[span, :], right_low[span, :] = split(right[...])
    for place, starts in enumerate(((1, 3), (0, 2))):
        columns = slice(place * half, (place + 1) * half)
        right = right_high[:, columns], right_low[:, columns]
        for kind, start in enumerate(starts):
            at = slice(start * rows, (start + 2) * rows)
            outs[2 * place + kind][...] = dot3((left_high[at, :], left_low[at, :]), right, NN).reshape(2, rows, half)


def ladder_part(gen, ham, first, second, where, after=()):
    rows, order = gen.shape
    return call(
        ladder_kernel,
        [jax.ShapeDtypeStruct((2, rows, order // 2), F32)] * 4,
        LARGE,
        (where, gen, ham, first, second),
        after,
        scratch_shapes=[pltpu.VMEM((order + rows, 2 * rows), BF16)] * 2
        + [pltpu.VMEM((2 * rows, order), BF16)] * 2,
    )


def fold_kernel(keep_low, got_low, keep_high, got_high, own_ref, far_ref, near_ref):
    half = far_ref.shape[1]
    own_ref[:, :half] = keep_low[0] + got_low[1]
    own_ref[:, half:] = keep_high[1] + got_high[0]
    far_ref[...] = keep_low[1] + got_low[0]
    near_ref[...] = keep_high[0] + got_high[1]


def fold(keep_low, got_low, keep_high, got_high):
    _, rows, half = keep_low.shape
    return call(
        fold_kernel,
        [jax.ShapeDtypeStruct((rows, 2 * half), F32)] + [jax.ShapeDtypeStruct((rows, half), F32)] * 2,
        16,
        (keep_low, got_low, keep_high, got_high),
    )


def block_of(weight, index, rows):
    picked = weight[:, :rows]
    for other in range(1, weight.shape[1] // rows):
        picked = jnp.where(index == other, weight[:, other * rows : (other + 1) * rows], picked)
    return picked


def weighted(first_ref, second_ref):
    return (first_ref[...] - second_ref[...]).astype(F32)


def local_kernel(where_ref, mine_ref, near_ref, far_ref, low_ref, high_ref, first_ref, second_ref, out_ref, *scratch):
    ham_high, ham_low, gen_high, gen_low = scratch
    _, rows, half = mine_ref.shape
    weight = weighted(first_ref, second_ref)
    row = where_ref[1]
    near, far, across = partners(row)
    for place, ham_ref in enumerate((low_ref, high_ref)):
        span = slice(place * half, (place + 1) * half)
        ham_high[:, span], ham_low[:, span] = split(ham_ref[:rows, :] * weight[:, span])
        for gen_ref, block in ((mine_ref, row), (near_ref, near), (far_ref, far)):
            at = pl.ds(pl.multiple_of(block * rows, 64), rows)
            gen_high[at, span], gen_low[at, span] = split(gen_ref[place])
        at = pl.ds(pl.multiple_of(across * rows, 64), rows)
        gen_high[at, span] = jnp.zeros((rows, half), BF16)
        gen_low[at, span] = jnp.zeros((rows, half), BF16)
    for start in range(0, 2 * half, TILE):
        span = slice(start, start + TILE)
        out_ref[:, span] = dot3((ham_high[...], ham_low[...]), (gen_high[:, span], gen_low[:, span]), NN)


def local_term(slabs, ham_halves, first, second, where, after=()):
    _, rows, half = slabs[0].shape
    return call(
        local_kernel,
        jax.ShapeDtypeStruct((rows, 2 * half), F32),
        26,
        (where, *slabs, *ham_halves, first, second),
        after,
        scratch_shapes=[pltpu.VMEM((rows, 2 * half), BF16)] * 2 + [pltpu.VMEM((2 * half, 2 * half), BF16)] * 2,
    )


def chosen(pick_ref, gen_ref, weight):
    rows, half = gen_ref.shape[1:]
    kind = pick_ref[1]
    low, high = gen_ref[0] * weight[:, :half], gen_ref[1] * weight[:, half:]
    outer = jnp.concatenate([low[:, :rows], high[:, half - rows :]], axis=1)
    inner = jnp.concatenate([low[:, rows:], high[:, : half - rows]], axis=1)
    return jnp.where(kind == 0, outer, jnp.where(kind == 1, inner, jnp.where(kind == 2, low, high)))


def place_pair(pick_ref, own_ref, got_ref, right_high, right_low):
    rows = right_high.shape[0] // 2
    own_at = pl.multiple_of(pick_ref[0], 64)
    got_at = pl.multiple_of(rows - pick_ref[0], 64)
    for at, ref in ((own_at, own_ref), (got_at, got_ref)):
        right_high[pl.ds(at, rows), :], right_low[pl.ds(at, rows), :] = split(ref[:rows, :])


def pair_kernel(place, pick_ref, gen_ref, own_ref, got_ref, local_ref, first_ref, second_ref, out_ref, right_high, right_low):
    half = own_ref.shape[1]
    place_pair(pick_ref, own_ref, got_ref, right_high, right_low)
    left = split(chosen(pick_ref, gen_ref, weighted(first_ref, second_ref)))
    for start in range(0, half, TILE):
        end = min(start + TILE, half)
        local = local_ref[:, place * half + start : place * half + end]
        out_ref[:, start:end] = dot3(left, (right_high[:, start:end], right_low[:, start:end]), NN) - local


def pair_product(place, pick, slab, own, got, local, first, second, after=()):
    _, rows, half = slab.shape
    return call(
        functools.partial(pair_kernel, place),
        jax.ShapeDtypeStruct((rows, half), F32),
        16,
        (pick, slab, own, got, local, first, second),
        after,
        scratch_shapes=[pltpu.VMEM((2 * rows, half), BF16)] * 2,
    )


def columns_of(gen_ref, index, weight):
    rows = gen_ref.shape[1]
    left = jnp.where(index < 2, gen_ref[0, :, :rows], gen_ref[1, :, :rows])
    right = jnp.where(index < 2, gen_ref[0, :, rows:], gen_ref[1, :, rows:])
    return jnp.where(index % 2 == 0, left, right) * block_of(weight, index, rows)


def ready_kernel(where_ref, near_ref, far_ref, low_ref, high_ref, first_ref, second_ref, *outs):
    _, rows, half = near_ref.shape
    weight = weighted(first_ref, second_ref)
    row = where_ref[1]
    near, far, _ = partners(row)
    sides = ((near_ref, far_ref, low_ref, far), (far_ref, near_ref, high_ref, near))
    for place, (gen_ref, other_ref, ham_ref, index) in enumerate(sides):
        part, left_high, left_low, right_high, right_low = outs[5 * place : 5 * place + 5]
        left = split(columns_of(gen_ref, row, weight))
        for start in range(0, half, TILE):
            span = slice(start, min(start + TILE, half))
            part[:, span] = dot3(left, split(ham_ref[:rows, span]), NN)
        left_high[...], left_low[...] = split(columns_of(gen_ref, index, weight))
        right_high[...], right_low[...] = split(other_ref[place])


def ready(where, gen_near, gen_far, ham_halves, first, second):
    _, rows, half = gen_near.shape
    side = (
        [jax.ShapeDtypeStruct((rows, half), F32)]
        + [jax.ShapeDtypeStruct((rows, rows), BF16)] * 2
        + [jax.ShapeDtypeStruct((rows, half), BF16)] * 2
    )
    outs = call(
        ready_kernel,
        side * 2,
        24,
        (where, gen_near, gen_far, *ham_halves, first, second),
    )
    return outs[:5], outs[5:]


def send_kernel(pick_ref, part_ref, first_high, first_low, other_high, other_low, got_ref, block_ref, first_ref, second_ref, out_ref, *scratch):
    left_high, left_low, right_high, right_low = scratch
    rows, half = out_ref.shape
    weight = block_of(weighted(first_ref, second_ref), pick_ref[2], rows)
    block = jnp.concatenate([block_ref[rows:, :rows], block_ref[rows:, rows:]], axis=0)
    left_high[:, :rows], left_low[:, :rows] = first_high[...], first_low[...]
    left_high[:, rows:], left_low[:, rows:] = split(-block * weight)
    right_high[:rows, :], right_low[:rows, :] = split(got_ref[:rows, :])
    right_high[rows:, :], right_low[rows:, :] = other_high[...], other_low[...]
    for start in range(0, half, TILE):
        span = slice(start, min(start + TILE, half))
        product = dot3((left_high[...], left_low[...]), (right_high[:, span], right_low[:, span]), NN)
        out_ref[:, span] = part_ref[:, span] + product


def send_product(pick, prepared, got, block, first, second, after=()):
    rows, half = prepared[0].shape
    return call(
        send_kernel,
        jax.ShapeDtypeStruct((rows, half), F32),
        18,
        (pick, *prepared, got, block, first, second),
        after,
        scratch_shapes=[pltpu.VMEM((rows, 2 * rows), BF16)] * 2 + [pltpu.VMEM((2 * rows, half), BF16)] * 2,
    )


def halves_kernel(x_ref, high, low):
    for start in range(0, x_ref.shape[0], TILE):
        span = slice(start, start + TILE)
        high[span, :], low[span, :] = split(x_ref[span, :])


def halves(x, after=()):
    return call(halves_kernel, [jax.ShapeDtypeStruct(x.shape, BF16)] * 2, 16, (x,), after)


def turn_first_kernel(own_ref, got_ref, high_ref, low_ref, out_ref):
    half = own_ref.shape[1]
    left = split(own_ref[...] + got_ref[...])
    for start in range(0, high_ref.shape[0], TILE):
        span = slice(start, start + TILE)
        out_ref[:, span] = dot3(left, (high_ref[span, :half], low_ref[span, :half]), NT)


def turn_first(own, got, recouple_parts):
    rows, half = own.shape
    return call(
        turn_first_kernel,
        jax.ShapeDtypeStruct((rows, 2 * half), F32),
        20,
        (own, got, *recouple_parts),
    )


def turn_kernel(count, first_ref, own_ref, got_ref, high_ref, low_ref, out_ref, turned):
    half = own_ref.shape[1]
    left = split(own_ref[...] + got_ref[...])
    order = 2 * half
    for start in range(0, order, TILE):
        span = slice(start, start + TILE)
        product = dot3(left, (high_ref[span, half:], low_ref[span, half:]), NT)
        turned[span, :] = (first_ref[:, span] + product).T
    pack(turned, out_ref, count, order // count)


def turn(first, own, got, recouple_parts, count):
    rows, order = first.shape
    return call(
        functools.partial(turn_kernel, count),
        message_shape(rows, order, count),
        24,
        (first, own, got, *recouple_parts),
        scratch_shapes=[pltpu.VMEM((order, rows), F32)],
    )


def finish_kernel(where_ref, message_ref, own_hbm, low_hbm, high_hbm, out_ref, turned, own_ref, part_ref, arrived):
    rows, order = out_ref.shape
    half = low_hbm.shape[1]
    count = message_ref.shape[0]
    copies = [
        pltpu.make_async_copy(own_hbm, own_ref, arrived.at[0]),
        pltpu.make_async_copy(low_hbm, part_ref.at[0], arrived.at[1]),
        pltpu.make_async_copy(high_hbm, part_ref.at[1], arrived.at[2]),
    ]
    for copy in copies:
        copy.start()
    unpack(message_ref, turned, count, order // count)
    for copy in copies:
        copy.wait()
    for place in range(2):
        for start in range(0, half, LANES):
            at = place * half + start
            span = slice(at, at + LANES)
            total = own_ref[:, span] + part_ref[place, :, start : start + LANES] + turned[span, :].T
            out_ref[:, span] = jnp.where(live(total.shape, where_ref, rows, at), total, 0.0)


def finish(message, own, low, high, where):
    rows, order = own.shape
    return call(
        finish_kernel,
        jax.ShapeDtypeStruct((rows, order), F32),
        52,
        (where, message, own, low, high),
        in_specs=[SMEM, VMEM, ANY, ANY, ANY],
        scratch_shapes=[
            pltpu.VMEM((order, rows), F32),
            pltpu.VMEM((rows, order), F32),
            pltpu.VMEM((2, rows, order // 2), F32),
            pltpu.SemaphoreType.DMA((3,)),
        ],
    )


def hold_kernel(*refs):
    del refs


def hold(arrays, after):
    count = len(arrays)
    return call(
        hold_kernel,
        [jax.ShapeDtypeStruct(x.shape, x.dtype) for x in arrays],
        2,
        arrays,
        after,
        in_specs=[ANY] * count,
        out_specs=[ANY] * count,
        aliases={k: k for k in range(count)},
    )


def exchange(message):
    return lax.all_to_all(message, "chan", 0, 0, tiled=True)


def shards(generator, hamiltonian, recoupling, channel_size, hole_first, hole_second):
    gen, ham, recouple = generator[0], hamiltonian[0], recoupling[0]
    rows = gen.shape[0]
    count = lax.axis_size("chan")
    holes = (hole_first, hole_second)
    row = lax.axis_index("row").astype(jnp.int32)
    where = jnp.stack([channel_size[0], row])
    near, far, _ = partners(row)
    far_pick = jnp.stack([jnp.where(row < 2, 0, rows), jnp.where((row == 0) | (row == 3), 0, 1), far]).astype(jnp.int32)
    near_pick = jnp.stack([jnp.where(row % 2 == 0, 0, rows), jnp.where(row < 2, 2, 3), near]).astype(jnp.int32)

    def to_near(x):
        return lax.ppermute(x, "row", [(0, 1), (1, 0), (2, 3), (3, 2)])

    def to_far(x):
        return lax.ppermute(x, "row", [(0, 3), (3, 0), (1, 2), (2, 1)])

    gen_message = encode(gen, where, count)
    gen_moved = exchange(gen_message)
    keep_low, send_low, keep_high, send_high = ladder_part(gen, ham, *holes, where, after=(gen_message,))
    got_low, got_high = to_near(send_low), to_far(send_high)
    ham_message = encode(ham, where, count, after=(send_low,))
    ham_moved = exchange(ham_message)
    gen_bar = gen_bar_of(read(gen_moved, rows, after=(ham_message,), flops=SLOW), recouple)
    (gen_bar,) = hold((gen_bar,), (got_low, got_high))
    gen_near, gen_far = to_near(gen_bar), to_far(gen_bar)
    ham_bar = ham_bar_of(ham_moved, recouple, where, rows, flops=SLOW)
    ham_bar = hold(ham_bar, (gen_near, gen_far))
    from_far, from_near = to_far(ham_bar[0]), to_near(ham_bar[1])
    ladder_own, ladder_far, ladder_near = fold(keep_low, got_low, keep_high, got_high)
    local = local_term((gen_bar, gen_near, gen_far), ham_bar, *holes, where, after=(ladder_far,))
    for_near, for_far = ready(where, gen_near, gen_far, ham_bar, *holes)
    send_near = send_product(far_pick, for_near, from_far, from_near, *holes, after=(local,))
    term_near = to_near(send_near)
    send_far = send_product(near_pick, for_far, from_near, from_far, *holes, after=(local,))
    term_far = to_far(send_far)
    sent = (send_near, send_far)
    own = (
        pair_product(0, far_pick, gen_bar, ham_bar[0], from_far, local, *holes, after=sent),
        pair_product(1, near_pick, gen_bar, ham_bar[1], from_near, local, *holes, after=sent),
    )
    recouple_parts = halves(recouple, after=sent)
    first_half = turn_first(own[0], term_near, recouple_parts)
    message = turn(first_half, own[1], term_far, recouple_parts, count)
    back = exchange(message)
    return finish(back, ladder_own, to_far(ladder_far), to_near(ladder_near), where)[None]


def solution(mesh):
    in_specs = (
        P("chan", "row", None),
        P("chan", "row", None),
        P("chan", None, None),
        P("chan"),
        P("chan", None),
        P("chan", None),
    )
    out_specs = P("chan", "row", None)
    return jax.shard_map(shards, mesh=mesh, in_specs=in_specs, out_specs=out_specs, check_vma=False)
```

```python
import functools

import jax
import jax.numpy as jnp
from jax import lax
from jax.experimental import pallas as pl
from jax.experimental.pallas import tpu as pltpu
from jax.sharding import PartitionSpec as P

F32 = jnp.float32
BF16 = jnp.bfloat16
MIB = 1024 * 1024
LARGE = 60
LARGEST = 62
NN = ((1,), (0,))
NT = ((1,), (1,))
TILE = 256
LANES = 128
SUB = 8
FAST = 1000
SLOW = 10**12


def split(x):
    high = x.astype(BF16)
    return high, (x - high.astype(F32)).astype(BF16)


def dot3(a, b, dims):
    def one(left, right):
        return lax.dot_general(left, right, (dims, ((), ())), preferred_element_type=F32)

    return one(a[0], b[0]) + (one(a[0], b[1]) + one(a[1], b[0]))


VMEM = pl.BlockSpec(memory_space=pltpu.VMEM)
SMEM = pl.BlockSpec(memory_space=pltpu.SMEM)
ANY = pl.BlockSpec(memory_space=pl.ANY)


def call(kernel, out_shape, mib, inputs, after=(), flops=FAST, in_specs=None, out_specs=None, scratch_shapes=(), aliases=None):
    first, last = len(inputs), len(inputs) + len(after)

    def body(*refs):
        kernel(*refs[:first], *refs[last:])

    if in_specs is None:
        in_specs = [SMEM if x.ndim == 1 else VMEM for x in inputs]
    if out_specs is None:
        out_specs = [VMEM] * len(out_shape) if isinstance(out_shape, list) else VMEM
    return pl.pallas_call(
        body,
        out_shape=out_shape,
        in_specs=list(in_specs) + [ANY] * len(after),
        out_specs=out_specs,
        scratch_shapes=list(scratch_shapes),
        input_output_aliases=aliases or {},
        compiler_params=pltpu.CompilerParams(vmem_limit_bytes=mib * MIB),
        cost_estimate=pl.CostEstimate(flops=flops, bytes_accessed=4_000_000, transcendentals=0),
    )(*inputs, *after)


def message_shape(rows, order, count):
    return jax.ShapeDtypeStruct((count, 1, rows * order // count), F32)


def upper(shape):
    return lax.broadcasted_iota(jnp.int32, shape, 0) < shape[0] // 2


def swapped(x):
    middle = x.shape[0] // 2
    return jnp.concatenate([x[middle:], x[:middle]], axis=0)


def put(target, channel, at, tile):
    target[channel, :, at : at + tile.size] = tile.reshape(1, tile.size)
    return at + tile.size


def get(source, channel, at, rows):
    return source[channel, :, at : at + rows * LANES].reshape(rows, LANES)


def lane_parts(rows):
    return [(lane, min(LANES, rows - lane)) for lane in range(0, rows, LANES)]


def pack(source, target, count, width):
    parts = lane_parts(source.shape[1])

    def pair(step, _):
        base = pl.multiple_of(step * 2 * width, SUB)
        whole = ([], [])
        last = ([], [])
        for lane, size in parts:
            tile = [source[pl.ds(base + SUB * k, SUB), lane : lane + size] for k in range(5)]
            top = upper(tile[0].shape)
            turned = [swapped(tile[k]) for k in range(2, 5)]
            whole[0].append(tile[:2])
            last[0].append(tile[2])
            whole[1].append([jnp.where(top, turned[0], turned[1]), jnp.where(top, turned[1], turned[2])])
            last[1].append(turned[2])
        top = upper((SUB, LANES))
        for odd in range(2):
            channel = 2 * step + odd
            at = 0
            for tiles in whole[odd][:-1]:
                for tile in tiles:
                    at = put(target, channel, at, tile)
            at = put(target, channel, at, jnp.concatenate(whole[odd][-1], axis=1))
            first, second, tail = last[odd]
            at = put(target, channel, at, jnp.where(top, first, swapped(second)))
            put(target, channel, at, jnp.concatenate([tail[: SUB // 4], tail[SUB // 4 : SUB // 2]], axis=1))
        return 0

    lax.fori_loop(0, count // 2, pair, 0, unroll=4)


def unpack(source, target, count, width):
    parts = lane_parts(target.shape[1])
    rest = parts[-1][1]
    size = SUB * LANES

    def pair(step, _):
        base = pl.multiple_of(step * 2 * width, SUB)
        whole = ([], [])
        last = ([], [])
        for odd in range(2):
            channel = 2 * step + odd
            at = 0
            for _ in parts[:-1]:
                whole[odd].append([get(source, channel, at, SUB), get(source, channel, at + size, SUB)])
                at += 2 * size
            tail = get(source, channel, at, SUB)
            whole[odd].append([tail[:, :rest], tail[:, rest:]])
            at += size
            shared = get(source, channel, at, SUB)
            corner = get(source, channel, at + size, SUB // 4)
            corner = [corner[:, :rest], corner[:, rest:]]
            last[odd].extend([shared, swapped(shared), jnp.concatenate(corner + corner, axis=0)])
        for place, (lane, size_) in enumerate(parts):
            even, odd = whole[0][place], [swapped(tile) for tile in whole[1][place]]
            top = upper(even[0].shape)
            tiles = even + [
                jnp.where(top, last[0][place], odd[0]),
                jnp.where(top, odd[0], odd[1]),
                jnp.where(top, odd[1], swapped(last[1][place])),
            ]
            for k, tile in enumerate(tiles):
                target[pl.ds(base + SUB * k, SUB), lane : lane + size_] = tile
        return 0

    lax.fori_loop(0, count // 2, pair, 0, unroll=4)


def live(shape, where_ref, rows, start):
    row = lax.broadcasted_iota(jnp.int32, shape, 0) + where_ref[1] * rows
    column = lax.broadcasted_iota(jnp.int32, shape, 1) + start
    return (row < where_ref[0]) & (column < where_ref[0])


def encode_kernel(count, where_ref, x_hbm, out_ref, x_ref, turned, arrived):
    rows, order = x_ref.shape
    fetches = [
        pltpu.make_async_copy(x_hbm.at[:, pl.ds(start, TILE)], x_ref.at[:, pl.ds(start, TILE)], arrived.at[start // TILE])
        for start in range(0, order, TILE)
    ]
    for fetch in fetches:
        fetch.start()
    for start, fetch in zip(range(0, order, TILE), fetches):
        fetch.wait()
        block = x_ref[:, start : start + TILE]
        turned[start : start + TILE, :] = jnp.where(live(block.shape, where_ref, rows, start), block, 0.0).T
    pack(turned, out_ref, count, order // count)


def encode(x, where, count, after=()):
    rows, order = x.shape
    return call(
        functools.partial(encode_kernel, count),
        message_shape(rows, order, count),
        LARGEST,
        (where, x),
        after,
        in_specs=[SMEM, ANY],
        scratch_shapes=[
            pltpu.VMEM((rows, order), F32),
            pltpu.VMEM((order, rows), F32),
            pltpu.SemaphoreType.DMA((order // TILE,)),
        ],
    )


def read_kernel(message_ref, high, low, turned):
    order = turned.shape[0]
    count = message_ref.shape[0]
    unpack(message_ref, turned, count, order // count)
    for start in range(0, order, TILE):
        span = slice(start, start + TILE)
        high[:, span], low[:, span] = split(turned[span, :].T)


def read(message, rows, after=(), flops=FAST):
    order = message.shape[0] * message.shape[2] // rows
    return call(
        read_kernel,
        [jax.ShapeDtypeStruct((rows, order), BF16)] * 2,
        12,
        (message,),
        after,
        flops,
        scratch_shapes=[pltpu.VMEM((order, rows), F32)],
    )


def bar_product(high, low, recouple_ref, outs, fetches=()):
    order = recouple_ref.shape[0]
    width = order // 2
    for start in range(0, order, TILE):
        if fetches:
            fetches[start // TILE].wait()
        product = dot3((high[...], low[...]), split(recouple_ref[:, start : start + TILE]), NN)
        for place, out in enumerate(outs):
            begin, end = max(start, place * width), min(start + TILE, (place + 1) * width)
            if begin < end:
                out[:, begin - place * width : end - place * width] = product[:, begin - start : end - start]


def gen_bar_kernel(high, low, recouple_ref, out_ref):
    bar_product(high, low, recouple_ref, [out_ref.at[0], out_ref.at[1]])


def ham_bar_kernel(where_ref, message_ref, recouple_hbm, low_ref, high_ref, turned, high, low, recouple_ref, arrived):
    order, rows = turned.shape
    fetches = [
        pltpu.make_async_copy(
            recouple_hbm.at[:, pl.ds(start, TILE)], recouple_ref.at[:, pl.ds(start, TILE)], arrived.at[start // TILE]
        )
        for start in range(0, order, TILE)
    ]
    for fetch in fetches:
        fetch.start()
    read_kernel(message_ref, high, low, turned)
    bar_product(high, low, recouple_ref, [low_ref.at[pl.ds(0, rows)], high_ref.at[pl.ds(0, rows)]], fetches)
    across = where_ref[1] ^ 2
    left = jnp.where(across < 2, low_ref[:rows, :rows], high_ref[:rows, :rows])
    right = jnp.where(across < 2, low_ref[:rows, rows:], high_ref[:rows, rows:])
    block = jnp.where(across % 2 == 0, left, right)
    beside = jnp.concatenate([block[: rows // 2], block[rows // 2 :]], axis=1)
    low_ref[rows:, :] = beside
    high_ref[rows:, :] = beside


def gen_bar_of(moved, recoupling, after=()):
    rows, order = moved[0].shape
    return call(
        gen_bar_kernel,
        jax.ShapeDtypeStruct((2, rows, order // 2), F32),
        20,
        (*moved, recoupling),
        after,
    )


def ham_bar_of(message, recoupling, where, rows, after=(), flops=FAST):
    order = recoupling.shape[0]
    half = jax.ShapeDtypeStruct((rows + rows // 2, order // 2), F32)
    return call(
        ham_bar_kernel,
        [half, half],
        LARGE,
        (where, message, recoupling),
        after,
        flops,
        in_specs=[SMEM, VMEM, ANY],
        scratch_shapes=[
            pltpu.VMEM((order, rows), F32),
            pltpu.VMEM((rows, order), BF16),
            pltpu.VMEM((rows, order), BF16),
            pltpu.VMEM((order, order), F32),
            pltpu.SemaphoreType.DMA((order // TILE,)),
        ],
    )


def partners(row):
    return row ^ 1, 3 - row, row ^ 2


def ladder_kernel(where_ref, gen_ref, ham_ref, first_ref, second_ref, *refs):
    outs, (left_high, left_low, right_high, right_low) = refs[:4], refs[4:]
    rows, order = gen_ref.shape
    half = order // 2
    row = where_ref[1]
    position = lax.broadcasted_iota(jnp.int32, (1, order), 1)
    weight = jnp.where(position < where_ref[0], (first_ref[...] + second_ref[...] - 1).astype(F32), 0.0)
    mine = block_of(weight, row, rows)
    near, far, across = partners(row)
    for place, (left, right) in enumerate(((gen_ref, ham_ref), (ham_ref, gen_ref))):
        span = slice(place * rows, (place + 1) * rows)
        for block in range(order // rows):
            spot = jnp.where(block == near, 0, jnp.where(block == row, 1, jnp.where(block == far, 2, 3)))
            high, low = split(left[:, block * rows : (block + 1) * rows].T * mine)
            at = pl.ds(pl.multiple_of(spot * rows, 64), rows)
            left_high[at, span], left_low[at, span] = high, low

            @pl.when(block == near)
            def _():
                left_high[order:, span], left_low[order:, span] = high, low

        right_high[span, :], right_low[span, :] = split(right[...])
    for place, starts in enumerate(((1, 3), (0, 2))):
        columns = slice(place * half, (place + 1) * half)
        right = right_high[:, columns], right_low[:, columns]
        for kind, start in enumerate(starts):
            at = slice(start * rows, (start + 2) * rows)
            outs[2 * place + kind][...] = dot3((left_high[at, :], left_low[at, :]), right, NN).reshape(2, rows, half)


def ladder_part(gen, ham, first, second, where, after=()):
    rows, order = gen.shape
    return call(
        ladder_kernel,
        [jax.ShapeDtypeStruct((2, rows, order // 2), F32)] * 4,
        LARGE,
        (where, gen, ham, first, second),
        after,
        scratch_shapes=[pltpu.VMEM((order + rows, 2 * rows), BF16)] * 2
        + [pltpu.VMEM((2 * rows, order), BF16)] * 2,
    )


def fold_kernel(keep_low, got_low, keep_high, got_high, own_ref, far_ref, near_ref):
    half = far_ref.shape[1]
    own_ref[:, :half] = keep_low[0] + got_low[1]
    own_ref[:, half:] = keep_high[1] + got_high[0]
    far_ref[...] = keep_low[1] + got_low[0]
    near_ref[...] = keep_high[0] + got_high[1]


def fold(keep_low, got_low, keep_high, got_high):
    _, rows, half = keep_low.shape
    return call(
        fold_kernel,
        [jax.ShapeDtypeStruct((rows, 2 * half), F32)] + [jax.ShapeDtypeStruct((rows, half), F32)] * 2,
        16,
        (keep_low, got_low, keep_high, got_high),
    )


def block_of(weight, index, rows):
    picked = weight[:, :rows]
    for other in range(1, weight.shape[1] // rows):
        picked = jnp.where(index == other, weight[:, other * rows : (other + 1) * rows], picked)
    return picked


def weighted(first_ref, second_ref):
    return (first_ref[...] - second_ref[...]).astype(F32)


def local_kernel(where_ref, mine_ref, near_ref, far_ref, low_ref, high_ref, first_ref, second_ref, out_ref, *scratch):
    ham_high, ham_low, gen_high, gen_low = scratch
    _, rows, half = mine_ref.shape
    weight = weighted(first_ref, second_ref)
    row = where_ref[1]
    near, far, across = partners(row)
    for place, ham_ref in enumerate((low_ref, high_ref)):
        span = slice(place * half, (place + 1) * half)
        ham_high[:, span], ham_low[:, span] = split(ham_ref[:rows, :] * weight[:, span])
        for gen_ref, block in ((mine_ref, row), (near_ref, near), (far_ref, far)):
            at = pl.ds(pl.multiple_of(block * rows, 64), rows)
            gen_high[at, span], gen_low[at, span] = split(gen_ref[place])
        at = pl.ds(pl.multiple_of(across * rows, 64), rows)
        gen_high[at, span] = jnp.zeros((rows, half), BF16)
        gen_low[at, span] = jnp.zeros((rows, half), BF16)
    for start in range(0, 2 * half, TILE):
        span = slice(start, start + TILE)
        out_ref[:, span] = dot3((ham_high[...], ham_low[...]), (gen_high[:, span], gen_low[:, span]), NN)


def local_term(slabs, ham_halves, first, second, where, after=()):
    _, rows, half = slabs[0].shape
    return call(
        local_kernel,
        jax.ShapeDtypeStruct((rows, 2 * half), F32),
        26,
        (where, *slabs, *ham_halves, first, second),
        after,
        scratch_shapes=[pltpu.VMEM((rows, 2 * half), BF16)] * 2 + [pltpu.VMEM((2 * half, 2 * half), BF16)] * 2,
    )


def chosen(pick_ref, gen_ref, weight):
    rows, half = gen_ref.shape[1:]
    kind = pick_ref[1]
    low, high = gen_ref[0] * weight[:, :half], gen_ref[1] * weight[:, half:]
    outer = jnp.concatenate([low[:, :rows], high[:, half - rows :]], axis=1)
    inner = jnp.concatenate([low[:, rows:], high[:, : half - rows]], axis=1)
    return jnp.where(kind == 0, outer, jnp.where(kind == 1, inner, jnp.where(kind == 2, low, high)))


def place_pair(pick_ref, own_ref, got_ref, right_high, right_low):
    rows = right_high.shape[0] // 2
    own_at = pl.multiple_of(pick_ref[0], 64)
    got_at = pl.multiple_of(rows - pick_ref[0], 64)
    for at, ref in ((own_at, own_ref), (got_at, got_ref)):
        right_high[pl.ds(at, rows), :], right_low[pl.ds(at, rows), :] = split(ref[:rows, :])


def pair_kernel(place, pick_ref, gen_ref, own_ref, got_ref, local_ref, first_ref, second_ref, out_ref, right_high, right_low):
    half = own_ref.shape[1]
    place_pair(pick_ref, own_ref, got_ref, right_high, right_low)
    left = split(chosen(pick_ref, gen_ref, weighted(first_ref, second_ref)))
    for start in range(0, half, TILE):
        end = min(start + TILE, half)
        local = local_ref[:, place * half + start : place * half + end]
        out_ref[:, start:end] = dot3(left, (right_high[:, start:end], right_low[:, start:end]), NN) - local


def pair_product(place, pick, slab, own, got, local, first, second, after=()):
    _, rows, half = slab.shape
    return call(
        functools.partial(pair_kernel, place),
        jax.ShapeDtypeStruct((rows, half), F32),
        16,
        (pick, slab, own, got, local, first, second),
        after,
        scratch_shapes=[pltpu.VMEM((2 * rows, half), BF16)] * 2,
    )


def columns_of(gen_ref, index, weight):
    rows = gen_ref.shape[1]
    left = jnp.where(index < 2, gen_ref[0, :, :rows], gen_ref[1, :, :rows])
    right = jnp.where(index < 2, gen_ref[0, :, rows:], gen_ref[1, :, rows:])
    return jnp.where(index % 2 == 0, left, right) * block_of(weight, index, rows)


def ready_kernel(where_ref, near_ref, far_ref, low_ref, high_ref, first_ref, second_ref, *outs):
    _, rows, half = near_ref.shape
    weight = weighted(first_ref, second_ref)
    row = where_ref[1]
    near, far, _ = partners(row)
    sides = ((near_ref, far_ref, low_ref, far), (far_ref, near_ref, high_ref, near))
    for place, (gen_ref, other_ref, ham_ref, index) in enumerate(sides):
        part, left_high, left_low, right_high, right_low = outs[5 * place : 5 * place + 5]
        left = split(columns_of(gen_ref, row, weight))
        for start in range(0, half, TILE):
            span = slice(start, min(start + TILE, half))
            part[:, span] = dot3(left, split(ham_ref[:rows, span]), NN)
        left_high[...], left_low[...] = split(columns_of(gen_ref, index, weight))
        right_high[...], right_low[...] = split(other_ref[place])


def ready(where, gen_near, gen_far, ham_halves, first, second):
    _, rows, half = gen_near.shape
    side = (
        [jax.ShapeDtypeStruct((rows, half), F32)]
        + [jax.ShapeDtypeStruct((rows, rows), BF16)] * 2
        + [jax.ShapeDtypeStruct((rows, half), BF16)] * 2
    )
    outs = call(
        ready_kernel,
        side * 2,
        24,
        (where, gen_near, gen_far, *ham_halves, first, second),
    )
    return outs[:5], outs[5:]


def send_kernel(pick_ref, part_ref, first_high, first_low, other_high, other_low, got_ref, block_ref, first_ref, second_ref, out_ref, *scratch):
    left_high, left_low, right_high, right_low = scratch
    rows, half = out_ref.shape
    weight = block_of(weighted(first_ref, second_ref), pick_ref[2], rows)
    block = jnp.concatenate([block_ref[rows:, :rows], block_ref[rows:, rows:]], axis=0)
    left_high[:, :rows], left_low[:, :rows] = first_high[...], first_low[...]
    left_high[:, rows:], left_low[:, rows:] = split(-block * weight)
    right_high[:rows, :], right_low[:rows, :] = split(got_ref[:rows, :])
    right_high[rows:, :], right_low[rows:, :] = other_high[...], other_low[...]
    for start in range(0, half, TILE):
        span = slice(start, min(start + TILE, half))
        product = dot3((left_high[...], left_low[...]), (right_high[:, span], right_low[:, span]), NN)
        out_ref[:, span] = part_ref[:, span] + product


def send_product(pick, prepared, got, block, first, second, after=()):
    rows, half = prepared[0].shape
    return call(
        send_kernel,
        jax.ShapeDtypeStruct((rows, half), F32),
        18,
        (pick, *prepared, got, block, first, second),
        after,
        scratch_shapes=[pltpu.VMEM((rows, 2 * rows), BF16)] * 2 + [pltpu.VMEM((2 * rows, half), BF16)] * 2,
    )


def halves_kernel(x_ref, high, low):
    for start in range(0, x_ref.shape[0], TILE):
        span = slice(start, start + TILE)
        high[span, :], low[span, :] = split(x_ref[span, :])


def halves(x, after=()):
    return call(halves_kernel, [jax.ShapeDtypeStruct(x.shape, BF16)] * 2, 16, (x,), after)


def turn_first_kernel(own_ref, got_ref, high_ref, low_ref, out_ref):
    half = own_ref.shape[1]
    left = split(own_ref[...] + got_ref[...])
    for start in range(0, high_ref.shape[0], TILE):
        span = slice(start, start + TILE)
        out_ref[:, span] = dot3(left, (high_ref[span, :half], low_ref[span, :half]), NT)


def turn_first(own, got, recouple_parts):
    rows, half = own.shape
    return call(
        turn_first_kernel,
        jax.ShapeDtypeStruct((rows, 2 * half), F32),
        20,
        (own, got, *recouple_parts),
    )


def turn_kernel(count, first_ref, own_ref, got_ref, high_ref, low_ref, out_ref, turned):
    half = own_ref.shape[1]
    left = split(own_ref[...] + got_ref[...])
    order = 2 * half
    for start in range(0, order, TILE):
        span = slice(start, start + TILE)
        product = dot3(left, (high_ref[span, half:], low_ref[span, half:]), NT)
        turned[span, :] = (first_ref[:, span] + product).T
    pack(turned, out_ref, count, order // count)


def turn(first, own, got, recouple_parts, count):
    rows, order = first.shape
    return call(
        functools.partial(turn_kernel, count),
        message_shape(rows, order, count),
        24,
        (first, own, got, *recouple_parts),
        scratch_shapes=[pltpu.VMEM((order, rows), F32)],
    )


def finish_kernel(where_ref, message_ref, own_hbm, low_hbm, high_hbm, out_hbm, turned, own_ref, part_ref, out_ref, arrived, left):
    rows, order = out_ref.shape
    sent = []
    half = low_hbm.shape[1]
    count = message_ref.shape[0]
    copies = [
        pltpu.make_async_copy(own_hbm, own_ref, arrived.at[0]),
        pltpu.make_async_copy(low_hbm, part_ref.at[0], arrived.at[1]),
        pltpu.make_async_copy(high_hbm, part_ref.at[1], arrived.at[2]),
    ]
    for copy in copies:
        copy.start()
    unpack(message_ref, turned, count, order // count)
    for copy in copies:
        copy.wait()
    for place in range(2):
        for start in range(0, half, LANES):
            at = place * half + start
            span = slice(at, at + LANES)
            total = own_ref[:, span] + part_ref[place, :, start : start + LANES] + turned[span, :].T
            out_ref[:, span] = jnp.where(live(total.shape, where_ref, rows, at), total, 0.0)
            columns = pl.ds(at, LANES)
            sent.append(
                pltpu.make_async_copy(out_ref.at[:, columns], out_hbm.at[:, columns], left.at[at // LANES])
            )
            sent[-1].start()
    for copy in sent:
        copy.wait()


def finish(message, own, low, high, where):
    rows, order = own.shape
    return call(
        finish_kernel,
        jax.ShapeDtypeStruct((rows, order), F32),
        52,
        (where, message, own, low, high),
        in_specs=[SMEM, VMEM, ANY, ANY, ANY],
        out_specs=ANY,
        scratch_shapes=[
            pltpu.VMEM((order, rows), F32),
            pltpu.VMEM((rows, order), F32),
            pltpu.VMEM((2, rows, order // 2), F32),
            pltpu.VMEM((rows, order), F32),
            pltpu.SemaphoreType.DMA((3,)),
            pltpu.SemaphoreType.DMA((order // LANES,)),
        ],
    )


def hold_kernel(*refs):
    del refs


def hold(arrays, after):
    count = len(arrays)
    return call(
        hold_kernel,
        [jax.ShapeDtypeStruct(x.shape, x.dtype) for x in arrays],
        2,
        arrays,
        after,
        in_specs=[ANY] * count,
        out_specs=[ANY] * count,
        aliases={k: k for k in range(count)},
    )


def exchange(message):
    return lax.all_to_all(message, "chan", 0, 0, tiled=True)


def shards(generator, hamiltonian, recoupling, channel_size, hole_first, hole_second):
    gen, ham, recouple = generator[0], hamiltonian[0], recoupling[0]
    rows = gen.shape[0]
    count = lax.axis_size("chan")
    holes = (hole_first, hole_second)
    row = lax.axis_index("row").astype(jnp.int32)
    where = jnp.stack([channel_size[0], row])
    near, far, _ = partners(row)
    far_pick = jnp.stack([jnp.where(row < 2, 0, rows), jnp.where((row == 0) | (row == 3), 0, 1), far]).astype(jnp.int32)
    near_pick = jnp.stack([jnp.where(row % 2 == 0, 0, rows), jnp.where(row < 2, 2, 3), near]).astype(jnp.int32)

    def to_near(x):
        return lax.ppermute(x, "row", [(0, 1), (1, 0), (2, 3), (3, 2)])

    def to_far(x):
        return lax.ppermute(x, "row", [(0, 3), (3, 0), (1, 2), (2, 1)])

    gen_message = encode(gen, where, count)
    gen_moved = exchange(gen_message)
    keep_low, send_low, keep_high, send_high = ladder_part(gen, ham, *holes, where, after=(gen_message,))
    got_low, got_high = to_near(send_low), to_far(send_high)
    ham_message = encode(ham, where, count, after=(send_low,))
    ham_moved = exchange(ham_message)
    gen_bar = gen_bar_of(read(gen_moved, rows, after=(ham_message,), flops=SLOW), recouple)
    (gen_bar,) = hold((gen_bar,), (got_low, got_high))
    gen_near, gen_far = to_near(gen_bar), to_far(gen_bar)
    ham_bar = ham_bar_of(ham_moved, recouple, where, rows, flops=SLOW)
    ham_bar = hold(ham_bar, (gen_near, gen_far))
    from_far, from_near = to_far(ham_bar[0]), to_near(ham_bar[1])
    ladder_own, ladder_far, ladder_near = fold(keep_low, got_low, keep_high, got_high)
    local = local_term((gen_bar, gen_near, gen_far), ham_bar, *holes, where, after=(ladder_far,))
    for_near, for_far = ready(where, gen_near, gen_far, ham_bar, *holes)
    send_near = send_product(far_pick, for_near, from_far, from_near, *holes, after=(local,))
    term_near = to_near(send_near)
    send_far = send_product(near_pick, for_far, from_near, from_far, *holes, after=(local,))
    term_far = to_far(send_far)
    sent = (send_near, send_far)
    own = (
        pair_product(0, far_pick, gen_bar, ham_bar[0], from_far, local, *holes, after=sent),
        pair_product(1, near_pick, gen_bar, ham_bar[1], from_near, local, *holes, after=sent),
    )
    recouple_parts = halves(recouple, after=sent)
    first_half = turn_first(own[0], term_near, recouple_parts)
    message = turn(first_half, own[1], term_far, recouple_parts, count)
    back = exchange(message)
    return finish(back, ladder_own, to_far(ladder_far), to_near(ladder_near), where)[None]


def solution(mesh):
    in_specs = (
        P("chan", "row", None),
        P("chan", "row", None),
        P("chan", None, None),
        P("chan"),
        P("chan", None),
        P("chan", None),
    )
    out_specs = P("chan", "row", None)
    return jax.shard_map(shards, mesh=mesh, in_specs=in_specs, out_specs=out_specs, check_vma=False)
```
